32 devices in a mesh: sec: 2 (over core), dev: 16 (over z, y, x).
Axes of the slice: x: 2, y: 2, z: 4, core: 2. Of those that a mesh axis runs over, the one named last changes fastest.
Arguments:
- raw_pixels: float32 [2, 32, 512, 512], P(None, ('sec', 'dev')), may hold values from -8 to 8
- flat_field: float32 [32, 512, 512], P(('sec', 'dev')), may hold values from 0.5 to 1.5
- bias_rows: float32 [2, 32, 512], P(None, ('sec', 'dev')), may hold values from -6 to 6
- psf_taps: float32 [2, 1, 2, 41], replicated, may hold values from -1 to 1
- term_weights: float32 [2, 32, 1], P(None, ('sec', 'dev')), may hold values from -5 to 5
- warp_shift: float32 [2, 32, 2], P(None, ('sec', 'dev')), may hold values from -3 to 3
- warp_scale: float32 [2, 32, 2], P(None, ('sec', 'dev')), may hold values from 0.97 to 1.03
- owner_of: int32 [1024, 1], P(('sec', 'dev')), may hold values from 0 to 31; in each aligned block of 32 rows (0 to 31, 32 to 63, ...) at most 2 rows name the same one
- patch_slot: int32 [1024, 1], P(('sec', 'dev')), may hold values from 0 to 3
- weight_index: int32 [1024, 1], P(('sec', 'dev')), may hold values from 0 to 15
- weight_table: float32 [16], replicated, may hold values from 0.3 to 3
- detect_taps: float32 [2, 41], replicated, may hold values from -1 to 1
Outputs:
- coadd: float32 [4096, 512], P(('sec', 'dev'))
- detection: float32 [4096, 512], P(('sec', 'dev'))
The draws below stay inside these ranges and needn't reach their ends.
Inputs may be any that keep to these rules, and one draw needn't show every extreme that they name: `owner_of`: among the 32 rows of one slab no owner is named more than 2 times, a bound that some block reaches.
All inputs are finite; a program needn't handle non-finite values.
Results may differ from the reference program's by a relative error of at most 0.01.
Values may be sent and summed in bfloat16 or wider, within the bound.
No kernel may reach another device: no remote copies, remote signals or barrier semaphores. Data moves between devices by JAX's collectives and lax.ppermute only.
A program may use at most 128 MiB of HBM per device.

```python
import math
import jax
import jax.numpy as jnp
import numpy as np
from jax import lax

V = 2
SR = 512
SC = 512
P_SIZE = 128
TAPS = 41
TERMS = 1
CAP = 2
PATCH_DEV = 4
WT = 16
SLABS = 32
BLK_DEV = 32
BLOCKS = 1024
N_SEC = 2
N_DEV = 16


def set_ends(array, own_key, least, top_value):
    shape = array.shape
    index_at = [jax.random.randint(jax.random.fold_in(own_key, axis), (), 0, shape[axis]) for axis in range(len(shape))]
    array = array.at[tuple(index_at)].set(least)
    longest = shape.index(max(shape))
    index_at[longest] = (index_at[longest] + 1) % shape[longest]
    return array.at[tuple(index_at)].set(top_value)


def shard_levels(stream_key, extent, cuts, low, largest):
    level, own = 1.0, jax.random.fold_in(stream_key, 6)
    for dim, blocks in cuts:
        draws = jnp.exp(jax.random.uniform(jax.random.fold_in(own, dim), (blocks,), jnp.float32, low / len(cuts), largest / len(cuts)))
        level = level * jnp.repeat(draws, extent[dim] // blocks).reshape([-1 if axis == dim else 1 for axis in range(len(extent))])
    return level


def assign_block(rng, own, number, rows, count, top, limit, skew):
    order = jax.random.permutation(rng, count)
    packed, ordinary = shares(count, rows * top, limit, skew, True), shares(count, rows * top, limit, skew, False)
    places = jnp.arange(count)

    def named(tallies, rotation):
        used = int((tallies > 0).sum())
        fixed = max(1, used // 4)
        moved = fixed + (places - fixed + rotation * (used - fixed)) % max(1, count - fixed)
        return jnp.zeros((count,), jnp.int32).at[order[jnp.where(places < fixed, places, moved)]].set(jnp.asarray(tallies, jnp.int32))

    tallies = jnp.where(number % 4 == 0, named(packed, number // 4), named(ordinary, number - number // 4 - 1))
    mixed = jax.random.permutation(jax.random.fold_in(own, 3), count)
    giver, sink = mixed[0:count // 2 * 2:2], mixed[1:count // 2 * 2:2]
    margin = jnp.minimum(tallies[giver] - 1, limit - tallies[sink]) // 2
    margin = jnp.where((giver == order[0]) | (sink == order[0]) | (tallies[sink] == 0), 0, jnp.maximum(margin, 0))
    moved = jax.random.randint(jax.random.fold_in(own, 4), (count // 2,), 0, 1 << 20) % (margin + 1)
    tallies = tallies.at[giver].add(-moved).at[sink].add(moved)
    members = jnp.searchsorted(jnp.cumsum(tallies), jnp.arange(rows * top), side="right").astype(jnp.int32)
    listing = members.reshape(top, rows).T
    listing = listing[jax.random.permutation(jax.random.fold_in(own, 1), rows)]
    rotation = jax.random.randint(jax.random.fold_in(own, 2), (rows, 1), 0, top)
    return jnp.take_along_axis(listing, (jnp.arange(top)[None, :] + rotation) % top, axis=1)


def shares(number_of, total, reach, slope, full):
    portions = [(1 << 20) // math.isqrt(rank ** slope) + 1 for rank in range(1, number_of + 1)]
    largest = reach if full else min(reach, max(-(-total // number_of), total * portions[0] // sum(portions)))
    least = 1 if total - largest >= number_of - 1 else 0
    counts, rest = [largest] + [least] * (number_of - 1), total - largest - least * (number_of - 1)
    while rest > 0:
        candidates = [i for i in range(1, number_of) if counts[i] < largest] or [i for i in range(1, number_of) if counts[i] < reach]
        mass, left = sum([portions[i] for i in candidates]), rest
        for i in candidates:
            extra = min(reach - counts[i], max(1, left * portions[i] // mass), rest)
            counts[i] = counts[i] + extra
            rest = rest - extra
    return np.array(counts)


def normal_values(own_key, shape, spread, reach, split=(), kind=jnp.bfloat16):
    values = spread * jax.random.normal(own_key, shape, jnp.float32)
    if split:
        values = values * shard_levels(own_key, shape, split, -0.22, 0.18)
    return jnp.clip(values, -reach, reach).astype(kind)


def setup_inputs(seed: int = 0) -> dict:
    splits = jax.random.split(jax.random.key(seed), 13)
    raw_pixels = normal_values(splits[0], (V, SLABS, SR, SC), 1.0, 8.0, ((1, 32),), jnp.float32)
    flat_field = jnp.clip(1.0 + 0.1 * jax.random.normal(splits[1], (SLABS, SR, SC), jnp.float32), 0.5, 1.5)
    bias_rows = normal_values(splits[2], (V, SLABS, SR), 1.0, 6.0, ((1, 32),), jnp.float32)
    psf_taps = normal_values(splits[3], (V, TERMS, 2, TAPS), TAPS ** -0.5, 1.0, (), jnp.float32)
    term_weights = normal_values(splits[4], (V, SLABS, TERMS), 1.0, 5.0, ((1, 32),), jnp.float32)
    warp_shift = jnp.clip(jax.random.uniform(splits[5], (V, SLABS, 2), jnp.float32, -3.0, 3.0) * shard_levels(splits[5], (V, SLABS, 2), ((1, 32),), -0.4, 0.0), -3.0, 3.0)
    warp_scale = jnp.clip(0.97 + 0.059999943 * jax.random.uniform(splits[6], (V, SLABS, 2), jnp.float32) ** shard_levels(splits[6], (V, SLABS, 2), ((1, 32),), -0.2, 0.2), 0.97, 1.03)
    owner_of_keys = jax.random.split(jax.random.fold_in(splits[7], 1), BLOCKS // BLK_DEV)
    owner_of_turns = jax.random.permutation(jax.random.fold_in(splits[7], 3), BLOCKS // BLK_DEV)
    owner_of = jax.vmap(lambda own, number: assign_block(jax.random.fold_in(splits[7], 2), own, number, BLK_DEV, N_SEC * N_DEV, 1, CAP, 2))(owner_of_keys, owner_of_turns).reshape((BLOCKS, 1))
    patch_slot = set_ends(jax.random.randint(splits[8], (BLOCKS, 1), 0, PATCH_DEV), jax.random.fold_in(splits[8], 1), 0, PATCH_DEV - 1).astype(jnp.int32)
    weight_index = set_ends(jax.random.randint(splits[9], (BLOCKS, 1), 0, WT), jax.random.fold_in(splits[9], 1), 0, WT - 1).astype(jnp.int32)
    weight_table = jnp.clip(jnp.exp(jax.random.uniform(splits[10], (WT,), jnp.float32, math.log(0.3), math.log(3.0))), 0.3, 3.0)
    detect_taps = normal_values(splits[11], (2, TAPS), TAPS ** -0.5, 1.0, (), jnp.float32)
    return {"raw_pixels": raw_pixels, "flat_field": flat_field, "bias_rows": bias_rows, "psf_taps": psf_taps, "term_weights": term_weights, "warp_shift": warp_shift, "warp_scale": warp_scale, "owner_of": owner_of, "patch_slot": patch_slot, "weight_index": weight_index, "weight_table": weight_table, "detect_taps": detect_taps}


def to_bfloat(values):
    return lax.optimization_barrier(values.astype(jnp.bfloat16))


def smooth_axis(values, tap_values, axis_pos):
    length = values.shape[axis_pos]
    half_width = tap_values.shape[0] // 2
    padding = [(0, 0), (0, 0)]
    padding[axis_pos] = (half_width, half_width)
    padded = jnp.pad(values, padding)
    result = jnp.zeros(values.shape, jnp.float32)
    for tap_index in range(tap_values.shape[0]):
        window = lax.slice_in_dim(padded, tap_index, tap_index + length, axis=axis_pos)
        result = result + tap_values[tap_index] * window
    return result


def band_matrix(tap_values, length):
    half_width = tap_values.shape[0] // 2
    positions = jnp.arange(length, dtype=jnp.int32)
    offset = positions[None, :] - positions[:, None] + half_width
    matrix = jnp.zeros((length, length), jnp.float32)
    for tap_index in range(tap_values.shape[0]):
        matrix = matrix + jnp.where(offset == tap_index, tap_values[tap_index], 0.0)
    return matrix


def interpolation(shift_value, scale_value, length):
    centre = (length - 1) / 2.0
    positions = jnp.arange(length).astype(jnp.float32)
    source = scale_value * (positions - centre) + centre + shift_value
    return jnp.maximum(0.0, 1.0 - jnp.abs(positions[None, :] - source[:, None]))


def warp_visit(raw_visit, flat_slab, bias_visit, taps_visit, weights_visit, shift_visit, scale_visit):
    exposure = to_bfloat((raw_visit - bias_visit[:, None]) * flat_slab).astype(jnp.float32)
    matched = jnp.zeros(exposure.shape, jnp.float32)
    for term_index in range(taps_visit.shape[0]):
        across_taps = to_bfloat(taps_visit[term_index, 1]).astype(jnp.float32)
        down_taps = to_bfloat(taps_visit[term_index, 0]).astype(jnp.float32)
        smoothed = to_bfloat(smooth_axis(exposure, across_taps, 1)).astype(jnp.float32)
        matched = matched + weights_visit[term_index] * smooth_axis(smoothed, down_taps, 0)
    matched = to_bfloat(matched).astype(jnp.float32)
    warp_cols = to_bfloat(interpolation(shift_visit[1], scale_visit[1], exposure.shape[1])).astype(jnp.float32)
    warp_rows = to_bfloat(interpolation(shift_visit[0], scale_visit[0], exposure.shape[0])).astype(jnp.float32)
    half_warped = jnp.dot(matched, warp_cols.T, precision=lax.Precision.HIGHEST)
    half_warped = to_bfloat(half_warped).astype(jnp.float32)
    return jnp.dot(warp_rows, half_warped, precision=lax.Precision.HIGHEST).astype(jnp.bfloat16)


def cut_blocks(image, side):
    row_blocks = image.shape[0] // side
    col_blocks = image.shape[1] // side
    shaped = image.reshape(row_blocks, side, col_blocks, side).transpose(0, 2, 1, 3)
    return shaped.reshape(row_blocks * col_blocks, side, side)


def reference(raw_pixels, flat_field, bias_rows, psf_taps, term_weights, warp_shift, warp_scale, owner_of, patch_slot, weight_index, weight_table, detect_taps):
    slab_count = raw_pixels.shape[1]
    per_slab = owner_of.shape[0] // slab_count
    owners = owner_of[:, 0]
    slots = patch_slot[:, 0]
    indices = weight_index[:, 0]

    def accumulate(running, slab_index):
        numerator, weight_sum = running
        raw_slab = lax.dynamic_index_in_dim(raw_pixels, slab_index, 1, keepdims=False)
        flat_slab = lax.dynamic_index_in_dim(flat_field, slab_index, 0, keepdims=False)
        bias_slab = lax.dynamic_index_in_dim(bias_rows, slab_index, 1, keepdims=False)
        weights_slab = lax.dynamic_index_in_dim(term_weights, slab_index, 1, keepdims=False)
        shift_slab = lax.dynamic_index_in_dim(warp_shift, slab_index, 1, keepdims=False)
        scale_slab = lax.dynamic_index_in_dim(warp_scale, slab_index, 1, keepdims=False)
        pieces = []
        for visit_index in range(raw_pixels.shape[0]):
            warped = warp_visit(raw_slab[visit_index], flat_slab, bias_slab[visit_index], psf_taps[visit_index], weights_slab[visit_index], shift_slab[visit_index], scale_slab[visit_index])
            pieces.append(cut_blocks(warped, P_SIZE))
        blocks = jnp.concatenate(pieces, 0).astype(jnp.float32)
        start = (slab_index * per_slab).astype(jnp.int32)
        targets = lax.dynamic_slice_in_dim(owners, start, per_slab) * PATCH_DEV + lax.dynamic_slice_in_dim(slots, start, per_slab)
        weights = weight_table[lax.dynamic_slice_in_dim(indices, start, per_slab)]
        numerator = numerator.at[targets].add(weights[:, None, None] * blocks)
        weight_sum = weight_sum.at[targets].add(weights)
        return (numerator, weight_sum), None

    initial = (jnp.zeros((slab_count * PATCH_DEV, P_SIZE, P_SIZE), jnp.float32), jnp.zeros((slab_count * PATCH_DEV,), jnp.float32))
    (numerator, weight_sum), _ = lax.scan(accumulate, initial, jnp.arange(slab_count, dtype=jnp.int32))
    blocks_done = numerator / jnp.maximum(weight_sum, 1.0)[:, None, None]
    coadd = blocks_done.reshape(slab_count, PATCH_DEV, P_SIZE, P_SIZE).transpose(0, 2, 1, 3).reshape(slab_count * P_SIZE, PATCH_DEV * P_SIZE)
    along_rows = smooth_axis(coadd, detect_taps[0], 0)
    across_band = band_matrix(detect_taps[1], coadd.shape[1])
    detection = jnp.dot(along_rows, across_band.T, precision=lax.Precision.HIGHEST)
    return coadd, detection
```

```python
import functools
import math

import jax
import jax.numpy as jnp
from jax import lax
from jax.experimental import pallas as pl
from jax.experimental.pallas import tpu as pltpu
from jax.sharding import Mesh
from jax.sharding import PartitionSpec as P

SIDE = 128
CAP = 2
PATCH_DEV = 4
HALO = 32
VMEM_LIMIT = 48 * 1024 * 1024


def tap_row(tap, count, start, width, reverse):
    lane = lax.broadcasted_iota(jnp.int32, (1, width), 1)
    row = jnp.zeros((1, width), jnp.float32)
    for k in range(count):
        at = start + (count - 1 - k if reverse else k)
        row = jnp.where(lane == at, tap(k), row)
    return row


def toeplitz(row, height):
    return pltpu.roll(
        jnp.broadcast_to(row, (height, row.shape[1])), 0, 1, stride=1, stride_axis=0
    )


def store_band(band_ref, tiles):
    blocks = band_ref.shape[0] // SIDE
    for i in range(blocks):
        for j in range(blocks):
            place = (pl.ds(i * SIDE, SIDE), pl.ds(j * SIDE, SIDE))
            if abs(i - j) <= 1:
                first = (j - i + 1) * SIDE
                band_ref[place] = tiles[:, first : first + SIDE]
            else:
                band_ref[place] = jnp.zeros((SIDE, SIDE), band_ref.dtype)


def dot32(left, right):
    return jnp.dot(left, right, preferred_element_type=jnp.float32)


def warp_kernel(
    split,
    owner_ref,
    taps_ref,
    weights_ref,
    shift_ref,
    scale_ref,
    bias_ref,
    raw_ref,
    flat_ref,
    out_ref,
    count_ref,
    band_ref,
    left_ref,
    mid_ref,
):
    nz, pn = split
    visit = pl.program_id(0)
    rows, cols = raw_ref.shape[2], raw_ref.shape[3]
    terms, tap_count = taps_ref.shape[1], taps_ref.shape[3]
    half = tap_count // 2

    @pl.when(visit == 0)
    def _():
        def clear(i, c):
            count_ref[i] = 0
            return c

        lax.fori_loop(0, count_ref.shape[0], clear, 0)

    bias = jnp.broadcast_to(bias_ref[0], (SIDE, rows)).T
    for j in range(cols // SIDE):
        sl = pl.ds(j * SIDE, SIDE)
        left_ref[:, sl] = ((raw_ref[0, 0, :, sl] - bias) * flat_ref[0, :, sl]).astype(jnp.bfloat16)

    matched = None
    for term in range(terms):
        across = tap_row(
            lambda k: taps_ref[visit, term, 1, k], tap_count, SIDE - half, 3 * SIDE, True
        )
        store_band(band_ref, toeplitz(across, SIDE).astype(jnp.bfloat16))
        mid_ref[...] = dot32(left_ref[...], band_ref[...]).astype(jnp.bfloat16)
        down = tap_row(
            lambda k: taps_ref[visit, term, 0, k], tap_count, SIDE - half, 3 * SIDE, False
        )
        store_band(band_ref, toeplitz(down, SIDE).astype(jnp.bfloat16))
        part = weights_ref[visit, term] * dot32(band_ref[...], mid_ref[...])
        matched = part if matched is None else matched + part
    left_ref[...] = matched.astype(jnp.bfloat16)

    def hat(length, axis, shift, scale):
        centre = (length - 1) / 2.0
        shape = (1, length) if axis == 1 else (length, 1)
        out_pos = lax.broadcasted_iota(jnp.int32, shape, axis).astype(jnp.float32)
        source = scale * (out_pos - centre) + centre + shift
        in_pos = lax.broadcasted_iota(jnp.int32, (length, length), 1 - axis).astype(jnp.float32)
        return jnp.maximum(0.0, 1.0 - jnp.abs(in_pos - source)).astype(jnp.bfloat16)

    band_ref[...] = hat(cols, 1, shift_ref[visit, 1], scale_ref[visit, 1])
    mid_ref[...] = dot32(left_ref[...], band_ref[...]).astype(jnp.bfloat16)
    band_ref[...] = hat(rows, 0, shift_ref[visit, 0], scale_ref[visit, 0])
    left_ref[...] = dot32(band_ref[...], mid_ref[...]).astype(jnp.bfloat16)

    row_blocks, col_blocks = rows // SIDE, cols // SIDE
    for i in range(row_blocks):
        for j in range(col_blocks):
            owner = owner_ref[visit * (row_blocks * col_blocks) + i * col_blocks + j]
            rank = count_ref[owner]
            count_ref[owner] = rank + 1
            sec = owner // (nz * pn)
            dev = owner - sec * (nz * pn)
            z = dev // pn
            p = dev - z * pn
            slot = ((sec * pn + p) * nz + z) * CAP + rank
            out_ref[slot] = left_ref[pl.ds(i * SIDE, SIDE), pl.ds(j * SIDE, SIDE)]


def table_kernel(split, me_ref, meta_ref, table_ref, slot_ref, weight_ref, count_ref):
    nz, pn, ns = split
    blocks = meta_ref.shape[0] // (3 * ns * nz * pn)
    my_sec, my_z, my_p = me_ref[0], me_ref[1], me_ref[2]

    def clear(i, c):
        slot_ref[i] = -1
        weight_ref[i] = 0.0
        return c

    lax.fori_loop(0, slot_ref.shape[0], clear, 0)

    def source(g, c):
        sec = g // pn
        base = ((sec * nz + my_z) * pn + (g - sec * pn)) * (3 * blocks)
        for z in range(nz):
            count_ref[z] = 0

        def block(b, cc):
            owner = meta_ref[base + b]
            osec = owner // (nz * pn)
            dev = owner - osec * (nz * pn)
            oz = dev // pn
            op = dev - oz * pn

            @pl.when((osec == my_sec) & (op == my_p))
            def _():
                rank = count_ref[oz]
                count_ref[oz] = rank + 1
                at = (g * nz + oz) * CAP + rank
                slot_ref[at] = meta_ref[base + blocks + b]
                weight_ref[at] = table_ref[meta_ref[base + 2 * blocks + b]]

            return cc

        return lax.fori_loop(0, blocks, block, c)

    lax.fori_loop(0, ns * pn, source, 0)


def reduce_kernel(nz, slot_ref, weight_ref, in_ref, out_ref, acc_ref):
    z = pl.program_id(0)
    acc_ref[...] = jnp.zeros_like(acc_ref)
    for g in range(in_ref.shape[0]):
        for r in range(CAP):
            at = (g * nz + z) * CAP + r
            slot = slot_ref[at]

            @pl.when(slot >= 0)
            def _():
                acc_ref[slot] += weight_ref[at] * in_ref[g, 0, r].astype(jnp.float32)

    out_ref[0] = acc_ref[...].astype(out_ref.dtype)


def coadd_kernel(me_ref, table_ref, owner_ref, slot_ref, index_ref, in_ref, coadd_ref, low_ref, high_ref):
    owners = owner_ref[...]
    slots = slot_ref[...]
    index = index_ref[...]
    weights = jnp.zeros(index.shape, jnp.float32)
    for k in range(table_ref.shape[0]):
        weights = jnp.where(index == k, table_ref[k], weights)
    weights = jnp.where(owners == me_ref[3], weights, 0.0)
    for j in range(PATCH_DEV):
        total = jnp.sum(jnp.where(slots == j, weights, 0.0), keepdims=True)
        numerator = in_ref[0, j].astype(jnp.float32)
        for z in range(1, in_ref.shape[0]):
            numerator = numerator + in_ref[z, j].astype(jnp.float32)
        tile = numerator / jnp.maximum(total, 1.0)
        sl = pl.ds(j * SIDE, SIDE)
        coadd_ref[:, sl] = tile
        high_ref[:, sl] = tile[:HALO].astype(jnp.bfloat16)
        low_ref[:, sl] = tile[SIDE - HALO :].astype(jnp.bfloat16)


def split_dot(left, right):
    lh = left.astype(jnp.bfloat16)
    ll = (left - lh.astype(jnp.float32)).astype(jnp.bfloat16)
    rh = right.astype(jnp.bfloat16)
    rl = (right - rh.astype(jnp.float32)).astype(jnp.bfloat16)
    return dot32(lh, rh) + (dot32(lh, rl) + dot32(ll, rh))


def detect_kernel(taps_ref, coadd_ref, low_ref, high_ref, out_ref, ext_ref, band_ref):
    tap_count = taps_ref.shape[1]
    half = tap_count // 2
    depth = ext_ref.shape[0]
    ext_ref[...] = jnp.zeros_like(ext_ref)
    ext_ref[pl.ds(0, HALO)] = low_ref[...].astype(jnp.float32)
    ext_ref[pl.ds(HALO, SIDE)] = coadd_ref[...]
    ext_ref[pl.ds(HALO + SIDE, HALO)] = high_ref[...].astype(jnp.float32)
    down = tap_row(lambda k: taps_ref[0, k], tap_count, HALO - half, depth, False)
    along = split_dot(toeplitz(down, SIDE), ext_ref[...])
    across = tap_row(lambda k: taps_ref[1, k], tap_count, SIDE - half, 3 * SIDE, True)
    store_band(band_ref, toeplitz(across, SIDE))
    out_ref[...] = split_dot(along, band_ref[...])


def per_device(
    split,
    raw_pixels,
    flat_field,
    bias_rows,
    psf_taps,
    term_weights,
    warp_shift,
    warp_scale,
    owner_of,
    patch_slot,
    weight_index,
    weight_table,
    detect_taps,
):
    nz, pn, ns = split
    devices = nz * pn * ns
    visits, _, rows, cols = raw_pixels.shape
    blocks = owner_of.shape[0]
    smem = pl.BlockSpec(memory_space=pltpu.SMEM)
    vmem = pl.BlockSpec(memory_space=pltpu.VMEM)
    params = pltpu.CompilerParams(vmem_limit_bytes=VMEM_LIMIT)

    owners = owner_of.reshape(blocks)
    meta = jnp.concatenate([owners, patch_slot.reshape(blocks), weight_index.reshape(blocks)])
    meta = lax.all_gather(meta, ("sec", "z", "p"), tiled=True)
    sec, z, p = lax.axis_index("sec"), lax.axis_index("z"), lax.axis_index("p")
    me = jnp.stack([sec, z, p, (sec * nz + z) * pn + p]).astype(jnp.int32)

    slots = devices * CAP
    send = pl.pallas_call(
        functools.partial(warp_kernel, (nz, pn)),
        grid=(visits,),
        out_shape=jax.ShapeDtypeStruct((slots, SIDE, SIDE), jnp.bfloat16),
        in_specs=[
            smem,
            smem,
            smem,
            smem,
            smem,
            pl.BlockSpec((1, 1, rows), lambda v: (v, 0, 0)),
            pl.BlockSpec((1, 1, rows, cols), lambda v: (v, 0, 0, 0)),
            pl.BlockSpec((1, rows, cols), lambda v: (0, 0, 0)),
        ],
        out_specs=pl.BlockSpec((slots, SIDE, SIDE), lambda v: (0, 0, 0)),
        scratch_shapes=[
            pltpu.SMEM((devices,), jnp.int32),
            pltpu.VMEM((rows, rows), jnp.bfloat16),
            pltpu.VMEM((rows, cols), jnp.bfloat16),
            pltpu.VMEM((rows, cols), jnp.bfloat16),
        ],
        compiler_params=params,
        name="warp",
    )(
        owners,
        psf_taps,
        term_weights.reshape(visits, -1),
        warp_shift.reshape(visits, 2),
        warp_scale.reshape(visits, 2),
        bias_rows,
        raw_pixels,
        flat_field,
    )
    arrived = lax.all_to_all(send, ("sec", "p"), split_axis=0, concat_axis=0, tiled=True)

    slot_table, weight_of = pl.pallas_call(
        functools.partial(table_kernel, split),
        out_shape=(
            jax.ShapeDtypeStruct((slots,), jnp.int32),
            jax.ShapeDtypeStruct((slots,), jnp.float32),
        ),
        in_specs=[smem, smem, smem],
        out_specs=(smem, smem),
        scratch_shapes=[pltpu.SMEM((nz,), jnp.int32)],
        name="tables",
    )(me, meta, weight_table)

    group = ns * pn
    partial_sums = pl.pallas_call(
        functools.partial(reduce_kernel, nz),
        grid=(nz,),
        out_shape=jax.ShapeDtypeStruct((nz, PATCH_DEV, SIDE, SIDE), jnp.bfloat16),
        in_specs=[
            smem,
            smem,
            pl.BlockSpec((group, 1, CAP, SIDE, SIDE), lambda v: (0, v, 0, 0, 0)),
        ],
        out_specs=pl.BlockSpec((1, PATCH_DEV, SIDE, SIDE), lambda v: (v, 0, 0, 0)),
        scratch_shapes=[pltpu.VMEM((PATCH_DEV, SIDE, SIDE), jnp.float32)],
        compiler_params=params,
        name="plane_sums",
    )(slot_table, weight_of, arrived.reshape(group, nz, CAP, SIDE, SIDE))
    gathered = lax.all_to_all(partial_sums, "z", split_axis=0, concat_axis=0, tiled=True)

    per_field = meta.reshape(devices, 3, blocks)
    width = PATCH_DEV * SIDE
    coadd, low_rows, high_rows = pl.pallas_call(
        coadd_kernel,
        out_shape=(
            jax.ShapeDtypeStruct((SIDE, width), jnp.float32),
            jax.ShapeDtypeStruct((HALO, width), jnp.bfloat16),
            jax.ShapeDtypeStruct((HALO, width), jnp.bfloat16),
        ),
        in_specs=[smem, smem, vmem, vmem, vmem, vmem],
        out_specs=(vmem, vmem, vmem),
        compiler_params=params,
        name="coadd",
    )(me, weight_table, per_field[:, 0], per_field[:, 1], per_field[:, 2], gathered)

    forward = [(i, i + 1) for i in range(devices - 1)]
    backward = [(i + 1, i) for i in range(devices - 1)]
    low = lax.ppermute(low_rows, ("sec", "z", "p"), forward)
    high = lax.ppermute(high_rows, ("sec", "z", "p"), backward)

    detection = pl.pallas_call(
        detect_kernel,
        out_shape=jax.ShapeDtypeStruct((SIDE, width), jnp.float32),
        in_specs=[smem, vmem, vmem, vmem],
        out_specs=vmem,
        scratch_shapes=[
            pltpu.VMEM((2 * SIDE, width), jnp.float32),
            pltpu.VMEM((width, width), jnp.float32),
        ],
        compiler_params=params,
        name="detection",
    )(detect_taps, coadd, low, high)
    return coadd, detection


def solution(mesh):
    ns, nd = mesh.shape["sec"], mesh.shape["dev"]
    nz = math.gcd(nd, 4)
    pn = nd // nz
    cut = Mesh(mesh.devices.reshape(ns, nz, pn), ("sec", "z", "p"))
    every = ("sec", "z", "p")
    placed = (
        P(None, every, None, None),
        P(every, None, None),
        P(None, every, None),
        P(),
        P(None, every, None),
        P(None, every, None),
        P(None, every, None),
        P(every, None),
        P(every, None),
        P(every, None),
        P(),
        P(),
    )
    return jax.shard_map(
        functools.partial(per_device, (nz, pn, ns)),
        mesh=cut,
        in_specs=placed,
        out_specs=(P(every, None), P(every, None)),
        check_vma=False,
    )
```

```python
import functools
import math

import jax
import jax.numpy as jnp
from jax import lax
from jax.experimental import pallas as pl
from jax.experimental.pallas import tpu as pltpu
from jax.sharding import Mesh
from jax.sharding import PartitionSpec as P

SIDE = 128
CAP = 2
PATCH_DEV = 4
HALO = 32
FIELDS = 4
VMEM_LIMIT = 48 * 1024 * 1024


def tap_row(tap, count, start, width, reverse):
    lane = lax.broadcasted_iota(jnp.int32, (1, width), 1)
    row = jnp.zeros((1, width), jnp.float32)
    for k in range(count):
        at = start + (count - 1 - k if reverse else k)
        row = jnp.where(lane == at % width, tap(k), row)
    return row


def toeplitz(row, height):
    return pltpu.roll(
        jnp.broadcast_to(row, (height, row.shape[1])), 0, 1, stride=1, stride_axis=0
    )


def store_band(band_ref, tiles):
    blocks = band_ref.shape[0] // SIDE
    for i in range(blocks):
        for j in range(blocks):
            place = (pl.ds(i * SIDE, SIDE), pl.ds(j * SIDE, SIDE))
            if abs(i - j) <= 1:
                first = (j - i + 1) * SIDE
                band_ref[place] = tiles[:, first : first + SIDE]
            else:
                band_ref[place] = jnp.zeros((SIDE, SIDE), band_ref.dtype)


def dot32(left, right):
    return jnp.dot(left, right, preferred_element_type=jnp.float32)


def two_parts(value):
    high = value.astype(jnp.bfloat16)
    return high, (value - high.astype(jnp.float32)).astype(jnp.bfloat16)


def three_parts(value):
    high = value.astype(jnp.bfloat16)
    rest = value - high.astype(jnp.float32)
    mid = rest.astype(jnp.bfloat16)
    return high, mid, (rest - mid.astype(jnp.float32)).astype(jnp.bfloat16)


def warp_kernel(
    split,
    owner_hbm,
    patch_hbm,
    index_hbm,
    table_hbm,
    taps_hbm,
    weights_hbm,
    shift_hbm,
    scale_hbm,
    bias_hbm,
    raw_hbm,
    flat_hbm,
    out_ref,
    owner_ref,
    patch_ref,
    index_ref,
    table_ref,
    taps_ref,
    weights_ref,
    shift_ref,
    scale_ref,
    bias_ref,
    raw_ref,
    flat_ref,
    count_ref,
    band_ref,
    left_ref,
    mid_ref,
    slot_rows,
    weight_rows,
    small_sem,
    flat_sem,
    raw_sem,
):
    nz, pn = split
    visits, _, rows, cols = raw_ref.shape
    terms, tap_count = taps_ref.shape[1], taps_ref.shape[3]
    half = tap_count // 2
    per_dest = nz * CAP
    data_rows = per_dest * SIDE

    small = [
        pltpu.make_async_copy(src, dst, small_sem.at[i])
        for i, (src, dst) in enumerate(
            (
                (taps_hbm, taps_ref),
                (bias_hbm, bias_ref),
                (owner_hbm, owner_ref),
                (patch_hbm, patch_ref),
                (index_hbm, index_ref),
                (table_hbm, table_ref),
                (weights_hbm, weights_ref),
                (shift_hbm, shift_ref),
                (scale_hbm, scale_ref),
            )
        )
    ]
    for copy in small:
        copy.start()
    flat_copy = pltpu.make_async_copy(flat_hbm, flat_ref, flat_sem)
    raw_copies = [
        pltpu.make_async_copy(raw_hbm.at[v], raw_ref.at[v], raw_sem.at[v]) for v in range(visits)
    ]
    raw_copies[0].start()
    flat_copy.start()
    for copy in raw_copies[1:]:
        copy.start()

    out_ref[...] = jnp.zeros_like(out_ref)
    slot_rows[...] = jnp.full(slot_rows.shape, -1.0, jnp.float32)
    weight_rows[...] = jnp.zeros_like(weight_rows)

    def clear(i, c):
        count_ref[i] = 0
        return c

    lax.fori_loop(0, count_ref.shape[0], clear, 0)
    for copy in small:
        copy.wait()

    def hat(length, axis, shift, scale):
        centre = (length - 1) / 2.0
        shape = (1, length) if axis == 1 else (length, 1)
        out_pos = lax.broadcasted_iota(jnp.int32, shape, axis).astype(jnp.float32)
        source = scale * (out_pos - centre) + centre + shift
        in_pos = lax.broadcasted_iota(jnp.int32, (length, length), 1 - axis).astype(jnp.float32)
        return jnp.maximum(0.0, 1.0 - jnp.abs(in_pos - source)).astype(jnp.bfloat16)

    row_blocks, col_blocks = rows // SIDE, cols // SIDE
    for visit in range(visits):
        bias = jnp.broadcast_to(bias_ref[visit], (SIDE, rows)).T
        raw_copies[visit].wait()
        if visit == 0:
            flat_copy.wait()
        for j in range(cols // SIDE):
            sl = pl.ds(j * SIDE, SIDE)
            left_ref[:, sl] = ((raw_ref[visit, 0, :, sl] - bias) * flat_ref[0, :, sl]).astype(
                jnp.bfloat16
            )

        matched = None
        for term in range(terms):
            across = tap_row(
                lambda k: taps_ref[visit, term, 1, k], tap_count, SIDE - half, 3 * SIDE, True
            )
            store_band(band_ref, toeplitz(across, SIDE).astype(jnp.bfloat16))
            mid_ref[...] = dot32(left_ref[...], band_ref[...]).astype(jnp.bfloat16)
            down = tap_row(
                lambda k: taps_ref[visit, term, 0, k], tap_count, SIDE - half, 3 * SIDE, False
            )
            store_band(band_ref, toeplitz(down, SIDE).astype(jnp.bfloat16))
            part = weights_ref[0, term, visit] * dot32(band_ref[...], mid_ref[...])
            matched = part if matched is None else matched + part
        left_ref[...] = matched.astype(jnp.bfloat16)

        band_ref[...] = hat(cols, 1, shift_ref[visit, 0, 1], scale_ref[visit, 0, 1])
        mid_ref[...] = dot32(left_ref[...], band_ref[...]).astype(jnp.bfloat16)
        band_ref[...] = hat(rows, 0, shift_ref[visit, 0, 0], scale_ref[visit, 0, 0])
        left_ref[...] = dot32(band_ref[...], mid_ref[...]).astype(jnp.bfloat16)

        for i in range(row_blocks):
            for j in range(col_blocks):
                block = visit * (row_blocks * col_blocks) + i * col_blocks + j
                owner = owner_ref[block]
                rank = count_ref[owner]
                count_ref[owner] = rank + 1
                sec = owner // (nz * pn)
                dev = owner - sec * (nz * pn)
                z = dev // pn
                dest = sec * pn + dev - z * pn
                at = z * CAP + rank
                out_ref[dest, pl.ds(pl.multiple_of(at * SIDE, SIDE), SIDE), :] = left_ref[
                    pl.ds(i * SIDE, SIDE), pl.ds(j * SIDE, SIDE)
                ]
                line = pl.ds(dest * per_dest + at, 1)
                slot_rows[line, :] = jnp.full((1, SIDE), patch_ref[block].astype(jnp.float32))
                weight_rows[line, :] = jnp.full((1, SIDE), table_ref[index_ref[block]])

    for dest in range(out_ref.shape[0]):
        part = pl.ds(dest * per_dest, per_dest)
        fields = jnp.concatenate(
            [slot_rows[part, :]]
            + [w.astype(jnp.float32) for w in three_parts(weight_rows[part, :])],
            axis=0,
        )
        out_ref[dest, pl.ds(data_rows, fields.shape[0]), :] = fields.astype(jnp.bfloat16)


def sum_kernel(nz, in_ref, out_ref, weight_ref):
    sources = in_ref.shape[0]
    per_dest = nz * CAP
    data_rows = per_dest * SIDE
    for g in range(sources):
        fields = in_ref[g, pl.ds(data_rows, FIELDS * per_dest), :].astype(jnp.float32)
        slot = fields[:per_dest]
        weight = (
            fields[per_dest : 2 * per_dest]
            + fields[2 * per_dest : 3 * per_dest]
            + fields[3 * per_dest :]
        )
        for j in range(PATCH_DEV):
            weight_ref[g, j] = jnp.where(slot == float(j), weight, 0.0)
    step = 32
    for z in range(nz):
        for c in range(SIDE // step):
            sums = [jnp.zeros((step, SIDE), jnp.float32) for _ in range(PATCH_DEV)]
            for g in range(sources):
                for r in range(CAP):
                    at = z * CAP + r
                    value = in_ref[g, pl.ds(at * SIDE + c * step, step), :].astype(jnp.float32)
                    for j in range(PATCH_DEV):
                        sums[j] = sums[j] + weight_ref[g, j, pl.ds(at, 1), :] * value
            for j in range(PATCH_DEV):
                out_ref[z, pl.ds(j * SIDE + c * step, step), :] = sums[j].astype(jnp.bfloat16)
        totals = []
        for j in range(PATCH_DEV):
            total = jnp.zeros((1, SIDE), jnp.float32)
            for g in range(sources):
                for r in range(CAP):
                    total = total + weight_ref[g, j, pl.ds(z * CAP + r, 1), :]
            totals.append(total)
        parts = three_parts(jnp.concatenate(totals, axis=0))
        extra = jnp.concatenate(
            [q.astype(jnp.float32) for q in parts] + [jnp.zeros((PATCH_DEV, SIDE), jnp.float32)],
            axis=0,
        )
        out_ref[z, pl.ds(PATCH_DEV * SIDE, FIELDS * PATCH_DEV), :] = extra.astype(jnp.bfloat16)


def coadd_kernel(in_ref, coadd_ref, main_ref, rest_ref, low_ref, high_ref):
    sources = in_ref.shape[0]
    total = jnp.zeros((PATCH_DEV, SIDE), jnp.float32)
    for z in range(sources):
        extra = in_ref[z, pl.ds(PATCH_DEV * SIDE, FIELDS * PATCH_DEV), :].astype(jnp.float32)
        total = total + (
            extra[:PATCH_DEV] + extra[PATCH_DEV : 2 * PATCH_DEV] + extra[2 * PATCH_DEV : 3 * PATCH_DEV]
        )
    total = jnp.maximum(total, 1.0)
    for j in range(PATCH_DEV):
        numerator = in_ref[0, pl.ds(j * SIDE, SIDE), :].astype(jnp.float32)
        for z in range(1, sources):
            numerator = numerator + in_ref[z, pl.ds(j * SIDE, SIDE), :].astype(jnp.float32)
        tile = numerator / total[j : j + 1]
        sl = pl.ds(j * SIDE, SIDE)
        coadd_ref[:, sl] = tile
        main, rest = two_parts(tile)
        main_ref[:, sl] = main
        rest_ref[:, sl] = rest
        high_ref[:, sl] = main[:HALO]
        low_ref[:, sl] = main[SIDE - HALO :]


def prepare_kernel(taps_ref, across_ref, centre_ref, edge_ref, band_ref):
    tap_count = taps_ref.shape[1]
    half = tap_count // 2
    across = tap_row(lambda k: taps_ref[1, k], tap_count, SIDE - half, 3 * SIDE, True)
    store_band(band_ref, toeplitz(across, SIDE))
    across_ref[0], across_ref[1] = two_parts(band_ref[...])
    down = tap_row(lambda k: taps_ref[0, k], tap_count, SIDE - half, 3 * SIDE, False)
    centre_ref[0], centre_ref[1] = two_parts(toeplitz(down, SIDE)[:, SIDE : 2 * SIDE])
    lane = lax.broadcasted_iota(jnp.int32, (2 * HALO, SIDE), 1)
    row = lax.broadcasted_iota(jnp.int32, (2 * HALO, SIDE), 0)
    before = tap_row(lambda k: taps_ref[0, k], tap_count, HALO - half, SIDE, False)
    after = tap_row(lambda k: taps_ref[0, k], tap_count, SIDE - HALO - half, SIDE, False)
    edge = jnp.where(
        (row < HALO) & (lane < HALO),
        toeplitz(before, 2 * HALO),
        jnp.where(
            (row >= HALO) & (lane >= HALO) & (lane < 2 * HALO), toeplitz(after, 2 * HALO), 0.0
        ),
    )
    edge_ref[0], edge_ref[1] = two_parts(edge[:, : 2 * HALO])


def dot_parts(left, across_ref):
    main, rest = two_parts(left)
    return dot32(main, across_ref[0]) + (dot32(main, across_ref[1]) + dot32(rest, across_ref[0]))


def centre_kernel(main_ref, rest_ref, across_ref, centre_ref, out_ref):
    main = main_ref[...]
    along = dot32(centre_ref[0], main) + (
        dot32(centre_ref[0], rest_ref[...]) + dot32(centre_ref[1], main)
    )
    out_ref[...] = dot_parts(along, across_ref)


def edge_kernel(inner_ref, low_ref, high_ref, across_ref, edge_ref, out_ref):
    halo = jnp.concatenate([low_ref[...], high_ref[...]], axis=0)
    along = dot32(edge_ref[0], halo) + dot32(edge_ref[1], halo)
    extra = dot_parts(along, across_ref)
    out_ref[pl.ds(0, HALO)] = inner_ref[pl.ds(0, HALO)] + extra[:HALO]
    out_ref[pl.ds(HALO, SIDE - 2 * HALO)] = inner_ref[pl.ds(HALO, SIDE - 2 * HALO)]
    out_ref[pl.ds(SIDE - HALO, HALO)] = inner_ref[pl.ds(SIDE - HALO, HALO)] + extra[HALO:]


def per_device(
    split,
    raw_pixels,
    flat_field,
    bias_rows,
    psf_taps,
    term_weights,
    warp_shift,
    warp_scale,
    owner_of,
    patch_slot,
    weight_index,
    weight_table,
    detect_taps,
):
    nz, pn, ns = split
    devices = nz * pn * ns
    group = ns * pn
    visits, _, rows, cols = raw_pixels.shape
    blocks = owner_of.shape[0]
    per_dest = nz * CAP
    width = PATCH_DEV * SIDE
    smem = pl.BlockSpec(memory_space=pltpu.SMEM)
    vmem = pl.BlockSpec(memory_space=pltpu.VMEM)
    hbm = pl.BlockSpec(memory_space=pltpu.HBM)
    params = pltpu.CompilerParams(vmem_limit_bytes=VMEM_LIMIT)

    def shaped(shape, dtype):
        return jax.ShapeDtypeStruct(shape, dtype)

    weights = term_weights.transpose(1, 2, 0)
    send = pl.pallas_call(
        functools.partial(warp_kernel, (nz, pn)),
        out_shape=shaped((group, per_dest * SIDE + FIELDS * per_dest, SIDE), jnp.bfloat16),
        in_specs=[hbm] * 11,
        out_specs=vmem,
        scratch_shapes=[
            pltpu.SMEM((blocks,), jnp.int32),
            pltpu.SMEM((blocks,), jnp.int32),
            pltpu.SMEM((blocks,), jnp.int32),
            pltpu.SMEM(weight_table.shape, jnp.float32),
            pltpu.SMEM(psf_taps.shape, jnp.float32),
            pltpu.SMEM(weights.shape, jnp.float32),
            pltpu.SMEM(warp_shift.shape, jnp.float32),
            pltpu.SMEM(warp_scale.shape, jnp.float32),
            pltpu.VMEM(bias_rows.shape, jnp.float32),
            pltpu.VMEM(raw_pixels.shape, jnp.float32),
            pltpu.VMEM(flat_field.shape, jnp.float32),
            pltpu.SMEM((devices,), jnp.int32),
            pltpu.VMEM((rows, cols), jnp.bfloat16),
            pltpu.VMEM((rows, cols), jnp.bfloat16),
            pltpu.VMEM((rows, cols), jnp.bfloat16),
            pltpu.VMEM((group * per_dest, SIDE), jnp.float32),
            pltpu.VMEM((group * per_dest, SIDE), jnp.float32),
            pltpu.SemaphoreType.DMA((9,)),
            pltpu.SemaphoreType.DMA,
            pltpu.SemaphoreType.DMA((visits,)),
        ],
        compiler_params=pltpu.CompilerParams(vmem_limit_bytes=60 * 1024 * 1024),
        name="warp",
    )(
        owner_of.reshape(blocks),
        patch_slot.reshape(blocks),
        weight_index.reshape(blocks),
        weight_table,
        psf_taps,
        weights,
        warp_shift,
        warp_scale,
        bias_rows,
        raw_pixels,
        flat_field,
    )
    arrived = lax.all_to_all(send, ("sec", "p"), split_axis=0, concat_axis=0, tiled=True)

    across, centre, edge = pl.pallas_call(
        prepare_kernel,
        out_shape=(
            shaped((2, width, width), jnp.bfloat16),
            shaped((2, SIDE, SIDE), jnp.bfloat16),
            shaped((2, 2 * HALO, 2 * HALO), jnp.bfloat16),
        ),
        in_specs=[smem],
        out_specs=(vmem, vmem, vmem),
        scratch_shapes=[pltpu.VMEM((width, width), jnp.float32)],
        compiler_params=params,
        name="matrices",
    )(detect_taps)

    plane_sums = pl.pallas_call(
        functools.partial(sum_kernel, nz),
        out_shape=shaped((nz, PATCH_DEV * SIDE + FIELDS * PATCH_DEV, SIDE), jnp.bfloat16),
        in_specs=[vmem],
        out_specs=vmem,
        scratch_shapes=[pltpu.VMEM((group, PATCH_DEV, per_dest, SIDE), jnp.float32)],
        compiler_params=params,
        name="plane_sums",
    )(arrived)
    gathered = lax.all_to_all(plane_sums, "z", split_axis=0, concat_axis=0, tiled=True)

    coadd, main, rest, low_rows, high_rows = pl.pallas_call(
        coadd_kernel,
        out_shape=(
            shaped((SIDE, width), jnp.float32),
            shaped((SIDE, width), jnp.bfloat16),
            shaped((SIDE, width), jnp.bfloat16),
            shaped((HALO, width), jnp.bfloat16),
            shaped((HALO, width), jnp.bfloat16),
        ),
        in_specs=[vmem],
        out_specs=(vmem,) * 5,
        compiler_params=params,
        name="coadd",
    )(gathered)

    every = ("sec", "z", "p")
    low = lax.ppermute(low_rows, every, [(i, i + 1) for i in range(devices - 1)])
    high = lax.ppermute(high_rows, every, [(i + 1, i) for i in range(devices - 1)])

    inner = pl.pallas_call(
        centre_kernel,
        out_shape=shaped((SIDE, width), jnp.float32),
        in_specs=[vmem] * 4,
        out_specs=vmem,
        compiler_params=params,
        cost_estimate=pl.CostEstimate(
            flops=6 * SIDE * width * (SIDE + width), bytes_accessed=2 << 20, transcendentals=0
        ),
        name="detect_centre",
    )(main, rest, across, centre)
    detection = pl.pallas_call(
        edge_kernel,
        out_shape=shaped((SIDE, width), jnp.float32),
        in_specs=[vmem] * 5,
        out_specs=vmem,
        compiler_params=params,
        name="detect_edges",
    )(inner, low, high, across, edge)
    return coadd, detection


def solution(mesh):
    ns, nd = mesh.shape["sec"], mesh.shape["dev"]
    nz = math.gcd(nd, 4)
    pn = nd // nz
    cut = Mesh(mesh.devices.reshape(ns, nz, pn), ("sec", "z", "p"))
    every = ("sec", "z", "p")
    placed = (
        P(None, every, None, None),
        P(every, None, None),
        P(None, every, None),
        P(),
        P(None, every, None),
        P(None, every, None),
        P(None, every, None),
        P(every, None),
        P(every, None),
        P(every, None),
        P(),
        P(),
    )
    return jax.shard_map(
        functools.partial(per_device, (nz, pn, ns)),
        mesh=cut,
        in_specs=placed,
        out_specs=(P(every, None), P(every, None)),
        check_vma=False,
    )
```

```python
import functools
import math

import jax
import jax.numpy as jnp
from jax import lax
from jax.experimental import pallas as pl
from jax.experimental.pallas import tpu as pltpu
from jax.sharding import Mesh
from jax.sharding import PartitionSpec as P

SIDE = 128
CAP = 2
PATCH_DEV = 4
HALO = 32
FIELDS = 4
VMEM_LIMIT = 48 * 1024 * 1024


def tap_row(tap, count, start, width, reverse):
    lane = lax.broadcasted_iota(jnp.int32, (1, width), 1)
    row = jnp.zeros((1, width), jnp.float32)
    for k in range(count):
        at = start + (count - 1 - k if reverse else k)
        row = jnp.where(lane == at % width, tap(k), row)
    return row


def toeplitz(row, height):
    return pltpu.roll(
        jnp.broadcast_to(row, (height, row.shape[1])), 0, 1, stride=1, stride_axis=0
    )


def store_band(band_ref, tiles):
    blocks = band_ref.shape[0] // SIDE
    for i in range(blocks):
        for j in range(blocks):
            place = (pl.ds(i * SIDE, SIDE), pl.ds(j * SIDE, SIDE))
            if abs(i - j) <= 1:
                first = (j - i + 1) * SIDE
                band_ref[place] = tiles[:, first : first + SIDE]
            else:
                band_ref[place] = jnp.zeros((SIDE, SIDE), band_ref.dtype)


def dot32(left, right):
    return jnp.dot(left, right, preferred_element_type=jnp.float32)


def two_parts(value):
    high = value.astype(jnp.bfloat16)
    return high, (value - high.astype(jnp.float32)).astype(jnp.bfloat16)


def three_parts(value):
    high = value.astype(jnp.bfloat16)
    rest = value - high.astype(jnp.float32)
    mid = rest.astype(jnp.bfloat16)
    return high, mid, (rest - mid.astype(jnp.float32)).astype(jnp.bfloat16)


def warp_kernel(
    split,
    owner_hbm,
    patch_hbm,
    index_hbm,
    table_hbm,
    taps_hbm,
    weights_hbm,
    shift_hbm,
    scale_hbm,
    bias_hbm,
    raw_hbm,
    flat_hbm,
    *rest,
):
    nz, pn, ns = split
    outs, rest = rest[: ns * pn], rest[ns * pn :]
    warp_body(
        split,
        (
            owner_hbm,
            patch_hbm,
            index_hbm,
            table_hbm,
            taps_hbm,
            weights_hbm,
            shift_hbm,
            scale_hbm,
            bias_hbm,
            raw_hbm,
            flat_hbm,
        ),
        outs,
        *rest,
    )


def warp_body(
    split,
    inputs,
    outs,
    owner_ref,
    patch_ref,
    index_ref,
    table_ref,
    taps_ref,
    weights_ref,
    shift_ref,
    scale_ref,
    bias_ref,
    raw_ref,
    flat_ref,
    count_ref,
    band_ref,
    left_ref,
    mid_ref,
    slot_rows,
    weight_rows,
    small_sem,
    flat_sem,
    raw_sem,
    out_ref,
    out_sem,
):
    (
        owner_hbm,
        patch_hbm,
        index_hbm,
        table_hbm,
        taps_hbm,
        weights_hbm,
        shift_hbm,
        scale_hbm,
        bias_hbm,
        raw_hbm,
        flat_hbm,
    ) = inputs
    nz, pn, ns = split
    mine = lax.axis_index("sec") * pn + lax.axis_index("p")
    visits, _, rows, cols = raw_ref.shape
    terms, tap_count = taps_ref.shape[1], taps_ref.shape[3]
    half = tap_count // 2
    per_dest = nz * CAP
    data_rows = per_dest * SIDE

    small = [
        pltpu.make_async_copy(src, dst, small_sem.at[i])
        for i, (src, dst) in enumerate(
            (
                (taps_hbm, taps_ref),
                (bias_hbm, bias_ref),
                (owner_hbm, owner_ref),
                (patch_hbm, patch_ref),
                (index_hbm, index_ref),
                (table_hbm, table_ref),
                (weights_hbm, weights_ref),
                (shift_hbm, shift_ref),
                (scale_hbm, scale_ref),
            )
        )
    ]
    for copy in small:
        copy.start()
    flat_copy = pltpu.make_async_copy(flat_hbm, flat_ref, flat_sem)
    raw_copies = [
        pltpu.make_async_copy(raw_hbm.at[v], raw_ref.at[v], raw_sem.at[v]) for v in range(visits)
    ]
    raw_copies[0].start()
    flat_copy.start()
    for copy in raw_copies[1:]:
        copy.start()

    out_ref[...] = jnp.zeros_like(out_ref)
    slot_rows[...] = jnp.full(slot_rows.shape, -1.0, jnp.float32)
    weight_rows[...] = jnp.zeros_like(weight_rows)

    def clear(i, c):
        count_ref[i] = 0
        return c

    lax.fori_loop(0, count_ref.shape[0], clear, 0)
    for copy in small:
        copy.wait()

    def hat(length, axis, shift, scale):
        centre = (length - 1) / 2.0
        shape = (1, length) if axis == 1 else (length, 1)
        out_pos = lax.broadcasted_iota(jnp.int32, shape, axis).astype(jnp.float32)
        source = scale * (out_pos - centre) + centre + shift
        in_pos = lax.broadcasted_iota(jnp.int32, (length, length), 1 - axis).astype(jnp.float32)
        return jnp.maximum(0.0, 1.0 - jnp.abs(in_pos - source)).astype(jnp.bfloat16)

    row_blocks, col_blocks = rows // SIDE, cols // SIDE
    for visit in range(visits):
        bias = jnp.broadcast_to(bias_ref[visit], (SIDE, rows)).T
        raw_copies[visit].wait()
        if visit == 0:
            flat_copy.wait()
        for j in range(cols // SIDE):
            sl = pl.ds(j * SIDE, SIDE)
            left_ref[:, sl] = ((raw_ref[visit, 0, :, sl] - bias) * flat_ref[0, :, sl]).astype(
                jnp.bfloat16
            )

        matched = None
        for term in range(terms):
            across = tap_row(
                lambda k: taps_ref[visit, term, 1, k], tap_count, SIDE - half, 3 * SIDE, True
            )
            store_band(band_ref, toeplitz(across, SIDE).astype(jnp.bfloat16))
            mid_ref[...] = dot32(left_ref[...], band_ref[...]).astype(jnp.bfloat16)
            down = tap_row(
                lambda k: taps_ref[visit, term, 0, k], tap_count, SIDE - half, 3 * SIDE, False
            )
            store_band(band_ref, toeplitz(down, SIDE).astype(jnp.bfloat16))
            part = weights_ref[0, term, visit] * dot32(band_ref[...], mid_ref[...])
            matched = part if matched is None else matched + part
        left_ref[...] = matched.astype(jnp.bfloat16)

        band_ref[...] = hat(cols, 1, shift_ref[visit, 0, 1], scale_ref[visit, 0, 1])
        mid_ref[...] = dot32(left_ref[...], band_ref[...]).astype(jnp.bfloat16)
        band_ref[...] = hat(rows, 0, shift_ref[visit, 0, 0], scale_ref[visit, 0, 0])
        left_ref[...] = dot32(band_ref[...], mid_ref[...]).astype(jnp.bfloat16)

        for i in range(row_blocks):
            for j in range(col_blocks):
                block = visit * (row_blocks * col_blocks) + i * col_blocks + j
                owner = owner_ref[block]
                rank = count_ref[owner]
                count_ref[owner] = rank + 1
                sec = owner // (nz * pn)
                dev = owner - sec * (nz * pn)
                z = dev // pn
                dest = (sec * pn + dev - z * pn) ^ mine
                at = (z ^ lax.axis_index("z")) * CAP + rank
                out_ref[dest, pl.ds(pl.multiple_of(at * SIDE, SIDE), SIDE), :] = left_ref[
                    pl.ds(i * SIDE, SIDE), pl.ds(j * SIDE, SIDE)
                ]
                line = pl.ds(dest * per_dest + at, 1)
                slot_rows[line, :] = jnp.full((1, SIDE), patch_ref[block].astype(jnp.float32))
                weight_rows[line, :] = jnp.full((1, SIDE), table_ref[index_ref[block]])

    def out_copy(dest):
        return pltpu.make_async_copy(out_ref.at[dest], outs[dest], out_sem.at[dest])

    for dest in range(out_ref.shape[0]):
        part = pl.ds(dest * per_dest, per_dest)
        fields = jnp.concatenate(
            [slot_rows[part, :]]
            + [w.astype(jnp.float32) for w in three_parts(weight_rows[part, :])],
            axis=0,
        )
        out_ref[dest, pl.ds(data_rows, fields.shape[0]), :] = fields.astype(jnp.bfloat16)
        out_copy(dest).start()
    for dest in range(out_ref.shape[0]):
        out_copy(dest).wait()


def sum_kernel(nz, sources, *refs):
    ins, outs, weight_ref = refs[:sources], refs[sources:-1], refs[-1]
    per_dest = nz * CAP
    data_rows = per_dest * SIDE
    for g in range(sources):
        fields = ins[g][pl.ds(data_rows, FIELDS * per_dest), :].astype(jnp.float32)
        slot = fields[:per_dest]
        weight = (
            fields[per_dest : 2 * per_dest]
            + fields[2 * per_dest : 3 * per_dest]
            + fields[3 * per_dest :]
        )
        for j in range(PATCH_DEV):
            weight_ref[g, j] = jnp.where(slot == float(j), weight, 0.0)
    step = 32
    for z in range(nz):
        for c in range(SIDE // step):
            sums = [jnp.zeros((step, SIDE), jnp.float32) for _ in range(PATCH_DEV)]
            for g in range(sources):
                for r in range(CAP):
                    at = z * CAP + r
                    value = ins[g][pl.ds(at * SIDE + c * step, step), :].astype(jnp.float32)
                    for j in range(PATCH_DEV):
                        sums[j] = sums[j] + weight_ref[g, j, pl.ds(at, 1), :] * value
            for j in range(PATCH_DEV):
                outs[z][pl.ds(j * SIDE + c * step, step), :] = sums[j].astype(jnp.bfloat16)
        totals = []
        for j in range(PATCH_DEV):
            total = jnp.zeros((1, SIDE), jnp.float32)
            for g in range(sources):
                for r in range(CAP):
                    total = total + weight_ref[g, j, pl.ds(z * CAP + r, 1), :]
            totals.append(total)
        parts = three_parts(jnp.concatenate(totals, axis=0))
        extra = jnp.concatenate(
            [q.astype(jnp.float32) for q in parts] + [jnp.zeros((PATCH_DEV, SIDE), jnp.float32)],
            axis=0,
        )
        outs[z][pl.ds(PATCH_DEV * SIDE, FIELDS * PATCH_DEV), :] = extra.astype(jnp.bfloat16)


def coadd_kernel(sources, *refs):
    ins, (coadd_ref, main_ref, rest_ref, low_ref, high_ref) = refs[:sources], refs[sources:]
    total = jnp.zeros((PATCH_DEV, SIDE), jnp.float32)
    for z in range(sources):
        extra = ins[z][pl.ds(PATCH_DEV * SIDE, FIELDS * PATCH_DEV), :].astype(jnp.float32)
        total = total + (
            extra[:PATCH_DEV] + extra[PATCH_DEV : 2 * PATCH_DEV] + extra[2 * PATCH_DEV : 3 * PATCH_DEV]
        )
    total = jnp.maximum(total, 1.0)
    for j in range(PATCH_DEV):
        numerator = ins[0][pl.ds(j * SIDE, SIDE), :].astype(jnp.float32)
        for z in range(1, sources):
            numerator = numerator + ins[z][pl.ds(j * SIDE, SIDE), :].astype(jnp.float32)
        tile = numerator / total[j : j + 1]
        sl = pl.ds(j * SIDE, SIDE)
        coadd_ref[:, sl] = tile
        main, rest = two_parts(tile)
        main_ref[:, sl] = main
        rest_ref[:, sl] = rest
        high_ref[:, sl] = main[:HALO]
        low_ref[:, sl] = main[SIDE - HALO :]


def prepare_kernel(taps_ref, across_ref, centre_ref, edge_ref, band_ref):
    tap_count = taps_ref.shape[1]
    half = tap_count // 2
    across = tap_row(lambda k: taps_ref[1, k], tap_count, SIDE - half, 3 * SIDE, True)
    store_band(band_ref, toeplitz(across, SIDE))
    across_ref[0], across_ref[1] = two_parts(band_ref[...])
    down = tap_row(lambda k: taps_ref[0, k], tap_count, SIDE - half, 3 * SIDE, False)
    centre_ref[0], centre_ref[1] = two_parts(toeplitz(down, SIDE)[:, SIDE : 2 * SIDE])
    lane = lax.broadcasted_iota(jnp.int32, (2 * HALO, SIDE), 1)
    row = lax.broadcasted_iota(jnp.int32, (2 * HALO, SIDE), 0)
    before = tap_row(lambda k: taps_ref[0, k], tap_count, HALO - half, SIDE, False)
    after = tap_row(lambda k: taps_ref[0, k], tap_count, SIDE - HALO - half, SIDE, False)
    edge = jnp.where(
        (row < HALO) & (lane < HALO),
        toeplitz(before, 2 * HALO),
        jnp.where(
            (row >= HALO) & (lane >= HALO) & (lane < 2 * HALO), toeplitz(after, 2 * HALO), 0.0
        ),
    )
    edge_ref[0], edge_ref[1] = two_parts(edge[:, : 2 * HALO])


def dot_parts(left, across_ref):
    main, rest = two_parts(left)
    return dot32(main, across_ref[0]) + (dot32(main, across_ref[1]) + dot32(rest, across_ref[0]))


def centre_kernel(main_ref, rest_ref, across_ref, centre_ref, out_ref):
    main = main_ref[...]
    along = dot32(centre_ref[0], main) + (
        dot32(centre_ref[0], rest_ref[...]) + dot32(centre_ref[1], main)
    )
    out_ref[...] = dot_parts(along, across_ref)


def edge_kernel(inner_ref, low_ref, high_ref, across_ref, edge_ref, out_ref):
    halo = jnp.concatenate([low_ref[...], high_ref[...]], axis=0)
    along = dot32(edge_ref[0], halo) + dot32(edge_ref[1], halo)
    extra = dot_parts(along, across_ref)
    out_ref[pl.ds(0, HALO)] = inner_ref[pl.ds(0, HALO)] + extra[:HALO]
    out_ref[pl.ds(HALO, SIDE - 2 * HALO)] = inner_ref[pl.ds(HALO, SIDE - 2 * HALO)]
    out_ref[pl.ds(SIDE - HALO, HALO)] = inner_ref[pl.ds(SIDE - HALO, HALO)] + extra[HALO:]


def per_device(
    split,
    raw_pixels,
    flat_field,
    bias_rows,
    psf_taps,
    term_weights,
    warp_shift,
    warp_scale,
    owner_of,
    patch_slot,
    weight_index,
    weight_table,
    detect_taps,
):
    nz, pn, ns = split
    devices = nz * pn * ns
    group = ns * pn
    visits, _, rows, cols = raw_pixels.shape
    blocks = owner_of.shape[0]
    per_dest = nz * CAP
    payload = per_dest * (SIDE + FIELDS)
    width = PATCH_DEV * SIDE
    smem = pl.BlockSpec(memory_space=pltpu.SMEM)
    vmem = pl.BlockSpec(memory_space=pltpu.VMEM)
    hbm = pl.BlockSpec(memory_space=pltpu.HBM)
    params = pltpu.CompilerParams(vmem_limit_bytes=VMEM_LIMIT)

    def shaped(shape, dtype):
        return jax.ShapeDtypeStruct(shape, dtype)

    weights = term_weights.transpose(1, 2, 0)
    send = pl.pallas_call(
        functools.partial(warp_kernel, split),
        out_shape=[shaped((payload, SIDE), jnp.bfloat16)] * group,
        in_specs=[hbm] * 11,
        out_specs=[hbm] * group,
        scratch_shapes=[
            pltpu.SMEM((blocks,), jnp.int32),
            pltpu.SMEM((blocks,), jnp.int32),
            pltpu.SMEM((blocks,), jnp.int32),
            pltpu.SMEM(weight_table.shape, jnp.float32),
            pltpu.SMEM(psf_taps.shape, jnp.float32),
            pltpu.SMEM(weights.shape, jnp.float32),
            pltpu.SMEM(warp_shift.shape, jnp.float32),
            pltpu.SMEM(warp_scale.shape, jnp.float32),
            pltpu.VMEM(bias_rows.shape, jnp.float32),
            pltpu.VMEM(raw_pixels.shape, jnp.float32),
            pltpu.VMEM(flat_field.shape, jnp.float32),
            pltpu.SMEM((devices,), jnp.int32),
            pltpu.VMEM((rows, cols), jnp.bfloat16),
            pltpu.VMEM((rows, cols), jnp.bfloat16),
            pltpu.VMEM((rows, cols), jnp.bfloat16),
            pltpu.VMEM((group * per_dest, SIDE), jnp.float32),
            pltpu.VMEM((group * per_dest, SIDE), jnp.float32),
            pltpu.SemaphoreType.DMA((9,)),
            pltpu.SemaphoreType.DMA,
            pltpu.SemaphoreType.DMA((visits,)),
            pltpu.VMEM((group, payload, SIDE), jnp.bfloat16),
            pltpu.SemaphoreType.DMA((group,)),
        ],
        compiler_params=pltpu.CompilerParams(vmem_limit_bytes=60 * 1024 * 1024),
        name="warp",
    )(
        owner_of.reshape(blocks),
        patch_slot.reshape(blocks),
        weight_index.reshape(blocks),
        weight_table,
        psf_taps,
        weights,
        warp_shift,
        warp_scale,
        bias_rows,
        raw_pixels,
        flat_field,
    )
    far_first = sorted(range(1, group), key=lambda k: (k == pn, -bin(k % pn).count("1")))
    arrived = [send[0]] + [
        lax.ppermute(send[k], ("sec", "p"), [(g, g ^ k) for g in range(group)])
        for k in far_first
    ]

    across, centre, edge = pl.pallas_call(
        prepare_kernel,
        out_shape=(
            shaped((2, width, width), jnp.bfloat16),
            shaped((2, SIDE, SIDE), jnp.bfloat16),
            shaped((2, 2 * HALO, 2 * HALO), jnp.bfloat16),
        ),
        in_specs=[smem],
        out_specs=(vmem, vmem, vmem),
        scratch_shapes=[pltpu.VMEM((width, width), jnp.float32)],
        compiler_params=params,
        name="matrices",
    )(detect_taps)

    plane_sums = pl.pallas_call(
        functools.partial(sum_kernel, nz, group),
        out_shape=[shaped((PATCH_DEV * (SIDE + FIELDS), SIDE), jnp.bfloat16)] * nz,
        in_specs=[vmem] * group,
        out_specs=[vmem] * nz,
        scratch_shapes=[pltpu.VMEM((group, PATCH_DEV, per_dest, SIDE), jnp.float32)],
        compiler_params=params,
        name="plane_sums",
    )(*arrived)
    gathered = [plane_sums[0]] + [
        lax.ppermute(plane_sums[d], "z", [(z, z ^ d) for z in range(nz)]) for d in range(1, nz)
    ]

    coadd, main, rest, low_rows, high_rows = pl.pallas_call(
        functools.partial(coadd_kernel, nz),
        out_shape=(
            shaped((SIDE, width), jnp.float32),
            shaped((SIDE, width), jnp.bfloat16),
            shaped((SIDE, width), jnp.bfloat16),
            shaped((HALO, width), jnp.bfloat16),
            shaped((HALO, width), jnp.bfloat16),
        ),
        in_specs=[vmem] * nz,
        out_specs=(vmem,) * 5,
        compiler_params=params,
        name="coadd",
    )(*gathered)

    every = ("sec", "z", "p")
    low = lax.ppermute(low_rows, every, [(i, i + 1) for i in range(devices - 1)])
    high = lax.ppermute(high_rows, every, [(i + 1, i) for i in range(devices - 1)])

    inner = pl.pallas_call(
        centre_kernel,
        out_shape=shaped((SIDE, width), jnp.float32),
        in_specs=[vmem] * 4,
        out_specs=vmem,
        compiler_params=params,
        cost_estimate=pl.CostEstimate(
            flops=6 * SIDE * width * (SIDE + width), bytes_accessed=2 << 20, transcendentals=0
        ),
        name="detect_centre",
    )(main, rest, across, centre)
    detection = pl.pallas_call(
        edge_kernel,
        out_shape=shaped((SIDE, width), jnp.float32),
        in_specs=[vmem] * 5,
        out_specs=vmem,
        compiler_params=params,
        name="detect_edges",
    )(inner, low, high, across, edge)
    return coadd, detection


def solution(mesh):
    ns, nd = mesh.shape["sec"], mesh.shape["dev"]
    nz = math.gcd(nd, 4)
    pn = nd // nz
    cut = Mesh(mesh.devices.reshape(ns, nz, pn), ("sec", "z", "p"))
    every = ("sec", "z", "p")
    placed = (
        P(None, every, None, None),
        P(every, None, None),
        P(None, every, None),
        P(),
        P(None, every, None),
        P(None, every, None),
        P(None, every, None),
        P(every, None),
        P(every, None),
        P(every, None),
        P(),
        P(),
    )
    return jax.shard_map(
        functools.partial(per_device, (nz, pn, ns)),
        mesh=cut,
        in_specs=placed,
        out_specs=(P(every, None), P(every, None)),
        check_vma=False,
    )
```

```python
import functools
import math

import jax
import jax.numpy as jnp
from jax import lax
from jax.experimental import pallas as pl
from jax.experimental.pallas import tpu as pltpu
from jax.sharding import Mesh
from jax.sharding import PartitionSpec as P

SIDE = 128
CAP = 2
PATCH_DEV = 4
HALO = 32
FIELDS = 4
ORDER = {2: 0, 3: 1, 7: 2, 1: 3, 5: 4, 6: 5}
VMEM_LIMIT = 48 * 1024 * 1024


def tap_row(tap, count, start, width, reverse):
    lane = lax.broadcasted_iota(jnp.int32, (1, width), 1)
    row = jnp.zeros((1, width), jnp.float32)
    for k in range(count):
        at = start + (count - 1 - k if reverse else k)
        row = jnp.where(lane == at % width, tap(k), row)
    return row


def toeplitz(row, height):
    return pltpu.roll(
        jnp.broadcast_to(row, (height, row.shape[1])), 0, 1, stride=1, stride_axis=0
    )


def store_band(band_ref, tiles):
    blocks = band_ref.shape[0] // SIDE
    for i in range(blocks):
        for j in range(blocks):
            place = (pl.ds(i * SIDE, SIDE), pl.ds(j * SIDE, SIDE))
            if abs(i - j) <= 1:
                first = (j - i + 1) * SIDE
                band_ref[place] = tiles[:, first : first + SIDE]
            else:
                band_ref[place] = jnp.zeros((SIDE, SIDE), band_ref.dtype)


def dot32(left, right):
    return jnp.dot(left, right, preferred_element_type=jnp.float32)


def two_parts(value):
    high = value.astype(jnp.bfloat16)
    return high, (value - high.astype(jnp.float32)).astype(jnp.bfloat16)


def three_parts(value):
    high = value.astype(jnp.bfloat16)
    rest = value - high.astype(jnp.float32)
    mid = rest.astype(jnp.bfloat16)
    return high, mid, (rest - mid.astype(jnp.float32)).astype(jnp.bfloat16)


def warp_kernel(
    split,
    owner_hbm,
    patch_hbm,
    index_hbm,
    table_hbm,
    taps_hbm,
    weights_hbm,
    shift_hbm,
    scale_hbm,
    bias_hbm,
    raw_hbm,
    flat_hbm,
    *rest,
):
    nz, pn, ns = split
    outs, rest = rest[: ns * pn], rest[ns * pn :]
    warp_body(
        split,
        (
            owner_hbm,
            patch_hbm,
            index_hbm,
            table_hbm,
            taps_hbm,
            weights_hbm,
            shift_hbm,
            scale_hbm,
            bias_hbm,
            raw_hbm,
            flat_hbm,
        ),
        outs,
        *rest,
    )


def warp_body(
    split,
    inputs,
    outs,
    owner_ref,
    patch_ref,
    index_ref,
    table_ref,
    taps_ref,
    weights_ref,
    shift_ref,
    scale_ref,
    bias_ref,
    raw_ref,
    flat_ref,
    count_ref,
    band_ref,
    left_ref,
    mid_ref,
    slot_rows,
    weight_rows,
    small_sem,
    flat_sem,
    raw_sem,
    out_ref,
    out_sem,
):
    (
        owner_hbm,
        patch_hbm,
        index_hbm,
        table_hbm,
        taps_hbm,
        weights_hbm,
        shift_hbm,
        scale_hbm,
        bias_hbm,
        raw_hbm,
        flat_hbm,
    ) = inputs
    nz, pn, ns = split
    mine = lax.axis_index("sec") * pn + lax.axis_index("p")
    visits, _, rows, cols = raw_ref.shape
    terms, tap_count = taps_ref.shape[1], taps_ref.shape[3]
    half = tap_count // 2
    per_dest = nz * CAP
    data_rows = per_dest * SIDE

    small = [
        pltpu.make_async_copy(src, dst, small_sem.at[i])
        for i, (src, dst) in enumerate(
            (
                (taps_hbm, taps_ref),
                (bias_hbm, bias_ref),
                (owner_hbm, owner_ref),
                (patch_hbm, patch_ref),
                (index_hbm, index_ref),
                (table_hbm, table_ref),
                (weights_hbm, weights_ref),
                (shift_hbm, shift_ref),
                (scale_hbm, scale_ref),
            )
        )
    ]
    for copy in small:
        copy.start()
    flat_copy = pltpu.make_async_copy(flat_hbm, flat_ref, flat_sem)
    raw_copies = [
        pltpu.make_async_copy(raw_hbm.at[v], raw_ref.at[v], raw_sem.at[v]) for v in range(visits)
    ]
    raw_copies[0].start()
    flat_copy.start()
    for copy in raw_copies[1:]:
        copy.start()

    out_ref[...] = jnp.zeros_like(out_ref)
    slot_rows[...] = jnp.full(slot_rows.shape, -1.0, jnp.float32)
    weight_rows[...] = jnp.zeros_like(weight_rows)

    def clear(i, c):
        count_ref[i] = 0
        return c

    lax.fori_loop(0, count_ref.shape[0], clear, 0)
    for copy in small:
        copy.wait()

    def hat(length, axis, shift, scale):
        centre = (length - 1) / 2.0
        shape = (1, length) if axis == 1 else (length, 1)
        out_pos = lax.broadcasted_iota(jnp.int32, shape, axis).astype(jnp.float32)
        source = scale * (out_pos - centre) + centre + shift
        in_pos = lax.broadcasted_iota(jnp.int32, (length, length), 1 - axis).astype(jnp.float32)
        return jnp.maximum(0.0, 1.0 - jnp.abs(in_pos - source)).astype(jnp.bfloat16)

    row_blocks, col_blocks = rows // SIDE, cols // SIDE
    for visit in range(visits):
        bias = jnp.broadcast_to(bias_ref[visit], (SIDE, rows)).T
        raw_copies[visit].wait()
        if visit == 0:
            flat_copy.wait()
        for j in range(cols // SIDE):
            sl = pl.ds(j * SIDE, SIDE)
            left_ref[:, sl] = ((raw_ref[visit, 0, :, sl] - bias) * flat_ref[0, :, sl]).astype(
                jnp.bfloat16
            )

        matched = None
        for term in range(terms):
            across = tap_row(
                lambda k: taps_ref[visit, term, 1, k], tap_count, SIDE - half, 3 * SIDE, True
            )
            store_band(band_ref, toeplitz(across, SIDE).astype(jnp.bfloat16))
            mid_ref[...] = dot32(left_ref[...], band_ref[...]).astype(jnp.bfloat16)
            down = tap_row(
                lambda k: taps_ref[visit, term, 0, k], tap_count, SIDE - half, 3 * SIDE, False
            )
            store_band(band_ref, toeplitz(down, SIDE).astype(jnp.bfloat16))
            part = weights_ref[0, term, visit] * dot32(band_ref[...], mid_ref[...])
            matched = part if matched is None else matched + part
        left_ref[...] = matched.astype(jnp.bfloat16)

        band_ref[...] = hat(cols, 1, shift_ref[visit, 0, 1], scale_ref[visit, 0, 1])
        mid_ref[...] = dot32(left_ref[...], band_ref[...]).astype(jnp.bfloat16)
        band_ref[...] = hat(rows, 0, shift_ref[visit, 0, 0], scale_ref[visit, 0, 0])
        left_ref[...] = dot32(band_ref[...], mid_ref[...]).astype(jnp.bfloat16)

        for i in range(row_blocks):
            for j in range(col_blocks):
                block = visit * (row_blocks * col_blocks) + i * col_blocks + j
                owner = owner_ref[block]
                rank = count_ref[owner]
                count_ref[owner] = rank + 1
                sec = owner // (nz * pn)
                dev = owner - sec * (nz * pn)
                z = dev // pn
                dest = (sec * pn + dev - z * pn) ^ mine
                at = (z ^ lax.axis_index("z")) * CAP + rank
                out_ref[dest, pl.ds(pl.multiple_of(at * SIDE, SIDE), SIDE), :] = left_ref[
                    pl.ds(i * SIDE, SIDE), pl.ds(j * SIDE, SIDE)
                ]
                line = pl.ds(dest * per_dest + at, 1)
                slot_rows[line, :] = jnp.full((1, SIDE), patch_ref[block].astype(jnp.float32))
                weight_rows[line, :] = jnp.full((1, SIDE), table_ref[index_ref[block]])

    def out_copy(dest):
        return pltpu.make_async_copy(out_ref.at[dest], outs[dest], out_sem.at[dest])

    for dest in range(out_ref.shape[0]):
        part = pl.ds(dest * per_dest, per_dest)
        fields = jnp.concatenate(
            [slot_rows[part, :]]
            + [w.astype(jnp.float32) for w in three_parts(weight_rows[part, :])],
            axis=0,
        )
        out_ref[dest, pl.ds(data_rows, fields.shape[0]), :] = fields.astype(jnp.bfloat16)
        out_copy(dest).start()
    for dest in range(out_ref.shape[0]):
        out_copy(dest).wait()


def sum_kernel(nz, sources, *refs):
    ins, outs, weight_ref = refs[:sources], refs[sources:-1], refs[-1]
    per_dest = nz * CAP
    data_rows = per_dest * SIDE
    for g in range(sources):
        fields = ins[g][pl.ds(data_rows, FIELDS * per_dest), :].astype(jnp.float32)
        slot = fields[:per_dest]
        weight = (
            fields[per_dest : 2 * per_dest]
            + fields[2 * per_dest : 3 * per_dest]
            + fields[3 * per_dest :]
        )
        for j in range(PATCH_DEV):
            weight_ref[g, j] = jnp.where(slot == float(j), weight, 0.0)
    step = 32
    for z in range(nz):
        for c in range(SIDE // step):
            sums = [jnp.zeros((step, SIDE), jnp.float32) for _ in range(PATCH_DEV)]
            for g in range(sources):
                for r in range(CAP):
                    at = z * CAP + r
                    value = ins[g][pl.ds(at * SIDE + c * step, step), :].astype(jnp.float32)
                    for j in range(PATCH_DEV):
                        sums[j] = sums[j] + weight_ref[g, j, pl.ds(at, 1), :] * value
            for j in range(PATCH_DEV):
                outs[z][pl.ds(j * SIDE + c * step, step), :] = sums[j].astype(jnp.bfloat16)
        totals = []
        for j in range(PATCH_DEV):
            total = jnp.zeros((1, SIDE), jnp.float32)
            for g in range(sources):
                for r in range(CAP):
                    total = total + weight_ref[g, j, pl.ds(z * CAP + r, 1), :]
            totals.append(total)
        parts = three_parts(jnp.concatenate(totals, axis=0))
        extra = jnp.concatenate(
            [q.astype(jnp.float32) for q in parts] + [jnp.zeros((PATCH_DEV, SIDE), jnp.float32)],
            axis=0,
        )
        outs[z][pl.ds(PATCH_DEV * SIDE, FIELDS * PATCH_DEV), :] = extra.astype(jnp.bfloat16)


def coadd_kernel(sources, *refs):
    ins, (coadd_ref, main_ref, rest_ref, low_ref, high_ref) = refs[:sources], refs[sources:]
    total = jnp.zeros((PATCH_DEV, SIDE), jnp.float32)
    for z in range(sources):
        extra = ins[z][pl.ds(PATCH_DEV * SIDE, FIELDS * PATCH_DEV), :].astype(jnp.float32)
        total = total + (
            extra[:PATCH_DEV] + extra[PATCH_DEV : 2 * PATCH_DEV] + extra[2 * PATCH_DEV : 3 * PATCH_DEV]
        )
    total = jnp.maximum(total, 1.0)
    for j in range(PATCH_DEV):
        numerator = ins[0][pl.ds(j * SIDE, SIDE), :].astype(jnp.float32)
        for z in range(1, sources):
            numerator = numerator + ins[z][pl.ds(j * SIDE, SIDE), :].astype(jnp.float32)
        tile = numerator / total[j : j + 1]
        sl = pl.ds(j * SIDE, SIDE)
        coadd_ref[:, sl] = tile
        main, rest = two_parts(tile)
        main_ref[:, sl] = main
        rest_ref[:, sl] = rest
        high_ref[:, sl] = main[:HALO]
        low_ref[:, sl] = main[SIDE - HALO :]


def prepare_kernel(taps_ref, own_hbm, across_ref, centre_ref, edge_ref, own_ref, band_ref, own_sem):
    own_copy = pltpu.make_async_copy(own_hbm, own_ref, own_sem)
    own_copy.start()
    tap_count = taps_ref.shape[1]
    half = tap_count // 2
    across = tap_row(lambda k: taps_ref[1, k], tap_count, SIDE - half, 3 * SIDE, True)
    store_band(band_ref, toeplitz(across, SIDE))
    across_ref[0], across_ref[1] = two_parts(band_ref[...])
    down = tap_row(lambda k: taps_ref[0, k], tap_count, SIDE - half, 3 * SIDE, False)
    centre_ref[0], centre_ref[1] = two_parts(toeplitz(down, SIDE)[:, SIDE : 2 * SIDE])
    lane = lax.broadcasted_iota(jnp.int32, (2 * HALO, SIDE), 1)
    row = lax.broadcasted_iota(jnp.int32, (2 * HALO, SIDE), 0)
    before = tap_row(lambda k: taps_ref[0, k], tap_count, HALO - half, SIDE, False)
    after = tap_row(lambda k: taps_ref[0, k], tap_count, SIDE - HALO - half, SIDE, False)
    edge = jnp.where(
        (row < HALO) & (lane < HALO),
        toeplitz(before, 2 * HALO),
        jnp.where(
            (row >= HALO) & (lane >= HALO) & (lane < 2 * HALO), toeplitz(after, 2 * HALO), 0.0
        ),
    )
    edge_ref[0], edge_ref[1] = two_parts(edge[:, : 2 * HALO])
    own_copy.wait()


def dot_parts(left, across_ref):
    main, rest = two_parts(left)
    return dot32(main, across_ref[0]) + (dot32(main, across_ref[1]) + dot32(rest, across_ref[0]))


def centre_kernel(main_ref, rest_ref, across_ref, centre_ref, out_ref):
    main = main_ref[...]
    along = dot32(centre_ref[0], main) + (
        dot32(centre_ref[0], rest_ref[...]) + dot32(centre_ref[1], main)
    )
    out_ref[...] = dot_parts(along, across_ref)


def edge_kernel(inner_ref, low_ref, high_ref, across_ref, edge_ref, out_ref):
    halo = jnp.concatenate([low_ref[...], high_ref[...]], axis=0)
    along = dot32(edge_ref[0], halo) + dot32(edge_ref[1], halo)
    extra = dot_parts(along, across_ref)
    out_ref[pl.ds(0, HALO)] = inner_ref[pl.ds(0, HALO)] + extra[:HALO]
    out_ref[pl.ds(HALO, SIDE - 2 * HALO)] = inner_ref[pl.ds(HALO, SIDE - 2 * HALO)]
    out_ref[pl.ds(SIDE - HALO, HALO)] = inner_ref[pl.ds(SIDE - HALO, HALO)] + extra[HALO:]


def per_device(
    split,
    raw_pixels,
    flat_field,
    bias_rows,
    psf_taps,
    term_weights,
    warp_shift,
    warp_scale,
    owner_of,
    patch_slot,
    weight_index,
    weight_table,
    detect_taps,
):
    nz, pn, ns = split
    devices = nz * pn * ns
    group = ns * pn
    visits, _, rows, cols = raw_pixels.shape
    blocks = owner_of.shape[0]
    per_dest = nz * CAP
    payload = per_dest * (SIDE + FIELDS)
    width = PATCH_DEV * SIDE
    smem = pl.BlockSpec(memory_space=pltpu.SMEM)
    vmem = pl.BlockSpec(memory_space=pltpu.VMEM)
    hbm = pl.BlockSpec(memory_space=pltpu.HBM)
    params = pltpu.CompilerParams(vmem_limit_bytes=VMEM_LIMIT)

    def shaped(shape, dtype):
        return jax.ShapeDtypeStruct(shape, dtype)

    weights = term_weights.transpose(1, 2, 0)
    send = pl.pallas_call(
        functools.partial(warp_kernel, split),
        out_shape=[shaped((payload, SIDE), jnp.bfloat16)] * group,
        in_specs=[hbm] * 11,
        out_specs=[hbm] * group,
        scratch_shapes=[
            pltpu.SMEM((blocks,), jnp.int32),
            pltpu.SMEM((blocks,), jnp.int32),
            pltpu.SMEM((blocks,), jnp.int32),
            pltpu.SMEM(weight_table.shape, jnp.float32),
            pltpu.SMEM(psf_taps.shape, jnp.float32),
            pltpu.SMEM(weights.shape, jnp.float32),
            pltpu.SMEM(warp_shift.shape, jnp.float32),
            pltpu.SMEM(warp_scale.shape, jnp.float32),
            pltpu.VMEM(bias_rows.shape, jnp.float32),
            pltpu.VMEM(raw_pixels.shape, jnp.float32),
            pltpu.VMEM(flat_field.shape, jnp.float32),
            pltpu.SMEM((devices,), jnp.int32),
            pltpu.VMEM((rows, cols), jnp.bfloat16),
            pltpu.VMEM((rows, cols), jnp.bfloat16),
            pltpu.VMEM((rows, cols), jnp.bfloat16),
            pltpu.VMEM((group * per_dest, SIDE), jnp.float32),
            pltpu.VMEM((group * per_dest, SIDE), jnp.float32),
            pltpu.SemaphoreType.DMA((9,)),
            pltpu.SemaphoreType.DMA,
            pltpu.SemaphoreType.DMA((visits,)),
            pltpu.VMEM((group, payload, SIDE), jnp.bfloat16),
            pltpu.SemaphoreType.DMA((group,)),
        ],
        compiler_params=pltpu.CompilerParams(vmem_limit_bytes=60 * 1024 * 1024),
        name="warp",
    )(
        owner_of.reshape(blocks),
        patch_slot.reshape(blocks),
        weight_index.reshape(blocks),
        weight_table,
        psf_taps,
        weights,
        warp_shift,
        warp_scale,
        bias_rows,
        raw_pixels,
        flat_field,
    )
    peers = [pn] + sorted((k for k in range(1, group) if k != pn), key=lambda k: ORDER.get(k, k))
    arrived = [
        lax.ppermute(send[k], ("sec", "p"), [(g, g ^ k) for g in range(group)]) for k in peers
    ]

    across, centre, edge, own = pl.pallas_call(
        prepare_kernel,
        out_shape=(
            shaped((2, width, width), jnp.bfloat16),
            shaped((2, SIDE, SIDE), jnp.bfloat16),
            shaped((2, 2 * HALO, 2 * HALO), jnp.bfloat16),
            shaped((payload, SIDE), jnp.bfloat16),
        ),
        in_specs=[smem, hbm],
        out_specs=(vmem,) * 4,
        scratch_shapes=[pltpu.VMEM((width, width), jnp.float32), pltpu.SemaphoreType.DMA],
        compiler_params=params,
        cost_estimate=pl.CostEstimate(flops=0, bytes_accessed=8 << 20, transcendentals=0),
        name="matrices",
    )(detect_taps, send[0])

    plane_sums = pl.pallas_call(
        functools.partial(sum_kernel, nz, group),
        out_shape=[shaped((PATCH_DEV * (SIDE + FIELDS), SIDE), jnp.bfloat16)] * nz,
        in_specs=[vmem] * group,
        out_specs=[vmem] * nz,
        scratch_shapes=[pltpu.VMEM((group, PATCH_DEV, per_dest, SIDE), jnp.float32)],
        compiler_params=params,
        name="plane_sums",
    )(own, *arrived)
    gathered = [plane_sums[0]] + [
        lax.ppermute(plane_sums[d], "z", [(z, z ^ d) for z in range(nz)])
        for d in sorted(range(1, nz), key=lambda d: d == 1)
    ]

    coadd, main, rest, low_rows, high_rows = pl.pallas_call(
        functools.partial(coadd_kernel, nz),
        out_shape=(
            shaped((SIDE, width), jnp.float32),
            shaped((SIDE, width), jnp.bfloat16),
            shaped((SIDE, width), jnp.bfloat16),
            shaped((HALO, width), jnp.bfloat16),
            shaped((HALO, width), jnp.bfloat16),
        ),
        in_specs=[vmem] * nz,
        out_specs=(vmem,) * 5,
        compiler_params=params,
        name="coadd",
    )(*gathered)

    every = ("sec", "z", "p")
    low = lax.ppermute(low_rows, every, [(i, i + 1) for i in range(devices - 1)])
    high = lax.ppermute(high_rows, every, [(i + 1, i) for i in range(devices - 1)])

    inner = pl.pallas_call(
        centre_kernel,
        out_shape=shaped((SIDE, width), jnp.float32),
        in_specs=[vmem] * 4,
        out_specs=vmem,
        compiler_params=params,
        cost_estimate=pl.CostEstimate(
            flops=6 * SIDE * width * (SIDE + width), bytes_accessed=2 << 20, transcendentals=0
        ),
        name="detect_centre",
    )(main, rest, across, centre)
    detection = pl.pallas_call(
        edge_kernel,
        out_shape=shaped((SIDE, width), jnp.float32),
        in_specs=[vmem] * 5,
        out_specs=vmem,
        compiler_params=params,
        name="detect_edges",
    )(inner, low, high, across, edge)
    return coadd, detection


def solution(mesh):
    ns, nd = mesh.shape["sec"], mesh.shape["dev"]
    nz = math.gcd(nd, 4)
    pn = nd // nz
    cut = Mesh(mesh.devices.reshape(ns, nz, pn), ("sec", "z", "p"))
    every = ("sec", "z", "p")
    placed = (
        P(None, every, None, None),
        P(every, None, None),
        P(None, every, None),
        P(),
        P(None, every, None),
        P(None, every, None),
        P(None, every, None),
        P(every, None),
        P(every, None),
        P(every, None),
        P(),
        P(),
    )
    return jax.shard_map(
        functools.partial(per_device, (nz, pn, ns)),
        mesh=cut,
        in_specs=placed,
        out_specs=(P(every, None), P(every, None)),
        check_vma=False,
    )
```

```python
import functools
import math

import jax
import jax.numpy as jnp
from jax import lax
from jax.experimental import pallas as pl
from jax.experimental.pallas import tpu as pltpu
from jax.sharding import Mesh
from jax.sharding import PartitionSpec as P

SIDE = 128
CAP = 2
PATCH_DEV = 4
HALO = 32
FIELDS = 4
ORDER = {1: 0, 3: 1, 7: 2, 2: 3, 6: 4, 5: 5}
VMEM_LIMIT = 48 * 1024 * 1024


def tap_row(tap, count, start, width, reverse):
    lane = lax.broadcasted_iota(jnp.int32, (1, width), 1)
    row = jnp.zeros((1, width), jnp.float32)
    for k in range(count):
        at = start + (count - 1 - k if reverse else k)
        row = jnp.where(lane == at % width, tap(k), row)
    return row


def toeplitz(row, height):
    return pltpu.roll(
        jnp.broadcast_to(row, (height, row.shape[1])), 0, 1, stride=1, stride_axis=0
    )


def store_band(band_ref, tiles):
    blocks = band_ref.shape[0] // SIDE
    for i in range(blocks):
        for j in range(blocks):
            place = (pl.ds(i * SIDE, SIDE), pl.ds(j * SIDE, SIDE))
            if abs(i - j) <= 1:
                first = (j - i + 1) * SIDE
                band_ref[place] = tiles[:, first : first + SIDE]
            else:
                band_ref[place] = jnp.zeros((SIDE, SIDE), band_ref.dtype)


def dot32(left, right):
    return jnp.dot(left, right, preferred_element_type=jnp.float32)


def two_parts(value):
    high = value.astype(jnp.bfloat16)
    return high, (value - high.astype(jnp.float32)).astype(jnp.bfloat16)


def three_parts(value):
    high = value.astype(jnp.bfloat16)
    rest = value - high.astype(jnp.float32)
    mid = rest.astype(jnp.bfloat16)
    return high, mid, (rest - mid.astype(jnp.float32)).astype(jnp.bfloat16)


def warp_kernel(
    split,
    owner_hbm,
    patch_hbm,
    index_hbm,
    table_hbm,
    taps_hbm,
    weights_hbm,
    shift_hbm,
    scale_hbm,
    bias_hbm,
    raw_hbm,
    flat_hbm,
    *rest,
):
    nz, pn, ns = split
    outs, rest = rest[: ns * pn], rest[ns * pn :]
    warp_body(
        split,
        (
            owner_hbm,
            patch_hbm,
            index_hbm,
            table_hbm,
            taps_hbm,
            weights_hbm,
            shift_hbm,
            scale_hbm,
            bias_hbm,
            raw_hbm,
            flat_hbm,
        ),
        outs,
        *rest,
    )


def warp_body(
    split,
    inputs,
    outs,
    owner_ref,
    patch_ref,
    index_ref,
    table_ref,
    taps_ref,
    weights_ref,
    shift_ref,
    scale_ref,
    bias_ref,
    raw_ref,
    flat_ref,
    count_ref,
    band_ref,
    left_ref,
    mid_ref,
    slot_rows,
    weight_rows,
    small_sem,
    flat_sem,
    raw_sem,
    out_ref,
    out_sem,
):
    (
        owner_hbm,
        patch_hbm,
        index_hbm,
        table_hbm,
        taps_hbm,
        weights_hbm,
        shift_hbm,
        scale_hbm,
        bias_hbm,
        raw_hbm,
        flat_hbm,
    ) = inputs
    nz, pn, ns = split
    mine = lax.axis_index("sec") * pn + lax.axis_index("p")
    visits, _, rows, cols = raw_ref.shape
    terms, tap_count = taps_ref.shape[1], taps_ref.shape[3]
    half = tap_count // 2
    per_dest = nz * CAP
    data_rows = per_dest * SIDE

    small = [
        pltpu.make_async_copy(src, dst, small_sem.at[i])
        for i, (src, dst) in enumerate(
            (
                (taps_hbm, taps_ref),
                (bias_hbm, bias_ref),
                (owner_hbm, owner_ref),
                (patch_hbm, patch_ref),
                (index_hbm, index_ref),
                (table_hbm, table_ref),
                (weights_hbm, weights_ref),
                (shift_hbm, shift_ref),
                (scale_hbm, scale_ref),
            )
        )
    ]
    for copy in small:
        copy.start()
    flat_copy = pltpu.make_async_copy(flat_hbm, flat_ref, flat_sem)
    raw_copies = [
        pltpu.make_async_copy(raw_hbm.at[v], raw_ref.at[v], raw_sem.at[v]) for v in range(visits)
    ]
    raw_copies[0].start()
    flat_copy.start()
    for copy in raw_copies[1:]:
        copy.start()

    out_ref[...] = jnp.zeros_like(out_ref)
    slot_rows[...] = jnp.full(slot_rows.shape, -1.0, jnp.float32)
    weight_rows[...] = jnp.zeros_like(weight_rows)

    def clear(i, c):
        count_ref[i] = 0
        return c

    lax.fori_loop(0, count_ref.shape[0], clear, 0)
    for copy in small:
        copy.wait()

    def hat(length, axis, shift, scale):
        centre = (length - 1) / 2.0
        shape = (1, length) if axis == 1 else (length, 1)
        out_pos = lax.broadcasted_iota(jnp.int32, shape, axis).astype(jnp.float32)
        source = scale * (out_pos - centre) + centre + shift
        in_pos = lax.broadcasted_iota(jnp.int32, (length, length), 1 - axis).astype(jnp.float32)
        return jnp.maximum(0.0, 1.0 - jnp.abs(in_pos - source)).astype(jnp.bfloat16)

    for visit in range(visits):
        for term in range(terms):
            for axis, reverse in ((1, True), (0, False)):
                row = tap_row(
                    lambda k: taps_ref[visit, term, axis, k],
                    tap_count,
                    SIDE - half,
                    3 * SIDE,
                    reverse,
                )
                store_band(
                    band_ref.at[visit, 2 * term + 1 - axis], toeplitz(row, SIDE).astype(jnp.bfloat16)
                )
        band_ref[visit, 2 * terms] = hat(cols, 1, shift_ref[visit, 0, 1], scale_ref[visit, 0, 1])
        band_ref[visit, 2 * terms + 1] = hat(
            rows, 0, shift_ref[visit, 0, 0], scale_ref[visit, 0, 0]
        )

    def windows(length):
        wide = 2 * SIDE
        for at in range(0, length, wide):
            low, high = max(0, at - SIDE), min(length, at + wide + SIDE)
            yield pl.ds(at, min(wide, length - at)), pl.ds(low, high - low)

    def times_band(out, source, band):
        for o, k in windows(cols):
            out[:, o] = dot32(source[:, k], band[k, o]).astype(jnp.bfloat16)

    def band_times(out, band, source):
        for o, k in windows(rows):
            out[o, :] = dot32(band[o, k], source[k, :]).astype(jnp.bfloat16)

    row_blocks, col_blocks = rows // SIDE, cols // SIDE
    for visit in range(visits):
        left, mid = left_ref.at[visit], mid_ref.at[visit]
        bias = jnp.broadcast_to(bias_ref[visit], (SIDE, rows)).T
        raw_copies[visit].wait()
        if visit == 0:
            flat_copy.wait()
        for j in range(cols // SIDE):
            sl = pl.ds(j * SIDE, SIDE)
            left[:, sl] = ((raw_ref[visit, 0, :, sl] - bias) * flat_ref[0, :, sl]).astype(
                jnp.bfloat16
            )

        if terms == 1:
            times_band(mid, left, band_ref.at[visit, 0])
            for o, k in windows(rows):
                part = dot32(band_ref[visit, 1, o, k], mid[k, :])
                left[o, :] = (weights_ref[0, 0, visit] * part).astype(jnp.bfloat16)
        else:
            matched = None
            for term in range(terms):
                times_band(mid, left, band_ref.at[visit, 2 * term])
                part = weights_ref[0, term, visit] * dot32(band_ref[visit, 2 * term + 1], mid[...])
                matched = part if matched is None else matched + part
            left[...] = matched.astype(jnp.bfloat16)
        times_band(mid, left, band_ref.at[visit, 2 * terms])
        band_times(left, band_ref.at[visit, 2 * terms + 1], mid)

    for visit in range(visits):
        for i in range(row_blocks):
            for j in range(col_blocks):
                block = visit * (row_blocks * col_blocks) + i * col_blocks + j
                owner = owner_ref[block]
                rank = count_ref[owner]
                count_ref[owner] = rank + 1
                sec = owner // (nz * pn)
                dev = owner - sec * (nz * pn)
                z = dev // pn
                dest = (sec * pn + dev - z * pn) ^ mine
                at = (z ^ lax.axis_index("z")) * CAP + rank
                out_ref[dest, pl.ds(pl.multiple_of(at * SIDE, SIDE), SIDE), :] = left_ref[
                    visit, pl.ds(i * SIDE, SIDE), pl.ds(j * SIDE, SIDE)
                ]
                line = pl.ds(dest * per_dest + at, 1)
                slot_rows[line, :] = jnp.full((1, SIDE), patch_ref[block].astype(jnp.float32))
                weight_rows[line, :] = jnp.full((1, SIDE), table_ref[index_ref[block]])

    def out_copy(dest):
        return pltpu.make_async_copy(out_ref.at[dest], outs[dest], out_sem.at[dest])

    for dest in range(out_ref.shape[0]):
        part = pl.ds(dest * per_dest, per_dest)
        fields = jnp.concatenate(
            [slot_rows[part, :]]
            + [w.astype(jnp.float32) for w in three_parts(weight_rows[part, :])],
            axis=0,
        )
        out_ref[dest, pl.ds(data_rows, fields.shape[0]), :] = fields.astype(jnp.bfloat16)
        out_copy(dest).start()
    for dest in range(out_ref.shape[0]):
        out_copy(dest).wait()


def sum_kernel(nz, sources, *refs):
    ins, outs, weight_ref = refs[:sources], refs[sources:-1], refs[-1]
    per_dest = nz * CAP
    data_rows = per_dest * SIDE
    for g in range(sources):
        fields = ins[g][pl.ds(data_rows, FIELDS * per_dest), :].astype(jnp.float32)
        slot = fields[:per_dest]
        weight = (
            fields[per_dest : 2 * per_dest]
            + fields[2 * per_dest : 3 * per_dest]
            + fields[3 * per_dest :]
        )
        for j in range(PATCH_DEV):
            weight_ref[g, j] = jnp.where(slot == float(j), weight, 0.0)
    step = 32
    for z in range(nz):
        for c in range(SIDE // step):
            sums = [jnp.zeros((step, SIDE), jnp.float32) for _ in range(PATCH_DEV)]
            for g in range(sources):
                for r in range(CAP):
                    at = z * CAP + r
                    value = ins[g][pl.ds(at * SIDE + c * step, step), :].astype(jnp.float32)
                    for j in range(PATCH_DEV):
                        sums[j] = sums[j] + weight_ref[g, j, pl.ds(at, 1), :] * value
            for j in range(PATCH_DEV):
                outs[z][pl.ds(j * SIDE + c * step, step), :] = sums[j].astype(jnp.bfloat16)
        totals = []
        for j in range(PATCH_DEV):
            total = jnp.zeros((1, SIDE), jnp.float32)
            for g in range(sources):
                for r in range(CAP):
                    total = total + weight_ref[g, j, pl.ds(z * CAP + r, 1), :]
            totals.append(total)
        parts = three_parts(jnp.concatenate(totals, axis=0))
        extra = jnp.concatenate(
            [q.astype(jnp.float32) for q in parts] + [jnp.zeros((PATCH_DEV, SIDE), jnp.float32)],
            axis=0,
        )
        outs[z][pl.ds(PATCH_DEV * SIDE, FIELDS * PATCH_DEV), :] = extra.astype(jnp.bfloat16)


def coadd_kernel(sources, *refs):
    ins, (coadd_ref, main_ref, rest_ref, first_ref, second_ref) = refs[:sources], refs[sources:]
    odd = lax.axis_index("p") % 2
    total = jnp.zeros((PATCH_DEV, SIDE), jnp.float32)
    for z in range(sources):
        extra = ins[z][pl.ds(PATCH_DEV * SIDE, FIELDS * PATCH_DEV), :].astype(jnp.float32)
        total = total + (
            extra[:PATCH_DEV] + extra[PATCH_DEV : 2 * PATCH_DEV] + extra[2 * PATCH_DEV : 3 * PATCH_DEV]
        )
    total = jnp.maximum(total, 1.0)
    for j in range(PATCH_DEV):
        numerator = ins[0][pl.ds(j * SIDE, SIDE), :].astype(jnp.float32)
        for z in range(1, sources):
            numerator = numerator + ins[z][pl.ds(j * SIDE, SIDE), :].astype(jnp.float32)
        tile = numerator / total[j : j + 1]
        sl = pl.ds(j * SIDE, SIDE)
        coadd_ref[:, sl] = tile
        main, rest = two_parts(tile)
        main_ref[:, sl] = main
        rest_ref[:, sl] = rest

    @pl.when(odd == 0)
    def _():
        first_ref[...] = main_ref[pl.ds(SIDE - HALO, HALO)]
        second_ref[...] = main_ref[pl.ds(0, HALO)]

    @pl.when(odd == 1)
    def _():
        first_ref[...] = main_ref[pl.ds(0, HALO)]
        second_ref[...] = main_ref[pl.ds(SIDE - HALO, HALO)]


def prepare_kernel(taps_ref, own_hbm, across_ref, centre_ref, edge_ref, own_ref, band_ref, own_sem):
    own_copy = pltpu.make_async_copy(own_hbm, own_ref, own_sem)
    own_copy.start()
    tap_count = taps_ref.shape[1]
    half = tap_count // 2
    across = tap_row(lambda k: taps_ref[1, k], tap_count, SIDE - half, 3 * SIDE, True)
    store_band(band_ref, toeplitz(across, SIDE))
    across_ref[0], across_ref[1] = two_parts(band_ref[...])
    down = tap_row(lambda k: taps_ref[0, k], tap_count, SIDE - half, 3 * SIDE, False)
    centre_ref[0], centre_ref[1] = two_parts(toeplitz(down, SIDE)[:, SIDE : 2 * SIDE])
    lane = lax.broadcasted_iota(jnp.int32, (2 * HALO, SIDE), 1)
    row = lax.broadcasted_iota(jnp.int32, (2 * HALO, SIDE), 0)
    before = tap_row(lambda k: taps_ref[0, k], tap_count, HALO - half, SIDE, False)
    after = tap_row(lambda k: taps_ref[0, k], tap_count, SIDE - HALO - half, SIDE, False)
    edge = jnp.where(
        (row < HALO) & (lane < HALO),
        toeplitz(before, 2 * HALO),
        jnp.where(
            (row >= HALO) & (lane >= HALO) & (lane < 2 * HALO), toeplitz(after, 2 * HALO), 0.0
        ),
    )
    edge_ref[0], edge_ref[1] = two_parts(edge[:, : 2 * HALO])
    own_copy.wait()


def dot_parts(left, across_ref):
    main, rest = two_parts(left)
    both = dot32(jnp.concatenate([main, rest], axis=0), across_ref[0])
    return both[: left.shape[0]] + (dot32(main, across_ref[1]) + both[left.shape[0] :])


def centre_kernel(main_ref, rest_ref, across_ref, centre_ref, out_ref):
    main = main_ref[...]
    along = dot32(centre_ref[0], main) + (
        dot32(centre_ref[0], rest_ref[...]) + dot32(centre_ref[1], main)
    )
    out_ref[...] = dot_parts(along, across_ref)


def edge_kernel(inner_ref, first_ref, second_ref, across_ref, edge_ref, out_ref, halo_ref):
    odd = lax.axis_index("p") % 2
    halo_ref[pl.ds(pl.multiple_of((1 - odd) * HALO, HALO), HALO)] = first_ref[...]
    halo_ref[pl.ds(pl.multiple_of(odd * HALO, HALO), HALO)] = second_ref[...]
    halo = halo_ref[...]
    along = dot32(edge_ref[0], halo) + dot32(edge_ref[1], halo)
    extra = dot_parts(along, across_ref)
    out_ref[pl.ds(0, HALO)] = inner_ref[pl.ds(0, HALO)] + extra[:HALO]
    out_ref[pl.ds(HALO, SIDE - 2 * HALO)] = inner_ref[pl.ds(HALO, SIDE - 2 * HALO)]
    out_ref[pl.ds(SIDE - HALO, HALO)] = inner_ref[pl.ds(SIDE - HALO, HALO)] + extra[HALO:]


def per_device(
    split,
    raw_pixels,
    flat_field,
    bias_rows,
    psf_taps,
    term_weights,
    warp_shift,
    warp_scale,
    owner_of,
    patch_slot,
    weight_index,
    weight_table,
    detect_taps,
):
    nz, pn, ns = split
    devices = nz * pn * ns
    group = ns * pn
    visits, _, rows, cols = raw_pixels.shape
    blocks = owner_of.shape[0]
    terms = psf_taps.shape[1]
    per_dest = nz * CAP
    payload = per_dest * (SIDE + FIELDS)
    width = PATCH_DEV * SIDE
    smem = pl.BlockSpec(memory_space=pltpu.SMEM)
    vmem = pl.BlockSpec(memory_space=pltpu.VMEM)
    hbm = pl.BlockSpec(memory_space=pltpu.HBM)
    params = pltpu.CompilerParams(vmem_limit_bytes=VMEM_LIMIT)

    def shaped(shape, dtype):
        return jax.ShapeDtypeStruct(shape, dtype)

    weights = term_weights.transpose(1, 2, 0)
    send = pl.pallas_call(
        functools.partial(warp_kernel, split),
        out_shape=[shaped((payload, SIDE), jnp.bfloat16)] * group,
        in_specs=[hbm] * 11,
        out_specs=[hbm] * group,
        scratch_shapes=[
            pltpu.SMEM((blocks,), jnp.int32),
            pltpu.SMEM((blocks,), jnp.int32),
            pltpu.SMEM((blocks,), jnp.int32),
            pltpu.SMEM(weight_table.shape, jnp.float32),
            pltpu.SMEM(psf_taps.shape, jnp.float32),
            pltpu.SMEM(weights.shape, jnp.float32),
            pltpu.SMEM(warp_shift.shape, jnp.float32),
            pltpu.SMEM(warp_scale.shape, jnp.float32),
            pltpu.VMEM(bias_rows.shape, jnp.float32),
            pltpu.VMEM(raw_pixels.shape, jnp.float32),
            pltpu.VMEM(flat_field.shape, jnp.float32),
            pltpu.SMEM((devices,), jnp.int32),
            pltpu.VMEM((visits, 2 * terms + 2, rows, cols), jnp.bfloat16),
            pltpu.VMEM((visits, rows, cols), jnp.bfloat16),
            pltpu.VMEM((visits, rows, cols), jnp.bfloat16),
            pltpu.VMEM((group * per_dest, SIDE), jnp.float32),
            pltpu.VMEM((group * per_dest, SIDE), jnp.float32),
            pltpu.SemaphoreType.DMA((9,)),
            pltpu.SemaphoreType.DMA,
            pltpu.SemaphoreType.DMA((visits,)),
            pltpu.VMEM((group, payload, SIDE), jnp.bfloat16),
            pltpu.SemaphoreType.DMA((group,)),
        ],
        compiler_params=pltpu.CompilerParams(vmem_limit_bytes=60 * 1024 * 1024),
        name="warp",
    )(
        owner_of.reshape(blocks),
        patch_slot.reshape(blocks),
        weight_index.reshape(blocks),
        weight_table,
        psf_taps,
        weights,
        warp_shift,
        warp_scale,
        bias_rows,
        raw_pixels,
        flat_field,
    )
    peers = [pn] + sorted((k for k in range(1, group) if k != pn), key=lambda k: ORDER.get(k, k))
    arrived = [
        lax.ppermute(send[k], ("sec", "p"), [(g, g ^ k) for g in range(group)]) for k in peers
    ]

    across, centre, edge, own = pl.pallas_call(
        prepare_kernel,
        out_shape=(
            shaped((2, width, width), jnp.bfloat16),
            shaped((2, SIDE, SIDE), jnp.bfloat16),
            shaped((2, 2 * HALO, 2 * HALO), jnp.bfloat16),
            shaped((payload, SIDE), jnp.bfloat16),
        ),
        in_specs=[smem, hbm],
        out_specs=(vmem,) * 4,
        scratch_shapes=[pltpu.VMEM((width, width), jnp.float32), pltpu.SemaphoreType.DMA],
        compiler_params=params,
        cost_estimate=pl.CostEstimate(flops=0, bytes_accessed=8 << 20, transcendentals=0),
        name="matrices",
    )(detect_taps, send[0])

    plane_sums = pl.pallas_call(
        functools.partial(sum_kernel, nz, group),
        out_shape=[shaped((PATCH_DEV * (SIDE + FIELDS), SIDE), jnp.bfloat16)] * nz,
        in_specs=[vmem] * group,
        out_specs=[vmem] * nz,
        scratch_shapes=[pltpu.VMEM((group, PATCH_DEV, per_dest, SIDE), jnp.float32)],
        compiler_params=params,
        name="plane_sums",
    )(own, *arrived)
    gathered = [plane_sums[0]] + [
        lax.ppermute(plane_sums[d], "z", [(z, z ^ d) for z in range(nz)])
        for d in sorted(range(1, nz), key=lambda d: d == 1)
    ]

    coadd, main, rest, first_rows, second_rows = pl.pallas_call(
        functools.partial(coadd_kernel, nz),
        out_shape=(
            shaped((SIDE, width), jnp.float32),
            shaped((SIDE, width), jnp.bfloat16),
            shaped((SIDE, width), jnp.bfloat16),
            shaped((HALO, width), jnp.bfloat16),
            shaped((HALO, width), jnp.bfloat16),
        ),
        in_specs=[vmem] * nz,
        out_specs=(vmem,) * 5,
        compiler_params=params,
        name="coadd",
    )(*gathered)

    every = ("sec", "z", "p")

    def swap(rows, start):
        pairs = [(i, i + 1) for i in range(start, devices - 1, 2)]
        return lax.ppermute(rows, every, pairs + [(j, i) for i, j in pairs])

    first, second = swap(first_rows, 0), swap(second_rows, 1)

    inner = pl.pallas_call(
        centre_kernel,
        out_shape=shaped((SIDE, width), jnp.float32),
        in_specs=[vmem] * 4,
        out_specs=vmem,
        compiler_params=params,
        cost_estimate=pl.CostEstimate(
            flops=6 * SIDE * width * (SIDE + width), bytes_accessed=2 << 20, transcendentals=0
        ),
        name="detect_centre",
    )(main, rest, across, centre)
    detection = pl.pallas_call(
        edge_kernel,
        out_shape=shaped((SIDE, width), jnp.float32),
        in_specs=[vmem] * 5,
        out_specs=vmem,
        scratch_shapes=[pltpu.VMEM((2 * HALO, width), jnp.bfloat16)],
        compiler_params=params,
        name="detect_edges",
    )(inner, first, second, across, edge)
    return coadd, detection


def solution(mesh):
    ns, nd = mesh.shape["sec"], mesh.shape["dev"]
    nz = math.gcd(nd, 4)
    pn = nd // nz
    cut = Mesh(mesh.devices.reshape(ns, nz, pn), ("sec", "z", "p"))
    every = ("sec", "z", "p")
    placed = (
        P(None, every, None, None),
        P(every, None, None),
        P(None, every, None),
        P(),
        P(None, every, None),
        P(None, every, None),
        P(None, every, None),
        P(every, None),
        P(every, None),
        P(every, None),
        P(),
        P(),
    )
    return jax.shard_map(
        functools.partial(per_device, (nz, pn, ns)),
        mesh=cut,
        in_specs=placed,
        out_specs=(P(every, None), P(every, None)),
        check_vma=False,
    )
```

```python
import functools
import math

import jax
import jax.numpy as jnp
from jax import lax
from jax.experimental import pallas as pl
from jax.experimental.pallas import tpu as pltpu
from jax.sharding import Mesh
from jax.sharding import PartitionSpec as P

SIDE = 128
CAP = 2
PATCH_DEV = 4
HALO = 32
FIELDS = 4
VMEM_LIMIT = 48 * 1024 * 1024


def turned(q, pn):
    bits = (pn.bit_length() - 1) // 2
    return ((q >> bits) | (q << bits)) & (pn - 1) if bits else q


def shifted(d, nz):
    return 0 if d == 0 else d % (nz - 1) + 1


def tap_row(tap, count, start, width, reverse):
    lane = lax.broadcasted_iota(jnp.int32, (1, width), 1)
    row = jnp.zeros((1, width), jnp.float32)
    for k in range(count):
        at = start + (count - 1 - k if reverse else k)
        row = jnp.where(lane == at % width, tap(k), row)
    return row


def toeplitz(row, height):
    return pltpu.roll(
        jnp.broadcast_to(row, (height, row.shape[1])), 0, 1, stride=1, stride_axis=0
    )


def store_band(band_ref, tiles):
    blocks = band_ref.shape[0] // SIDE
    for i in range(blocks):
        for j in range(blocks):
            place = (pl.ds(i * SIDE, SIDE), pl.ds(j * SIDE, SIDE))
            if abs(i - j) <= 1:
                first = (j - i + 1) * SIDE
                band_ref[place] = tiles[:, first : first + SIDE]
            else:
                band_ref[place] = jnp.zeros((SIDE, SIDE), band_ref.dtype)


def dot32(left, right):
    return jnp.dot(left, right, preferred_element_type=jnp.float32)


def two_parts(value):
    high = value.astype(jnp.bfloat16)
    return high, (value - high.astype(jnp.float32)).astype(jnp.bfloat16)


def three_parts(value):
    high = value.astype(jnp.bfloat16)
    rest = value - high.astype(jnp.float32)
    mid = rest.astype(jnp.bfloat16)
    return high, mid, (rest - mid.astype(jnp.float32)).astype(jnp.bfloat16)


def warp_kernel(
    split,
    owner_hbm,
    patch_hbm,
    index_hbm,
    table_hbm,
    taps_hbm,
    weights_hbm,
    shift_hbm,
    scale_hbm,
    bias_hbm,
    raw_hbm,
    flat_hbm,
    *rest,
):
    nz, pn, ns = split
    outs, rest = rest[: ns * pn], rest[ns * pn :]
    warp_body(
        split,
        (
            owner_hbm,
            patch_hbm,
            index_hbm,
            table_hbm,
            taps_hbm,
            weights_hbm,
            shift_hbm,
            scale_hbm,
            bias_hbm,
            raw_hbm,
            flat_hbm,
        ),
        outs,
        *rest,
    )


def warp_body(
    split,
    inputs,
    outs,
    owner_ref,
    patch_ref,
    index_ref,
    table_ref,
    taps_ref,
    weights_ref,
    shift_ref,
    scale_ref,
    bias_ref,
    raw_ref,
    flat_ref,
    count_ref,
    band_ref,
    left_ref,
    mid_ref,
    slot_rows,
    weight_rows,
    small_sem,
    flat_sem,
    raw_sem,
    out_ref,
    out_sem,
):
    (
        owner_hbm,
        patch_hbm,
        index_hbm,
        table_hbm,
        taps_hbm,
        weights_hbm,
        shift_hbm,
        scale_hbm,
        bias_hbm,
        raw_hbm,
        flat_hbm,
    ) = inputs
    nz, pn, ns = split
    my_sec, my_p, my_z = lax.axis_index("sec"), lax.axis_index("p"), lax.axis_index("z")
    visits, _, rows, cols = raw_ref.shape
    terms, tap_count = taps_ref.shape[1], taps_ref.shape[3]
    half = tap_count // 2
    per_dest = nz * CAP
    data_rows = per_dest * SIDE

    small = [
        pltpu.make_async_copy(src, dst, small_sem.at[i])
        for i, (src, dst) in enumerate(
            (
                (taps_hbm, taps_ref),
                (bias_hbm, bias_ref),
                (owner_hbm, owner_ref),
                (patch_hbm, patch_ref),
                (index_hbm, index_ref),
                (table_hbm, table_ref),
                (weights_hbm, weights_ref),
                (shift_hbm, shift_ref),
                (scale_hbm, scale_ref),
            )
        )
    ]
    for copy in small:
        copy.start()
    flat_copy = pltpu.make_async_copy(flat_hbm, flat_ref, flat_sem)
    raw_copies = [
        pltpu.make_async_copy(raw_hbm.at[v], raw_ref.at[v], raw_sem.at[v]) for v in range(visits)
    ]
    raw_copies[0].start()
    flat_copy.start()
    for copy in raw_copies[1:]:
        copy.start()

    out_ref[...] = jnp.zeros_like(out_ref)
    slot_rows[...] = jnp.full(slot_rows.shape, -1.0, jnp.float32)
    weight_rows[...] = jnp.zeros_like(weight_rows)

    def clear(i, c):
        count_ref[i] = 0
        return c

    lax.fori_loop(0, count_ref.shape[0], clear, 0)
    for copy in small:
        copy.wait()

    def hat(length, axis, shift, scale):
        centre = (length - 1) / 2.0
        shape = (1, length) if axis == 1 else (length, 1)
        out_pos = lax.broadcasted_iota(jnp.int32, shape, axis).astype(jnp.float32)
        source = scale * (out_pos - centre) + centre + shift
        in_pos = lax.broadcasted_iota(jnp.int32, (length, length), 1 - axis).astype(jnp.float32)
        return jnp.maximum(0.0, 1.0 - jnp.abs(in_pos - source)).astype(jnp.bfloat16)

    for visit in range(visits):
        for term in range(terms):
            for axis, reverse in ((1, True), (0, False)):
                row = tap_row(
                    lambda k: taps_ref[visit, term, axis, k],
                    tap_count,
                    SIDE - half,
                    3 * SIDE,
                    reverse,
                )
                store_band(
                    band_ref.at[visit, 2 * term + 1 - axis], toeplitz(row, SIDE).astype(jnp.bfloat16)
                )
        band_ref[visit, 2 * terms] = hat(cols, 1, shift_ref[visit, 0, 1], scale_ref[visit, 0, 1])
        band_ref[visit, 2 * terms + 1] = hat(
            rows, 0, shift_ref[visit, 0, 0], scale_ref[visit, 0, 0]
        )

    def windows(length):
        wide = 2 * SIDE
        for at in range(0, length, wide):
            low, high = max(0, at - SIDE), min(length, at + wide + SIDE)
            yield pl.ds(at, min(wide, length - at)), pl.ds(low, high - low)

    def times_band(out, source, band):
        for o, k in windows(cols):
            out[:, o] = dot32(source[:, k], band[k, o]).astype(jnp.bfloat16)

    def band_times(out, band, source):
        for o, k in windows(rows):
            out[o, :] = dot32(band[o, k], source[k, :]).astype(jnp.bfloat16)

    row_blocks, col_blocks = rows // SIDE, cols // SIDE
    for visit in range(visits):
        left, mid = left_ref.at[visit], mid_ref.at[visit]
        bias = jnp.broadcast_to(bias_ref[visit], (SIDE, rows)).T
        raw_copies[visit].wait()
        if visit == 0:
            flat_copy.wait()
        for j in range(cols // SIDE):
            sl = pl.ds(j * SIDE, SIDE)
            left[:, sl] = ((raw_ref[visit, 0, :, sl] - bias) * flat_ref[0, :, sl]).astype(
                jnp.bfloat16
            )

        if terms == 1:
            times_band(mid, left, band_ref.at[visit, 0])
            for o, k in windows(rows):
                part = dot32(band_ref[visit, 1, o, k], mid[k, :])
                left[o, :] = (weights_ref[0, 0, visit] * part).astype(jnp.bfloat16)
        else:
            matched = None
            for term in range(terms):
                times_band(mid, left, band_ref.at[visit, 2 * term])
                part = weights_ref[0, term, visit] * dot32(band_ref[visit, 2 * term + 1], mid[...])
                matched = part if matched is None else matched + part
            left[...] = matched.astype(jnp.bfloat16)
        times_band(mid, left, band_ref.at[visit, 2 * terms])
        band_times(left, band_ref.at[visit, 2 * terms + 1], mid)

    for visit in range(visits):
        for i in range(row_blocks):
            for j in range(col_blocks):
                block = visit * (row_blocks * col_blocks) + i * col_blocks + j
                owner = owner_ref[block]
                rank = count_ref[owner]
                count_ref[owner] = rank + 1
                sec = owner // (nz * pn)
                dev = owner - sec * (nz * pn)
                z = dev // pn
                step = (dev - z * pn) ^ my_p
                step = jnp.where(my_sec == 0, step, turned(step, pn))
                dest = (sec ^ my_sec) * pn + step
                apart = z ^ my_z
                later = jnp.where(apart > 1, apart - 1, apart * (nz - 1))
                at = jnp.where(sec == 0, apart, later) * CAP + rank
                out_ref[dest, pl.ds(pl.multiple_of(at * SIDE, SIDE), SIDE), :] = left_ref[
                    visit, pl.ds(i * SIDE, SIDE), pl.ds(j * SIDE, SIDE)
                ]
                line = pl.ds(dest * per_dest + at, 1)
                slot_rows[line, :] = jnp.full((1, SIDE), patch_ref[block].astype(jnp.float32))
                weight_rows[line, :] = jnp.full((1, SIDE), table_ref[index_ref[block]])

    def out_copy(dest):
        return pltpu.make_async_copy(out_ref.at[dest], outs[dest], out_sem.at[dest])

    for dest in range(out_ref.shape[0]):
        part = pl.ds(dest * per_dest, per_dest)
        fields = jnp.concatenate(
            [slot_rows[part, :]]
            + [w.astype(jnp.float32) for w in three_parts(weight_rows[part, :])],
            axis=0,
        )
        out_ref[dest, pl.ds(data_rows, fields.shape[0]), :] = fields.astype(jnp.bfloat16)
        out_copy(dest).start()
    for dest in range(out_ref.shape[0]):
        out_copy(dest).wait()


def sum_kernel(nz, sources, *refs):
    ins, outs, weight_ref = refs[:sources], refs[sources:-1], refs[-1]
    per_dest = nz * CAP
    data_rows = per_dest * SIDE
    for g in range(sources):
        fields = ins[g][pl.ds(data_rows, FIELDS * per_dest), :].astype(jnp.float32)
        slot = fields[:per_dest]
        weight = (
            fields[per_dest : 2 * per_dest]
            + fields[2 * per_dest : 3 * per_dest]
            + fields[3 * per_dest :]
        )
        for j in range(PATCH_DEV):
            weight_ref[g, j] = jnp.where(slot == float(j), weight, 0.0)
    step = 32
    for z in range(nz):
        for c in range(SIDE // step):
            sums = [jnp.zeros((step, SIDE), jnp.float32) for _ in range(PATCH_DEV)]
            for g in range(sources):
                for r in range(CAP):
                    at = z * CAP + r
                    value = ins[g][pl.ds(at * SIDE + c * step, step), :].astype(jnp.float32)
                    for j in range(PATCH_DEV):
                        sums[j] = sums[j] + weight_ref[g, j, pl.ds(at, 1), :] * value
            for j in range(PATCH_DEV):
                outs[z][pl.ds(j * SIDE + c * step, step), :] = sums[j].astype(jnp.bfloat16)
        totals = []
        for j in range(PATCH_DEV):
            total = jnp.zeros((1, SIDE), jnp.float32)
            for g in range(sources):
                for r in range(CAP):
                    total = total + weight_ref[g, j, pl.ds(z * CAP + r, 1), :]
            totals.append(total)
        parts = three_parts(jnp.concatenate(totals, axis=0))
        extra = jnp.concatenate(
            [q.astype(jnp.float32) for q in parts] + [jnp.zeros((PATCH_DEV, SIDE), jnp.float32)],
            axis=0,
        )
        outs[z][pl.ds(PATCH_DEV * SIDE, FIELDS * PATCH_DEV), :] = extra.astype(jnp.bfloat16)


def coadd_kernel(sources, *refs):
    ins, (coadd_ref, main_ref, rest_ref, first_ref, second_ref) = refs[:sources], refs[sources:]
    odd = lax.axis_index("p") % 2
    total = jnp.zeros((PATCH_DEV, SIDE), jnp.float32)
    for z in range(sources):
        extra = ins[z][pl.ds(PATCH_DEV * SIDE, FIELDS * PATCH_DEV), :].astype(jnp.float32)
        total = total + (
            extra[:PATCH_DEV] + extra[PATCH_DEV : 2 * PATCH_DEV] + extra[2 * PATCH_DEV : 3 * PATCH_DEV]
        )
    total = jnp.maximum(total, 1.0)
    for j in range(PATCH_DEV):
        numerator = ins[0][pl.ds(j * SIDE, SIDE), :].astype(jnp.float32)
        for z in range(1, sources):
            numerator = numerator + ins[z][pl.ds(j * SIDE, SIDE), :].astype(jnp.float32)
        tile = numerator / total[j : j + 1]
        sl = pl.ds(j * SIDE, SIDE)
        coadd_ref[:, sl] = tile
        main, rest = two_parts(tile)
        main_ref[:, sl] = main
        rest_ref[:, sl] = rest

    @pl.when(odd == 0)
    def _():
        first_ref[...] = main_ref[pl.ds(SIDE - HALO, HALO)]
        second_ref[...] = main_ref[pl.ds(0, HALO)]

    @pl.when(odd == 1)
    def _():
        first_ref[...] = main_ref[pl.ds(0, HALO)]
        second_ref[...] = main_ref[pl.ds(SIDE - HALO, HALO)]


def prepare_kernel(taps_ref, own_hbm, across_ref, centre_ref, edge_ref, own_ref, band_ref, own_sem):
    own_copy = pltpu.make_async_copy(own_hbm, own_ref, own_sem)
    own_copy.start()
    tap_count = taps_ref.shape[1]
    half = tap_count // 2
    across = tap_row(lambda k: taps_ref[1, k], tap_count, SIDE - half, 3 * SIDE, True)
    store_band(band_ref, toeplitz(across, SIDE))
    across_ref[0], across_ref[1] = two_parts(band_ref[...])
    down = tap_row(lambda k: taps_ref[0, k], tap_count, SIDE - half, 3 * SIDE, False)
    centre_ref[0], centre_ref[1] = two_parts(toeplitz(down, SIDE)[:, SIDE : 2 * SIDE])
    lane = lax.broadcasted_iota(jnp.int32, (2 * HALO, SIDE), 1)
    row = lax.broadcasted_iota(jnp.int32, (2 * HALO, SIDE), 0)
    before = tap_row(lambda k: taps_ref[0, k], tap_count, HALO - half, SIDE, False)
    after = tap_row(lambda k: taps_ref[0, k], tap_count, SIDE - HALO - half, SIDE, False)
    edge = jnp.where(
        (row < HALO) & (lane < HALO),
        toeplitz(before, 2 * HALO),
        jnp.where(
            (row >= HALO) & (lane >= HALO) & (lane < 2 * HALO), toeplitz(after, 2 * HALO), 0.0
        ),
    )
    edge_ref[0], edge_ref[1] = two_parts(edge[:, : 2 * HALO])
    own_copy.wait()


def dot_parts(left, across_ref):
    main, rest = two_parts(left)
    both = dot32(jnp.concatenate([main, rest], axis=0), across_ref[0])
    return both[: left.shape[0]] + (dot32(main, across_ref[1]) + both[left.shape[0] :])


def centre_kernel(main_ref, rest_ref, across_ref, centre_ref, out_ref):
    main = main_ref[...]
    along = dot32(centre_ref[0], main) + (
        dot32(centre_ref[0], rest_ref[...]) + dot32(centre_ref[1], main)
    )
    out_ref[...] = dot_parts(along, across_ref)


def edge_kernel(inner_ref, first_ref, second_ref, across_ref, edge_ref, out_ref, halo_ref):
    odd = lax.axis_index("p") % 2
    halo_ref[pl.ds(pl.multiple_of((1 - odd) * HALO, HALO), HALO)] = first_ref[...]
    halo_ref[pl.ds(pl.multiple_of(odd * HALO, HALO), HALO)] = second_ref[...]
    halo = halo_ref[...]
    along = dot32(edge_ref[0], halo) + dot32(edge_ref[1], halo)
    extra = dot_parts(along, across_ref)
    out_ref[pl.ds(0, HALO)] = inner_ref[pl.ds(0, HALO)] + extra[:HALO]
    out_ref[pl.ds(HALO, SIDE - 2 * HALO)] = inner_ref[pl.ds(HALO, SIDE - 2 * HALO)]
    out_ref[pl.ds(SIDE - HALO, HALO)] = inner_ref[pl.ds(SIDE - HALO, HALO)] + extra[HALO:]


def per_device(
    split,
    raw_pixels,
    flat_field,
    bias_rows,
    psf_taps,
    term_weights,
    warp_shift,
    warp_scale,
    owner_of,
    patch_slot,
    weight_index,
    weight_table,
    detect_taps,
):
    nz, pn, ns = split
    devices = nz * pn * ns
    group = ns * pn
    visits, _, rows, cols = raw_pixels.shape
    blocks = owner_of.shape[0]
    terms = psf_taps.shape[1]
    per_dest = nz * CAP
    payload = per_dest * (SIDE + FIELDS)
    width = PATCH_DEV * SIDE
    smem = pl.BlockSpec(memory_space=pltpu.SMEM)
    vmem = pl.BlockSpec(memory_space=pltpu.VMEM)
    hbm = pl.BlockSpec(memory_space=pltpu.HBM)
    params = pltpu.CompilerParams(vmem_limit_bytes=VMEM_LIMIT)

    def shaped(shape, dtype):
        return jax.ShapeDtypeStruct(shape, dtype)

    weights = term_weights.transpose(1, 2, 0)
    send = pl.pallas_call(
        functools.partial(warp_kernel, split),
        out_shape=[shaped((payload, SIDE), jnp.bfloat16)] * group,
        in_specs=[hbm] * 11,
        out_specs=[hbm] * group,
        scratch_shapes=[
            pltpu.SMEM((blocks,), jnp.int32),
            pltpu.SMEM((blocks,), jnp.int32),
            pltpu.SMEM((blocks,), jnp.int32),
            pltpu.SMEM(weight_table.shape, jnp.float32),
            pltpu.SMEM(psf_taps.shape, jnp.float32),
            pltpu.SMEM(weights.shape, jnp.float32),
            pltpu.SMEM(warp_shift.shape, jnp.float32),
            pltpu.SMEM(warp_scale.shape, jnp.float32),
            pltpu.VMEM(bias_rows.shape, jnp.float32),
            pltpu.VMEM(raw_pixels.shape, jnp.float32),
            pltpu.VMEM(flat_field.shape, jnp.float32),
            pltpu.SMEM((devices,), jnp.int32),
            pltpu.VMEM((visits, 2 * terms + 2, rows, cols), jnp.bfloat16),
            pltpu.VMEM((visits, rows, cols), jnp.bfloat16),
            pltpu.VMEM((visits, rows, cols), jnp.bfloat16),
            pltpu.VMEM((group * per_dest, SIDE), jnp.float32),
            pltpu.VMEM((group * per_dest, SIDE), jnp.float32),
            pltpu.SemaphoreType.DMA((9,)),
            pltpu.SemaphoreType.DMA,
            pltpu.SemaphoreType.DMA((visits,)),
            pltpu.VMEM((group, payload, SIDE), jnp.bfloat16),
            pltpu.SemaphoreType.DMA((group,)),
        ],
        compiler_params=pltpu.CompilerParams(vmem_limit_bytes=60 * 1024 * 1024),
        name="warp",
    )(
        owner_of.reshape(blocks),
        patch_slot.reshape(blocks),
        weight_index.reshape(blocks),
        weight_table,
        psf_taps,
        weights,
        warp_shift,
        warp_scale,
        bias_rows,
        raw_pixels,
        flat_field,
    )
    def in_plane(part, k):
        pairs = []
        for sec in range(ns):
            for p in range(pn):
                q = k % pn if sec == 0 else turned(k % pn, pn)
                pairs.append((sec * pn + p, (sec ^ (k // pn)) * pn + (p ^ q)))
        return lax.ppermute(part, ("sec", "p"), pairs)

    def along_z(part, d):
        pairs = []
        for i in range(devices):
            apart = d if i < nz * pn else shifted(d, nz)
            pairs.append((i, i ^ (apart * pn)))
        return lax.ppermute(part, every, pairs)

    every = ("sec", "z", "p")
    peers = sorted(range(1, group), key=lambda k: (k != pn, -bin(k % pn).count("1"), k))
    arrived = [in_plane(send[k], k) for k in peers]

    across, centre, edge, own = pl.pallas_call(
        prepare_kernel,
        out_shape=(
            shaped((2, width, width), jnp.bfloat16),
            shaped((2, SIDE, SIDE), jnp.bfloat16),
            shaped((2, 2 * HALO, 2 * HALO), jnp.bfloat16),
            shaped((payload, SIDE), jnp.bfloat16),
        ),
        in_specs=[smem, hbm],
        out_specs=(vmem,) * 4,
        scratch_shapes=[pltpu.VMEM((width, width), jnp.float32), pltpu.SemaphoreType.DMA],
        compiler_params=params,
        cost_estimate=pl.CostEstimate(flops=0, bytes_accessed=8 << 20, transcendentals=0),
        name="matrices",
    )(detect_taps, send[0])

    plane_sums = pl.pallas_call(
        functools.partial(sum_kernel, nz, group),
        out_shape=[shaped((PATCH_DEV * (SIDE + FIELDS), SIDE), jnp.bfloat16)] * nz,
        in_specs=[vmem] * group,
        out_specs=[vmem] * nz,
        scratch_shapes=[pltpu.VMEM((group, PATCH_DEV, per_dest, SIDE), jnp.float32)],
        compiler_params=params,
        name="plane_sums",
    )(own, *arrived)
    gathered = [plane_sums[0]] + [along_z(plane_sums[d], d) for d in range(1, nz)]

    coadd, main, rest, first_rows, second_rows = pl.pallas_call(
        functools.partial(coadd_kernel, nz),
        out_shape=(
            shaped((SIDE, width), jnp.float32),
            shaped((SIDE, width), jnp.bfloat16),
            shaped((SIDE, width), jnp.bfloat16),
            shaped((HALO, width), jnp.bfloat16),
            shaped((HALO, width), jnp.bfloat16),
        ),
        in_specs=[vmem] * nz,
        out_specs=(vmem,) * 5,
        compiler_params=params,
        name="coadd",
    )(*gathered)


    def swap(rows, start):
        pairs = [(i, i + 1) for i in range(start, devices - 1, 2)]
        return lax.ppermute(rows, every, pairs + [(j, i) for i, j in pairs])

    first, second = swap(first_rows, 0), swap(second_rows, 1)

    inner = pl.pallas_call(
        centre_kernel,
        out_shape=shaped((SIDE, width), jnp.float32),
        in_specs=[vmem] * 4,
        out_specs=vmem,
        compiler_params=params,
        cost_estimate=pl.CostEstimate(
            flops=6 * SIDE * width * (SIDE + width), bytes_accessed=2 << 20, transcendentals=0
        ),
        name="detect_centre",
    )(main, rest, across, centre)
    detection = pl.pallas_call(
        edge_kernel,
        out_shape=shaped((SIDE, width), jnp.float32),
        in_specs=[vmem] * 5,
        out_specs=vmem,
        scratch_shapes=[pltpu.VMEM((2 * HALO, width), jnp.bfloat16)],
        compiler_params=params,
        name="detect_edges",
    )(inner, first, second, across, edge)
    return coadd, detection


def solution(mesh):
    ns, nd = mesh.shape["sec"], mesh.shape["dev"]
    nz = math.gcd(nd, 4)
    pn = nd // nz
    cut = Mesh(mesh.devices.reshape(ns, nz, pn), ("sec", "z", "p"))
    every = ("sec", "z", "p")
    placed = (
        P(None, every, None, None),
        P(every, None, None),
        P(None, every, None),
        P(),
        P(None, every, None),
        P(None, every, None),
        P(None, every, None),
        P(every, None),
        P(every, None),
        P(every, None),
        P(),
        P(),
    )
    return jax.shard_map(
        functools.partial(per_device, (nz, pn, ns)),
        mesh=cut,
        in_specs=placed,
        out_specs=(P(every, None), P(every, None)),
        check_vma=False,
    )
```

```python
import functools
import math

import jax
import jax.numpy as jnp
from jax import lax
from jax.experimental import pallas as pl
from jax.experimental.pallas import tpu as pltpu
from jax.sharding import Mesh
from jax.sharding import PartitionSpec as P

SIDE = 128
CAP = 2
PATCH_DEV = 4
HALO = 32
FIELDS = 4
VMEM_LIMIT = 48 * 1024 * 1024


def turned(q, pn):
    bits = (pn.bit_length() - 1) // 2
    return ((q >> bits) | (q << bits)) & (pn - 1) if bits else q


def shifted(d, nz):
    return 0 if d == 0 else d % (nz - 1) + 1


def tap_row(tap, count, start, width, reverse):
    lane = lax.broadcasted_iota(jnp.int32, (1, width), 1)
    row = jnp.zeros((1, width), jnp.float32)
    for k in range(count):
        at = start + (count - 1 - k if reverse else k)
        row = jnp.where(lane == at % width, tap(k), row)
    return row


def toeplitz(row, height):
    return pltpu.roll(
        jnp.broadcast_to(row, (height, row.shape[1])), 0, 1, stride=1, stride_axis=0
    )


def store_band(band_ref, tiles):
    blocks = band_ref.shape[0] // SIDE
    for i in range(blocks):
        for j in range(blocks):
            place = (pl.ds(i * SIDE, SIDE), pl.ds(j * SIDE, SIDE))
            if abs(i - j) <= 1:
                first = (j - i + 1) * SIDE
                band_ref[place] = tiles[:, first : first + SIDE]
            else:
                band_ref[place] = jnp.zeros((SIDE, SIDE), band_ref.dtype)


def dot32(left, right):
    return jnp.dot(left, right, preferred_element_type=jnp.float32)


def two_parts(value):
    high = value.astype(jnp.bfloat16)
    return high, (value - high.astype(jnp.float32)).astype(jnp.bfloat16)


def three_parts(value):
    high = value.astype(jnp.bfloat16)
    rest = value - high.astype(jnp.float32)
    mid = rest.astype(jnp.bfloat16)
    return high, mid, (rest - mid.astype(jnp.float32)).astype(jnp.bfloat16)


def warp_kernel(
    split,
    owner_hbm,
    patch_hbm,
    index_hbm,
    table_hbm,
    taps_hbm,
    weights_hbm,
    shift_hbm,
    scale_hbm,
    bias_hbm,
    raw_hbm,
    flat_hbm,
    *rest,
):
    nz, pn, ns = split
    outs, rest = rest[: ns * pn], rest[ns * pn :]
    warp_body(
        split,
        (
            owner_hbm,
            patch_hbm,
            index_hbm,
            table_hbm,
            taps_hbm,
            weights_hbm,
            shift_hbm,
            scale_hbm,
            bias_hbm,
            raw_hbm,
            flat_hbm,
        ),
        outs,
        *rest,
    )


def warp_body(
    split,
    inputs,
    outs,
    owner_ref,
    patch_ref,
    index_ref,
    table_ref,
    taps_ref,
    weights_ref,
    shift_ref,
    scale_ref,
    bias_ref,
    raw_ref,
    flat_ref,
    count_ref,
    band_ref,
    left_ref,
    mid_ref,
    slot_rows,
    weight_rows,
    small_sem,
    flat_sem,
    raw_sem,
    out_ref,
    out_sem,
):
    (
        owner_hbm,
        patch_hbm,
        index_hbm,
        table_hbm,
        taps_hbm,
        weights_hbm,
        shift_hbm,
        scale_hbm,
        bias_hbm,
        raw_hbm,
        flat_hbm,
    ) = inputs
    nz, pn, ns = split
    my_sec, my_p, my_z = lax.axis_index("sec"), lax.axis_index("p"), lax.axis_index("z")
    visits, _, rows, cols = raw_ref.shape
    terms, tap_count = taps_ref.shape[1], taps_ref.shape[3]
    half = tap_count // 2
    per_dest = nz * CAP
    data_rows = per_dest * SIDE

    small = [
        pltpu.make_async_copy(src, dst, small_sem.at[i])
        for i, (src, dst) in enumerate(
            (
                (taps_hbm, taps_ref),
                (bias_hbm, bias_ref),
                (owner_hbm, owner_ref),
                (patch_hbm, patch_ref),
                (index_hbm, index_ref),
                (table_hbm, table_ref),
                (weights_hbm, weights_ref),
                (shift_hbm, shift_ref),
                (scale_hbm, scale_ref),
            )
        )
    ]
    for copy in small:
        copy.start()
    flat_copy = pltpu.make_async_copy(flat_hbm, flat_ref, flat_sem)
    raw_copies = [
        pltpu.make_async_copy(raw_hbm.at[v], raw_ref.at[v], raw_sem.at[v]) for v in range(visits)
    ]
    raw_copies[0].start()
    flat_copy.start()
    for copy in raw_copies[1:]:
        copy.start()

    out_ref[...] = jnp.zeros_like(out_ref)
    slot_rows[...] = jnp.full(slot_rows.shape, -1.0, jnp.float32)
    weight_rows[...] = jnp.zeros_like(weight_rows)

    def clear(i, c):
        count_ref[i] = 0
        return c

    lax.fori_loop(0, count_ref.shape[0], clear, 0)
    for copy in small:
        copy.wait()

    def store_hat(ref, length, axis, shift, scale):
        centre = (length - 1) / 2.0
        count = length // SIDE
        for o in range(count):
            out_pos = o * SIDE + lax.broadcasted_iota(
                jnp.int32, (1, SIDE) if axis == 1 else (SIDE, 1), axis
            )
            source = scale * (out_pos.astype(jnp.float32) - centre) + centre + shift
            for i in range(count):
                at = (i, o) if axis == 1 else (o, i)
                place = tuple(pl.ds(k * SIDE, SIDE) for k in at)
                if abs(i - o) <= 1:
                    in_pos = i * SIDE + lax.broadcasted_iota(jnp.int32, (SIDE, SIDE), 1 - axis)
                    near = jnp.maximum(0.0, 1.0 - jnp.abs(in_pos.astype(jnp.float32) - source))
                    ref[place] = near.astype(jnp.bfloat16)
                else:
                    ref[place] = jnp.zeros((SIDE, SIDE), jnp.bfloat16)

    for visit in range(visits):
        for term in range(terms):
            for axis, reverse in ((1, True), (0, False)):
                row = tap_row(
                    lambda k: taps_ref[visit, term, axis, k],
                    tap_count,
                    SIDE - half,
                    3 * SIDE,
                    reverse,
                )
                store_band(
                    band_ref.at[visit, 2 * term + 1 - axis], toeplitz(row, SIDE).astype(jnp.bfloat16)
                )
        for axis, length in ((1, cols), (0, rows)):
            store_hat(
                band_ref.at[visit, 2 * terms + 1 - axis],
                length,
                axis,
                shift_ref[visit, 0, axis],
                scale_ref[visit, 0, axis],
            )

    def windows(length):
        wide = 2 * SIDE
        for at in range(0, length, wide):
            low, high = max(0, at - SIDE), min(length, at + wide + SIDE)
            yield pl.ds(at, min(wide, length - at)), pl.ds(low, high - low)

    def times_band(out, source, band):
        for o, k in windows(cols):
            out[:, o] = dot32(source[:, k], band[k, o]).astype(jnp.bfloat16)

    def band_times(out, band, source):
        for o, k in windows(rows):
            out[o, :] = dot32(band[o, k], source[k, :]).astype(jnp.bfloat16)

    row_blocks, col_blocks = rows // SIDE, cols // SIDE
    for visit in range(visits):
        left, mid = left_ref.at[visit], mid_ref.at[visit]
        bias = jnp.broadcast_to(bias_ref[visit], (SIDE, rows)).T
        raw_copies[visit].wait()
        if visit == 0:
            flat_copy.wait()
        for j in range(cols // SIDE):
            sl = pl.ds(j * SIDE, SIDE)
            left[:, sl] = ((raw_ref[visit, 0, :, sl] - bias) * flat_ref[0, :, sl]).astype(
                jnp.bfloat16
            )

        if terms == 1:
            times_band(mid, left, band_ref.at[visit, 0])
            for o, k in windows(rows):
                part = dot32(band_ref[visit, 1, o, k], mid[k, :])
                left[o, :] = (weights_ref[0, 0, visit] * part).astype(jnp.bfloat16)
        else:
            matched = None
            for term in range(terms):
                times_band(mid, left, band_ref.at[visit, 2 * term])
                part = weights_ref[0, term, visit] * dot32(band_ref[visit, 2 * term + 1], mid[...])
                matched = part if matched is None else matched + part
            left[...] = matched.astype(jnp.bfloat16)
        times_band(mid, left, band_ref.at[visit, 2 * terms])
        band_times(left, band_ref.at[visit, 2 * terms + 1], mid)

    for visit in range(visits):
        for i in range(row_blocks):
            for j in range(col_blocks):
                block = visit * (row_blocks * col_blocks) + i * col_blocks + j
                owner = owner_ref[block]
                rank = count_ref[owner]
                count_ref[owner] = rank + 1
                sec = owner // (nz * pn)
                dev = owner - sec * (nz * pn)
                z = dev // pn
                step = (dev - z * pn) ^ my_p
                step = jnp.where(my_sec == 0, step, turned(step, pn))
                dest = (sec ^ my_sec) * pn + step
                apart = z ^ my_z
                later = jnp.where(apart > 1, apart - 1, apart * (nz - 1))
                at = jnp.where(sec == 0, apart, later) * CAP + rank
                out_ref[dest, pl.ds(pl.multiple_of(at * SIDE, SIDE), SIDE), :] = left_ref[
                    visit, pl.ds(i * SIDE, SIDE), pl.ds(j * SIDE, SIDE)
                ]
                line = pl.ds(dest * per_dest + at, 1)
                slot_rows[line, :] = jnp.full((1, SIDE), patch_ref[block].astype(jnp.float32))
                weight_rows[line, :] = jnp.full((1, SIDE), table_ref[index_ref[block]])

    def out_copy(dest):
        return pltpu.make_async_copy(out_ref.at[dest], outs[dest], out_sem.at[dest])

    for dest in range(out_ref.shape[0]):
        part = pl.ds(dest * per_dest, per_dest)
        fields = jnp.concatenate(
            [slot_rows[part, :]]
            + [w.astype(jnp.float32) for w in three_parts(weight_rows[part, :])],
            axis=0,
        )
        out_ref[dest, pl.ds(data_rows, fields.shape[0]), :] = fields.astype(jnp.bfloat16)
        out_copy(dest).start()
    for dest in range(out_ref.shape[0]):
        out_copy(dest).wait()


def sum_kernel(nz, sources, chunks, *refs):
    ins, outs, weight_ref = refs[:sources], refs[sources:-1], refs[-1]
    per_dest = nz * CAP
    data_rows = per_dest * SIDE
    with_totals = chunks[0] == 0
    for g in range(sources):
        fields = ins[g][pl.ds(data_rows, FIELDS * per_dest), :].astype(jnp.float32)
        slot = fields[:per_dest]
        weight = (
            fields[per_dest : 2 * per_dest]
            + fields[2 * per_dest : 3 * per_dest]
            + fields[3 * per_dest :]
        )
        for j in range(PATCH_DEV):
            weight_ref[g, j] = jnp.where(slot == float(j), weight, 0.0)
    for z in range(nz):
        for place, c in enumerate(chunks):
            sums = [jnp.zeros((HALO, SIDE), jnp.float32) for _ in range(PATCH_DEV)]
            for g in range(sources):
                for r in range(CAP):
                    at = z * CAP + r
                    value = ins[g][pl.ds(at * SIDE + c * HALO, HALO), :].astype(jnp.float32)
                    for j in range(PATCH_DEV):
                        sums[j] = sums[j] + weight_ref[g, j, pl.ds(at, 1), :] * value
            for j in range(PATCH_DEV):
                row = (j * len(chunks) + place) * HALO
                outs[z][pl.ds(row, HALO), :] = sums[j].astype(jnp.bfloat16)
        if with_totals:
            totals = []
            for j in range(PATCH_DEV):
                total = jnp.zeros((1, SIDE), jnp.float32)
                for g in range(sources):
                    for r in range(CAP):
                        total = total + weight_ref[g, j, pl.ds(z * CAP + r, 1), :]
                totals.append(total)
            parts = [q.astype(jnp.float32) for q in three_parts(jnp.concatenate(totals, axis=0))]
            parts.append(jnp.zeros((PATCH_DEV, SIDE), jnp.float32))
            outs[z][pl.ds(PATCH_DEV * len(chunks) * HALO, FIELDS * PATCH_DEV), :] = (
                jnp.concatenate(parts, axis=0).astype(jnp.bfloat16)
            )


def totals_of(ins, start):
    total = jnp.zeros((PATCH_DEV, SIDE), jnp.float32)
    for ref in ins:
        extra = ref[pl.ds(start, FIELDS * PATCH_DEV), :].astype(jnp.float32)
        total = total + (
            extra[:PATCH_DEV] + extra[PATCH_DEV : 2 * PATCH_DEV] + extra[2 * PATCH_DEV : 3 * PATCH_DEV]
        )
    return jnp.maximum(total, 1.0)


def average(ins, row, count, total):
    numerator = ins[0][pl.ds(row, count), :].astype(jnp.float32)
    for ref in ins[1:]:
        numerator = numerator + ref[pl.ds(row, count), :].astype(jnp.float32)
    return numerator / total


def edges_kernel(*refs):
    ins, first_ref, second_ref = refs[:-2], refs[-2], refs[-1]
    odd = lax.axis_index("p") % 2
    total = totals_of(ins, 2 * PATCH_DEV * HALO)
    for j in range(PATCH_DEV):
        sl = pl.ds(j * SIDE, SIDE)
        rows = average(ins, 2 * j * HALO, 2 * HALO, total[j : j + 1])
        top, bottom = rows[:HALO], rows[HALO:]
        first_ref[:, sl] = jnp.where(odd == 0, bottom, top).astype(jnp.bfloat16)
        second_ref[:, sl] = jnp.where(odd == 0, top, bottom).astype(jnp.bfloat16)


def detect_kernel(nz, *refs):
    edges, inner = refs[:nz], refs[nz : 2 * nz]
    first_ref, second_ref, across_ref, centre_ref, edge_ref = refs[2 * nz : 2 * nz + 5]
    coadd_ref, out_ref, halo_ref = refs[2 * nz + 5 :]
    odd = lax.axis_index("p") % 2
    halo_ref[pl.ds(pl.multiple_of((1 - odd) * HALO, HALO), HALO)] = first_ref[...]
    halo_ref[pl.ds(pl.multiple_of(odd * HALO, HALO), HALO)] = second_ref[...]
    halo = halo_ref[...]
    total = totals_of(edges, 2 * PATCH_DEV * HALO)
    depth = SIDE - 2 * HALO
    for j in range(PATCH_DEV):
        sl = pl.ds(j * SIDE, SIDE)
        weight = total[j : j + 1]
        coadd_ref[pl.ds(0, HALO), sl] = average(edges, 2 * j * HALO, HALO, weight)
        coadd_ref[pl.ds(HALO, depth), sl] = average(inner, j * depth, depth, weight)
        coadd_ref[pl.ds(SIDE - HALO, HALO), sl] = average(edges, (2 * j + 1) * HALO, HALO, weight)
    main, rest = two_parts(coadd_ref[...])
    along = dot32(centre_ref[0], main) + (
        dot32(centre_ref[0], rest) + dot32(centre_ref[1], main)
    )
    ends = dot32(edge_ref[0], halo) + dot32(edge_ref[1], halo)
    along = jnp.concatenate(
        [along[:HALO] + ends[:HALO], along[HALO : SIDE - HALO], along[SIDE - HALO :] + ends[HALO:]],
        axis=0,
    )
    out_ref[...] = dot_parts(along, across_ref)


def prepare_kernel(taps_ref, own_hbm, across_ref, centre_ref, edge_ref, own_ref, band_ref, own_sem):
    own_copy = pltpu.make_async_copy(own_hbm, own_ref, own_sem)
    own_copy.start()
    tap_count = taps_ref.shape[1]
    half = tap_count // 2
    across = tap_row(lambda k: taps_ref[1, k], tap_count, SIDE - half, 3 * SIDE, True)
    store_band(band_ref, toeplitz(across, SIDE))
    across_ref[0], across_ref[1] = two_parts(band_ref[...])
    down = tap_row(lambda k: taps_ref[0, k], tap_count, SIDE - half, 3 * SIDE, False)
    centre_ref[0], centre_ref[1] = two_parts(toeplitz(down, SIDE)[:, SIDE : 2 * SIDE])
    lane = lax.broadcasted_iota(jnp.int32, (2 * HALO, SIDE), 1)
    row = lax.broadcasted_iota(jnp.int32, (2 * HALO, SIDE), 0)
    before = tap_row(lambda k: taps_ref[0, k], tap_count, HALO - half, SIDE, False)
    after = tap_row(lambda k: taps_ref[0, k], tap_count, SIDE - HALO - half, SIDE, False)
    edge = jnp.where(
        (row < HALO) & (lane < HALO),
        toeplitz(before, 2 * HALO),
        jnp.where(
            (row >= HALO) & (lane >= HALO) & (lane < 2 * HALO), toeplitz(after, 2 * HALO), 0.0
        ),
    )
    edge_ref[0], edge_ref[1] = two_parts(edge[:, : 2 * HALO])
    own_copy.wait()


def dot_parts(left, across_ref):
    main, rest = two_parts(left)
    both = dot32(jnp.concatenate([main, rest], axis=0), across_ref[0])
    return both[: left.shape[0]] + (dot32(main, across_ref[1]) + both[left.shape[0] :])


def per_device(
    split,
    raw_pixels,
    flat_field,
    bias_rows,
    psf_taps,
    term_weights,
    warp_shift,
    warp_scale,
    owner_of,
    patch_slot,
    weight_index,
    weight_table,
    detect_taps,
):
    nz, pn, ns = split
    devices = nz * pn * ns
    group = ns * pn
    visits, _, rows, cols = raw_pixels.shape
    blocks = owner_of.shape[0]
    terms = psf_taps.shape[1]
    per_dest = nz * CAP
    payload = per_dest * (SIDE + FIELDS)
    width = PATCH_DEV * SIDE
    smem = pl.BlockSpec(memory_space=pltpu.SMEM)
    vmem = pl.BlockSpec(memory_space=pltpu.VMEM)
    hbm = pl.BlockSpec(memory_space=pltpu.HBM)
    params = pltpu.CompilerParams(vmem_limit_bytes=VMEM_LIMIT)

    def shaped(shape, dtype):
        return jax.ShapeDtypeStruct(shape, dtype)

    weights = term_weights.transpose(1, 2, 0)
    send = pl.pallas_call(
        functools.partial(warp_kernel, split),
        out_shape=[shaped((payload, SIDE), jnp.bfloat16)] * group,
        in_specs=[hbm] * 11,
        out_specs=[hbm] * group,
        scratch_shapes=[
            pltpu.SMEM((blocks,), jnp.int32),
            pltpu.SMEM((blocks,), jnp.int32),
            pltpu.SMEM((blocks,), jnp.int32),
            pltpu.SMEM(weight_table.shape, jnp.float32),
            pltpu.SMEM(psf_taps.shape, jnp.float32),
            pltpu.SMEM(weights.shape, jnp.float32),
            pltpu.SMEM(warp_shift.shape, jnp.float32),
            pltpu.SMEM(warp_scale.shape, jnp.float32),
            pltpu.VMEM(bias_rows.shape, jnp.float32),
            pltpu.VMEM(raw_pixels.shape, jnp.float32),
            pltpu.VMEM(flat_field.shape, jnp.float32),
            pltpu.SMEM((devices,), jnp.int32),
            pltpu.VMEM((visits, 2 * terms + 2, rows, cols), jnp.bfloat16),
            pltpu.VMEM((visits, rows, cols), jnp.bfloat16),
            pltpu.VMEM((visits, rows, cols), jnp.bfloat16),
            pltpu.VMEM((group * per_dest, SIDE), jnp.float32),
            pltpu.VMEM((group * per_dest, SIDE), jnp.float32),
            pltpu.SemaphoreType.DMA((9,)),
            pltpu.SemaphoreType.DMA,
            pltpu.SemaphoreType.DMA((visits,)),
            pltpu.VMEM((group, payload, SIDE), jnp.bfloat16),
            pltpu.SemaphoreType.DMA((group,)),
        ],
        compiler_params=pltpu.CompilerParams(vmem_limit_bytes=60 * 1024 * 1024),
        name="warp",
    )(
        owner_of.reshape(blocks),
        patch_slot.reshape(blocks),
        weight_index.reshape(blocks),
        weight_table,
        psf_taps,
        weights,
        warp_shift,
        warp_scale,
        bias_rows,
        raw_pixels,
        flat_field,
    )
    def in_plane(part, k):
        pairs = []
        for sec in range(ns):
            for p in range(pn):
                q = k % pn if sec == 0 else turned(k % pn, pn)
                pairs.append((sec * pn + p, (sec ^ (k // pn)) * pn + (p ^ q)))
        return lax.ppermute(part, ("sec", "p"), pairs)

    def along_z(part, d):
        pairs = []
        for i in range(devices):
            apart = d if i < nz * pn else shifted(d, nz)
            pairs.append((i, i ^ (apart * pn)))
        return lax.ppermute(part, every, pairs)

    every = ("sec", "z", "p")
    peers = sorted(range(1, group), key=lambda k: (k != pn, -bin(k % pn).count("1"), k))
    arrived = [in_plane(send[k], k) for k in peers]

    across, centre, edge, own = pl.pallas_call(
        prepare_kernel,
        out_shape=(
            shaped((2, width, width), jnp.bfloat16),
            shaped((2, SIDE, SIDE), jnp.bfloat16),
            shaped((2, 2 * HALO, 2 * HALO), jnp.bfloat16),
            shaped((payload, SIDE), jnp.bfloat16),
        ),
        in_specs=[smem, hbm],
        out_specs=(vmem,) * 4,
        scratch_shapes=[pltpu.VMEM((width, width), jnp.float32), pltpu.SemaphoreType.DMA],
        compiler_params=params,
        cost_estimate=pl.CostEstimate(flops=0, bytes_accessed=8 << 20, transcendentals=0),
        name="matrices",
    )(detect_taps, send[0])

    def plane_sums(chunks, rows, name):
        return pl.pallas_call(
            functools.partial(sum_kernel, nz, group, chunks),
            out_shape=[shaped((rows, SIDE), jnp.bfloat16)] * nz,
            in_specs=[vmem] * group,
            out_specs=[vmem] * nz,
            scratch_shapes=[pltpu.VMEM((group, PATCH_DEV, per_dest, SIDE), jnp.float32)],
            compiler_params=params,
            cost_estimate=pl.CostEstimate(flops=0, bytes_accessed=4 << 20, transcendentals=0),
            name=name,
        )(own, *arrived)

    last = SIDE // HALO - 1
    edge_rows = PATCH_DEV * (2 * HALO + FIELDS)
    edge_sums = plane_sums((0, last), edge_rows, "edge_sums")
    inner_sums = plane_sums(tuple(range(1, last)), PATCH_DEV * (SIDE - 2 * HALO), "inner_sums")
    edges = [edge_sums[0]] + [along_z(edge_sums[d], d) for d in range(1, nz)]
    inner = [inner_sums[0]] + [along_z(inner_sums[d], d) for d in range(1, nz)]

    first_rows, second_rows = pl.pallas_call(
        edges_kernel,
        out_shape=[shaped((HALO, width), jnp.bfloat16)] * 2,
        in_specs=[vmem] * nz,
        out_specs=[vmem] * 2,
        compiler_params=params,
        name="edge_rows",
    )(*edges)

    def swap(rows, start):
        pairs = [(i, i + 1) for i in range(start, devices - 1, 2)]
        return lax.ppermute(rows, every, pairs + [(j, i) for i, j in pairs])

    first, second = swap(first_rows, 0), swap(second_rows, 1)

    coadd, detection = pl.pallas_call(
        functools.partial(detect_kernel, nz),
        out_shape=[shaped((SIDE, width), jnp.float32)] * 2,
        in_specs=[vmem] * (2 * nz + 5),
        out_specs=[vmem] * 2,
        scratch_shapes=[pltpu.VMEM((2 * HALO, width), jnp.bfloat16)],
        compiler_params=params,
        name="coadd_detect",
    )(*edges, *inner, first, second, across, centre, edge)
    return coadd, detection


def solution(mesh):
    ns, nd = mesh.shape["sec"], mesh.shape["dev"]
    nz = math.gcd(nd, 4)
    pn = nd // nz
    cut = Mesh(mesh.devices.reshape(ns, nz, pn), ("sec", "z", "p"))
    every = ("sec", "z", "p")
    placed = (
        P(None, every, None, None),
        P(every, None, None),
        P(None, every, None),
        P(),
        P(None, every, None),
        P(None, every, None),
        P(None, every, None),
        P(every, None),
        P(every, None),
        P(every, None),
        P(),
        P(),
    )
    return jax.shard_map(
        functools.partial(per_device, (nz, pn, ns)),
        mesh=cut,
        in_specs=placed,
        out_specs=(P(every, None), P(every, None)),
        check_vma=False,
    )
```

```python
import functools
import math

import jax
import jax.numpy as jnp
from jax import lax
from jax.experimental import pallas as pl
from jax.experimental.pallas import tpu as pltpu
from jax.sharding import Mesh
from jax.sharding import PartitionSpec as P

SIDE = 128
CAP = 2
PATCH_DEV = 4
HALO = 32
FIELDS = 4
TIED = 2
TAIL = 2
PART = SIDE // 2
VMEM_LIMIT = 48 * 1024 * 1024


def turned(q, pn):
    bits = (pn.bit_length() - 1) // 2
    return ((q >> bits) | (q << bits)) & (pn - 1) if bits else q


def shifted(d, nz):
    return 0 if d == 0 else d % (nz - 1) + 1


def tap_row(tap, count, start, width, reverse):
    lane = lax.broadcasted_iota(jnp.int32, (1, width), 1)
    row = jnp.zeros((1, width), jnp.float32)
    for k in range(count):
        at = start + (count - 1 - k if reverse else k)
        row = jnp.where(lane == at % width, tap(k), row)
    return row


def toeplitz(row, height):
    return pltpu.roll(
        jnp.broadcast_to(row, (height, row.shape[1])), 0, 1, stride=1, stride_axis=0
    )


def store_band(band_ref, tiles):
    blocks = band_ref.shape[0] // SIDE
    for i in range(blocks):
        for j in range(blocks):
            place = (pl.ds(i * SIDE, SIDE), pl.ds(j * SIDE, SIDE))
            if abs(i - j) <= 1:
                first = (j - i + 1) * SIDE
                band_ref[place] = tiles[:, first : first + SIDE]
            else:
                band_ref[place] = jnp.zeros((SIDE, SIDE), band_ref.dtype)


def dot32(left, right):
    return jnp.dot(left, right, preferred_element_type=jnp.float32)


def two_parts(value):
    high = value.astype(jnp.bfloat16)
    return high, (value - high.astype(jnp.float32)).astype(jnp.bfloat16)


def three_parts(value):
    high = value.astype(jnp.bfloat16)
    rest = value - high.astype(jnp.float32)
    mid = rest.astype(jnp.bfloat16)
    return high, mid, (rest - mid.astype(jnp.float32)).astype(jnp.bfloat16)


def warp_kernel(
    split,
    owner_hbm,
    patch_hbm,
    index_hbm,
    table_hbm,
    taps_hbm,
    weights_hbm,
    shift_hbm,
    scale_hbm,
    bias_hbm,
    raw_hbm,
    flat_hbm,
    *rest,
):
    nz, pn, ns = split
    outs, rest = rest[: 2 * ns * pn], rest[2 * ns * pn :]
    warp_body(
        split,
        (
            owner_hbm,
            patch_hbm,
            index_hbm,
            table_hbm,
            taps_hbm,
            weights_hbm,
            shift_hbm,
            scale_hbm,
            bias_hbm,
            raw_hbm,
            flat_hbm,
        ),
        outs,
        *rest,
    )


def warp_body(
    split,
    inputs,
    outs,
    owner_ref,
    patch_ref,
    index_ref,
    table_ref,
    taps_ref,
    weights_ref,
    shift_ref,
    scale_ref,
    bias_ref,
    raw_ref,
    flat_ref,
    count_ref,
    band_ref,
    left_ref,
    mid_ref,
    slot_rows,
    weight_rows,
    small_sem,
    flat_sem,
    raw_sem,
    out_ref,
    out_sem,
):
    (
        owner_hbm,
        patch_hbm,
        index_hbm,
        table_hbm,
        taps_hbm,
        weights_hbm,
        shift_hbm,
        scale_hbm,
        bias_hbm,
        raw_hbm,
        flat_hbm,
    ) = inputs
    nz, pn, ns = split
    my_sec, my_p, my_z = lax.axis_index("sec"), lax.axis_index("p"), lax.axis_index("z")
    visits, _, rows, cols = raw_ref.shape
    terms, tap_count = taps_ref.shape[1], taps_ref.shape[3]
    half = tap_count // 2
    per_dest = nz * CAP
    data_rows = per_dest * PART
    edge_rows = data_rows + FIELDS * per_dest

    small = [
        pltpu.make_async_copy(src, dst, small_sem.at[i])
        for i, (src, dst) in enumerate(
            (
                (taps_hbm, taps_ref),
                (bias_hbm, bias_ref),
                (owner_hbm, owner_ref),
                (patch_hbm, patch_ref),
                (index_hbm, index_ref),
                (table_hbm, table_ref),
                (weights_hbm, weights_ref),
                (shift_hbm, shift_ref),
                (scale_hbm, scale_ref),
            )
        )
    ]
    for copy in small:
        copy.start()
    flat_copy = pltpu.make_async_copy(flat_hbm, flat_ref, flat_sem)
    raw_copies = [
        pltpu.make_async_copy(raw_hbm.at[v], raw_ref.at[v], raw_sem.at[v]) for v in range(visits)
    ]
    raw_copies[0].start()
    flat_copy.start()
    for copy in raw_copies[1:]:
        copy.start()

    out_ref[...] = jnp.zeros_like(out_ref)
    slot_rows[...] = jnp.full(slot_rows.shape, -1.0, jnp.float32)
    weight_rows[...] = jnp.zeros_like(weight_rows)

    def clear(i, c):
        count_ref[i] = 0
        return c

    lax.fori_loop(0, count_ref.shape[0], clear, 0)
    for copy in small:
        copy.wait()

    def store_hat(ref, length, axis, shift, scale):
        centre = (length - 1) / 2.0
        count = length // SIDE
        for o in range(count):
            out_pos = o * SIDE + lax.broadcasted_iota(
                jnp.int32, (1, SIDE) if axis == 1 else (SIDE, 1), axis
            )
            source = scale * (out_pos.astype(jnp.float32) - centre) + centre + shift
            for i in range(count):
                at = (i, o) if axis == 1 else (o, i)
                place = tuple(pl.ds(k * SIDE, SIDE) for k in at)
                if abs(i - o) <= 1:
                    in_pos = i * SIDE + lax.broadcasted_iota(jnp.int32, (SIDE, SIDE), 1 - axis)
                    near = jnp.maximum(0.0, 1.0 - jnp.abs(in_pos.astype(jnp.float32) - source))
                    ref[place] = near.astype(jnp.bfloat16)
                else:
                    ref[place] = jnp.zeros((SIDE, SIDE), jnp.bfloat16)

    for visit in range(visits):
        for term in range(terms):
            for axis, reverse in ((1, True), (0, False)):
                row = tap_row(
                    lambda k: taps_ref[visit, term, axis, k],
                    tap_count,
                    SIDE - half,
                    3 * SIDE,
                    reverse,
                )
                store_band(
                    band_ref.at[visit, 2 * term + 1 - axis], toeplitz(row, SIDE).astype(jnp.bfloat16)
                )
        for axis, length in ((1, cols), (0, rows)):
            store_hat(
                band_ref.at[visit, 2 * terms + 1 - axis],
                length,
                axis,
                shift_ref[visit, 0, axis],
                scale_ref[visit, 0, axis],
            )

    def windows(length):
        wide = 2 * SIDE
        for at in range(0, length, wide):
            low, high = max(0, at - SIDE), min(length, at + wide + SIDE)
            yield pl.ds(at, min(wide, length - at)), pl.ds(low, high - low)

    def times_band(out, source, band):
        for o, k in windows(cols):
            out[:, o] = dot32(source[:, k], band[k, o]).astype(jnp.bfloat16)

    def band_times(out, band, source):
        for o, k in windows(rows):
            out[o, :] = dot32(band[o, k], source[k, :]).astype(jnp.bfloat16)

    row_blocks, col_blocks = rows // SIDE, cols // SIDE
    for visit in range(visits):
        left, mid = left_ref.at[visit], mid_ref.at[visit]
        bias = jnp.broadcast_to(bias_ref[visit], (SIDE, rows)).T
        raw_copies[visit].wait()
        if visit == 0:
            flat_copy.wait()
        for j in range(cols // SIDE):
            sl = pl.ds(j * SIDE, SIDE)
            left[:, sl] = ((raw_ref[visit, 0, :, sl] - bias) * flat_ref[0, :, sl]).astype(
                jnp.bfloat16
            )

        if terms == 1:
            times_band(mid, left, band_ref.at[visit, 0])
            for o, k in windows(rows):
                part = dot32(band_ref[visit, 1, o, k], mid[k, :])
                left[o, :] = (weights_ref[0, 0, visit] * part).astype(jnp.bfloat16)
        else:
            matched = None
            for term in range(terms):
                times_band(mid, left, band_ref.at[visit, 2 * term])
                part = weights_ref[0, term, visit] * dot32(band_ref[visit, 2 * term + 1], mid[...])
                matched = part if matched is None else matched + part
            left[...] = matched.astype(jnp.bfloat16)
        times_band(mid, left, band_ref.at[visit, 2 * terms])
        band_times(left, band_ref.at[visit, 2 * terms + 1], mid)

    for visit in range(visits):
        for i in range(row_blocks):
            for j in range(col_blocks):
                block = visit * (row_blocks * col_blocks) + i * col_blocks + j
                owner = owner_ref[block]
                rank = count_ref[owner]
                count_ref[owner] = rank + 1
                sec = owner // (nz * pn)
                dev = owner - sec * (nz * pn)
                z = dev // pn
                step = (dev - z * pn) ^ my_p
                step = jnp.where(my_sec == 0, step, turned(step, pn))
                dest = (sec ^ my_sec) * pn + step
                apart = z ^ my_z
                later = jnp.where(apart > 1, apart - 1, apart * (nz - 1))
                at = jnp.where(sec == 0, apart, later) * CAP + rank
                first = pl.multiple_of(at * PART, PART)
                columns = pl.ds(j * SIDE, SIDE)
                for target, source, count in (
                    (first, 0, HALO),
                    (first + HALO, SIDE - HALO, HALO),
                    (first + edge_rows, HALO, SIDE - 2 * HALO),
                ):
                    out_ref[dest, pl.ds(target, count), :] = left_ref[
                        visit, pl.ds(i * SIDE + source, count), columns
                    ]
                line = pl.ds(dest * per_dest + at, 1)
                slot_rows[line, :] = jnp.full((1, SIDE), patch_ref[block].astype(jnp.float32))
                weight_rows[line, :] = jnp.full((1, SIDE), table_ref[index_ref[block]])

    group = out_ref.shape[0]
    copies = []
    for dest in range(group):
        part = pl.ds(dest * per_dest, per_dest)
        fields = jnp.concatenate(
            [slot_rows[part, :]]
            + [w.astype(jnp.float32) for w in three_parts(weight_rows[part, :])],
            axis=0,
        )
        out_ref[dest, pl.ds(data_rows, fields.shape[0]), :] = fields.astype(jnp.bfloat16)
    for i, rows_of in enumerate((pl.ds(0, edge_rows), pl.ds(edge_rows, data_rows))):
        for dest in range(group):
            copies.append(
                pltpu.make_async_copy(
                    out_ref.at[dest, rows_of], outs[i * group + dest], out_sem.at[i, dest]
                )
            )
            copies[-1].start()
    for copy in copies:
        copy.wait()


def add_blocks(nz, ins, weight_ref, outs):
    for z in range(nz):
        for place in range(PART // HALO):
            sums = [jnp.zeros((HALO, SIDE), jnp.float32) for _ in range(PATCH_DEV)]
            for g, ref in enumerate(ins):
                for r in range(CAP):
                    at = z * CAP + r
                    value = ref[pl.ds(at * PART + place * HALO, HALO), :].astype(jnp.float32)
                    for j in range(PATCH_DEV):
                        sums[j] = sums[j] + weight_ref[g, j, pl.ds(at, 1), :] * value
            for j in range(PATCH_DEV):
                row = j * PART + place * HALO
                outs[z][pl.ds(row, HALO), :] = sums[j].astype(jnp.bfloat16)


def edge_sum_kernel(nz, sources, *refs):
    ins, outs, weight_ref = refs[:sources], refs[sources:-1], refs[-1]
    per_dest = nz * CAP
    for g in range(sources):
        fields = ins[g][pl.ds(per_dest * PART, FIELDS * per_dest), :].astype(jnp.float32)
        slot = fields[:per_dest]
        weight = (
            fields[per_dest : 2 * per_dest]
            + fields[2 * per_dest : 3 * per_dest]
            + fields[3 * per_dest :]
        )
        for j in range(PATCH_DEV):
            weight_ref[g, j] = jnp.where(slot == float(j), weight, 0.0)
    add_blocks(nz, ins, weight_ref, outs)
    for z in range(nz):
        totals = []
        for j in range(PATCH_DEV):
            total = jnp.zeros((1, SIDE), jnp.float32)
            for g in range(sources):
                for r in range(CAP):
                    total = total + weight_ref[g, j, pl.ds(z * CAP + r, 1), :]
            totals.append(total)
        parts = [q.astype(jnp.float32) for q in three_parts(jnp.concatenate(totals, axis=0))]
        parts.append(jnp.zeros((PATCH_DEV, SIDE), jnp.float32))
        outs[z][pl.ds(PATCH_DEV * PART, FIELDS * PATCH_DEV), :] = jnp.concatenate(
            parts, axis=0
        ).astype(jnp.bfloat16)


def inner_sum_kernel(nz, sources, weight_ref, *refs):
    add_blocks(nz, refs[:sources], weight_ref, refs[sources:])


def totals_of(ins, start):
    total = jnp.zeros((PATCH_DEV, SIDE), jnp.float32)
    for ref in ins:
        extra = ref[pl.ds(start, FIELDS * PATCH_DEV), :].astype(jnp.float32)
        total = total + (
            extra[:PATCH_DEV] + extra[PATCH_DEV : 2 * PATCH_DEV] + extra[2 * PATCH_DEV : 3 * PATCH_DEV]
        )
    return jnp.maximum(total, 1.0)


def average(ins, row, count, total):
    numerator = ins[0][pl.ds(row, count), :].astype(jnp.float32)
    for ref in ins[1:]:
        numerator = numerator + ref[pl.ds(row, count), :].astype(jnp.float32)
    return numerator / total


def edges_kernel(*refs):
    ins, first_ref, second_ref = refs[:-2], refs[-2], refs[-1]
    odd = lax.axis_index("p") % 2
    total = totals_of(ins, 2 * PATCH_DEV * HALO)
    for j in range(PATCH_DEV):
        sl = pl.ds(j * SIDE, SIDE)
        rows = average(ins, 2 * j * HALO, 2 * HALO, total[j : j + 1])
        top, bottom = rows[:HALO], rows[HALO:]
        first_ref[:, sl] = jnp.where(odd == 0, bottom, top).astype(jnp.bfloat16)
        second_ref[:, sl] = jnp.where(odd == 0, top, bottom).astype(jnp.bfloat16)


def detect_kernel(nz, *refs):
    edges, inner = refs[:nz], refs[nz : 2 * nz]
    first_ref, second_ref, across_ref, centre_ref, edge_ref = refs[2 * nz : 2 * nz + 5]
    coadd_ref, out_ref, halo_ref = refs[2 * nz + 5 :]
    odd = lax.axis_index("p") % 2
    halo_ref[pl.ds(pl.multiple_of((1 - odd) * HALO, HALO), HALO)] = first_ref[...]
    halo_ref[pl.ds(pl.multiple_of(odd * HALO, HALO), HALO)] = second_ref[...]
    halo = halo_ref[...]
    total = totals_of(edges, 2 * PATCH_DEV * HALO)
    depth = SIDE - 2 * HALO
    for j in range(PATCH_DEV):
        sl = pl.ds(j * SIDE, SIDE)
        weight = total[j : j + 1]
        coadd_ref[pl.ds(0, HALO), sl] = average(edges, 2 * j * HALO, HALO, weight)
        coadd_ref[pl.ds(HALO, depth), sl] = average(inner, j * depth, depth, weight)
        coadd_ref[pl.ds(SIDE - HALO, HALO), sl] = average(edges, (2 * j + 1) * HALO, HALO, weight)
    main, rest = two_parts(coadd_ref[...])
    along = dot32(centre_ref[0], main) + (
        dot32(centre_ref[0], rest) + dot32(centre_ref[1], main)
    )
    ends = dot32(edge_ref[0], halo) + dot32(edge_ref[1], halo)
    along = jnp.concatenate(
        [along[:HALO] + ends[:HALO], along[HALO : SIDE - HALO], along[SIDE - HALO :] + ends[HALO:]],
        axis=0,
    )
    out_ref[...] = dot_parts(along, across_ref)


def prepare_kernel(taps_ref, *refs):
    owns_hbm, (across_ref, centre_ref, edge_ref), owns = refs[:2], refs[2:5], refs[5:7]
    band_ref, own_sem = refs[7:]
    own_copies = [
        pltpu.make_async_copy(owns_hbm[i], owns[i], own_sem.at[i]) for i in range(len(owns))
    ]
    for copy in own_copies:
        copy.start()
    tap_count = taps_ref.shape[1]
    half = tap_count // 2
    across = tap_row(lambda k: taps_ref[1, k], tap_count, SIDE - half, 3 * SIDE, True)
    store_band(band_ref, toeplitz(across, SIDE))
    across_ref[0], across_ref[1] = two_parts(band_ref[...])
    down = tap_row(lambda k: taps_ref[0, k], tap_count, SIDE - half, 3 * SIDE, False)
    centre_ref[0], centre_ref[1] = two_parts(toeplitz(down, SIDE)[:, SIDE : 2 * SIDE])
    lane = lax.broadcasted_iota(jnp.int32, (2 * HALO, SIDE), 1)
    row = lax.broadcasted_iota(jnp.int32, (2 * HALO, SIDE), 0)
    before = tap_row(lambda k: taps_ref[0, k], tap_count, HALO - half, SIDE, False)
    after = tap_row(lambda k: taps_ref[0, k], tap_count, SIDE - HALO - half, SIDE, False)
    edge = jnp.where(
        (row < HALO) & (lane < HALO),
        toeplitz(before, 2 * HALO),
        jnp.where(
            (row >= HALO) & (lane >= HALO) & (lane < 2 * HALO), toeplitz(after, 2 * HALO), 0.0
        ),
    )
    edge_ref[0], edge_ref[1] = two_parts(edge[:, : 2 * HALO])
    for copy in own_copies:
        copy.wait()


def dot_parts(left, across_ref):
    main, rest = two_parts(left)
    both = dot32(jnp.concatenate([main, rest], axis=0), across_ref[0])
    return both[: left.shape[0]] + (dot32(main, across_ref[1]) + both[left.shape[0] :])


def per_device(
    split,
    raw_pixels,
    flat_field,
    bias_rows,
    psf_taps,
    term_weights,
    warp_shift,
    warp_scale,
    owner_of,
    patch_slot,
    weight_index,
    weight_table,
    detect_taps,
):
    nz, pn, ns = split
    devices = nz * pn * ns
    group = ns * pn
    visits, _, rows, cols = raw_pixels.shape
    blocks = owner_of.shape[0]
    terms = psf_taps.shape[1]
    per_dest = nz * CAP
    inner_rows = per_dest * PART
    edge_rows = inner_rows + FIELDS * per_dest
    width = PATCH_DEV * SIDE
    smem = pl.BlockSpec(memory_space=pltpu.SMEM)
    vmem = pl.BlockSpec(memory_space=pltpu.VMEM)
    hbm = pl.BlockSpec(memory_space=pltpu.HBM)
    params = pltpu.CompilerParams(vmem_limit_bytes=VMEM_LIMIT)

    def shaped(shape, dtype):
        return jax.ShapeDtypeStruct(shape, dtype)

    weights = term_weights.transpose(1, 2, 0)
    send = pl.pallas_call(
        functools.partial(warp_kernel, split),
        out_shape=[shaped((edge_rows, SIDE), jnp.bfloat16)] * group
        + [shaped((inner_rows, SIDE), jnp.bfloat16)] * group,
        in_specs=[hbm] * 11,
        out_specs=[hbm] * (2 * group),
        scratch_shapes=[
            pltpu.SMEM((blocks,), jnp.int32),
            pltpu.SMEM((blocks,), jnp.int32),
            pltpu.SMEM((blocks,), jnp.int32),
            pltpu.SMEM(weight_table.shape, jnp.float32),
            pltpu.SMEM(psf_taps.shape, jnp.float32),
            pltpu.SMEM(weights.shape, jnp.float32),
            pltpu.SMEM(warp_shift.shape, jnp.float32),
            pltpu.SMEM(warp_scale.shape, jnp.float32),
            pltpu.VMEM(bias_rows.shape, jnp.float32),
            pltpu.VMEM(raw_pixels.shape, jnp.float32),
            pltpu.VMEM(flat_field.shape, jnp.float32),
            pltpu.SMEM((devices,), jnp.int32),
            pltpu.VMEM((visits, 2 * terms + 2, rows, cols), jnp.bfloat16),
            pltpu.VMEM((visits, rows, cols), jnp.bfloat16),
            pltpu.VMEM((visits, rows, cols), jnp.bfloat16),
            pltpu.VMEM((group * per_dest, SIDE), jnp.float32),
            pltpu.VMEM((group * per_dest, SIDE), jnp.float32),
            pltpu.SemaphoreType.DMA((9,)),
            pltpu.SemaphoreType.DMA,
            pltpu.SemaphoreType.DMA((visits,)),
            pltpu.VMEM((group, edge_rows + inner_rows, SIDE), jnp.bfloat16),
            pltpu.SemaphoreType.DMA((2, group)),
        ],
        compiler_params=pltpu.CompilerParams(vmem_limit_bytes=60 * 1024 * 1024),
        name="warp",
    )(
        owner_of.reshape(blocks),
        patch_slot.reshape(blocks),
        weight_index.reshape(blocks),
        weight_table,
        psf_taps,
        weights,
        warp_shift,
        warp_scale,
        bias_rows,
        raw_pixels,
        flat_field,
    )
    def in_plane(part, k):
        pairs = []
        for sec in range(ns):
            for p in range(pn):
                q = k % pn if sec == 0 else turned(k % pn, pn)
                pairs.append((sec * pn + p, (sec ^ (k // pn)) * pn + (p ^ q)))
        return lax.ppermute(part, ("sec", "p"), pairs)

    def along_z(part, d):
        pairs = []
        for i in range(devices):
            apart = d if i < nz * pn else shifted(d, nz)
            pairs.append((i, i ^ (apart * pn)))
        return lax.ppermute(part, every, pairs)

    every = ("sec", "z", "p")
    peers = sorted(range(1, group), key=lambda k: (k != pn, -bin(k % pn).count("1"), k))
    edge_blocks = [in_plane(send[k], k) for k in peers]

    across, centre, edge, own_edge, own_inner = pl.pallas_call(
        prepare_kernel,
        out_shape=(
            shaped((2, width, width), jnp.bfloat16),
            shaped((2, SIDE, SIDE), jnp.bfloat16),
            shaped((2, 2 * HALO, 2 * HALO), jnp.bfloat16),
            shaped((edge_rows, SIDE), jnp.bfloat16),
            shaped((inner_rows, SIDE), jnp.bfloat16),
        ),
        in_specs=[smem, hbm, hbm],
        out_specs=(vmem,) * 5,
        scratch_shapes=[pltpu.VMEM((width, width), jnp.float32), pltpu.SemaphoreType.DMA((2,))],
        compiler_params=params,
        cost_estimate=pl.CostEstimate(flops=0, bytes_accessed=8 << 20, transcendentals=0),
        name="matrices",
    )(detect_taps, send[0], send[group])

    busy = pl.CostEstimate(flops=0, bytes_accessed=4 << 20, transcendentals=0)
    edge_sums = list(pl.pallas_call(
        functools.partial(edge_sum_kernel, nz, group),
        out_shape=[shaped((PATCH_DEV * (PART + FIELDS), SIDE), jnp.bfloat16)] * nz
        + [shaped((group, PATCH_DEV, per_dest, SIDE), jnp.float32)],
        in_specs=[vmem] * group,
        out_specs=[vmem] * (nz + 1),
        compiler_params=params,
        cost_estimate=busy,
        name="edge_sums",
    )(own_edge, *edge_blocks))
    edges = [edge_sums[0]] + [along_z(edge_sums[d], d) for d in range(1, nz)]
    count = 2
    held = lax.optimization_barrier((edge_blocks[TIED], *(send[group + k] for k in peers[:-TAIL])))
    kept = lax.optimization_barrier((*edges[1:3], *(send[group + k] for k in peers[-TAIL:])))
    edges[1 : 1 + count], kept = kept[:count], kept[count:]
    inner_blocks = [in_plane(part, k) for part, k in zip((*held[1:], *kept), peers)]
    inner_sums = pl.pallas_call(
        functools.partial(inner_sum_kernel, nz, group),
        out_shape=[shaped((PATCH_DEV * PART, SIDE), jnp.bfloat16)] * nz,
        in_specs=[vmem] * (group + 1),
        out_specs=[vmem] * nz,
        compiler_params=params,
        cost_estimate=busy,
        name="inner_sums",
    )(edge_sums[nz], own_inner, *inner_blocks)
    inner = [inner_sums[0]] + [along_z(inner_sums[d], d) for d in range(1, nz)]

    first_rows, second_rows = pl.pallas_call(
        edges_kernel,
        out_shape=[shaped((HALO, width), jnp.bfloat16)] * 2,
        in_specs=[vmem] * nz,
        out_specs=[vmem] * 2,
        compiler_params=params,
        name="edge_rows",
    )(*edges)

    def swap(rows, start):
        pairs = [(i, i + 1) for i in range(start, devices - 1, 2)]
        return lax.ppermute(rows, every, pairs + [(j, i) for i, j in pairs])

    first, second = swap(first_rows, 0), swap(second_rows, 1)

    coadd, detection = pl.pallas_call(
        functools.partial(detect_kernel, nz),
        out_shape=[shaped((SIDE, width), jnp.float32)] * 2,
        in_specs=[vmem] * (2 * nz + 5),
        out_specs=[vmem] * 2,
        scratch_shapes=[pltpu.VMEM((2 * HALO, width), jnp.bfloat16)],
        compiler_params=params,
        name="coadd_detect",
    )(*edges, *inner, first, second, across, centre, edge)
    return coadd, detection


def solution(mesh):
    ns, nd = mesh.shape["sec"], mesh.shape["dev"]
    nz = math.gcd(nd, 4)
    pn = nd // nz
    cut = Mesh(mesh.devices.reshape(ns, nz, pn), ("sec", "z", "p"))
    every = ("sec", "z", "p")
    placed = (
        P(None, every, None, None),
        P(every, None, None),
        P(None, every, None),
        P(),
        P(None, every, None),
        P(None, every, None),
        P(None, every, None),
        P(every, None),
        P(every, None),
        P(every, None),
        P(),
        P(),
    )
    return jax.shard_map(
        functools.partial(per_device, (nz, pn, ns)),
        mesh=cut,
        in_specs=placed,
        out_specs=(P(every, None), P(every, None)),
        check_vma=False,
    )
```

```python
import functools
import math

import jax
import jax.numpy as jnp
from jax import lax
from jax.experimental import pallas as pl
from jax.experimental.pallas import tpu as pltpu
from jax.sharding import Mesh
from jax.sharding import PartitionSpec as P

SIDE = 128
CAP = 2
PATCH_DEV = 4
HALO = 32
FIELDS = 4
TIED = 2
TAIL = 2
PART = SIDE // 2
VMEM_LIMIT = 48 * 1024 * 1024


def turned(q, pn):
    bits = (pn.bit_length() - 1) // 2
    return ((q >> bits) | (q << bits)) & (pn - 1) if bits else q


def shifted(d, nz):
    return 0 if d == 0 else d % (nz - 1) + 1


def tap_row(tap, count, start, width, reverse):
    lane = lax.broadcasted_iota(jnp.int32, (1, width), 1)
    row = jnp.zeros((1, width), jnp.float32)
    for k in range(count):
        at = start + (count - 1 - k if reverse else k)
        row = jnp.where(lane == at % width, tap(k), row)
    return row


def toeplitz(row, height):
    return pltpu.roll(
        jnp.broadcast_to(row, (height, row.shape[1])), 0, 1, stride=1, stride_axis=0
    )


def store_band(band_ref, tiles):
    blocks = band_ref.shape[0] // SIDE
    for i in range(blocks):
        for j in range(blocks):
            place = (pl.ds(i * SIDE, SIDE), pl.ds(j * SIDE, SIDE))
            if abs(i - j) <= 1:
                first = (j - i + 1) * SIDE
                band_ref[place] = tiles[:, first : first + SIDE]
            else:
                band_ref[place] = jnp.zeros((SIDE, SIDE), band_ref.dtype)


def dot32(left, right):
    return jnp.dot(left, right, preferred_element_type=jnp.float32)


def two_parts(value):
    high = value.astype(jnp.bfloat16)
    return high, (value - high.astype(jnp.float32)).astype(jnp.bfloat16)


def three_parts(value):
    high = value.astype(jnp.bfloat16)
    rest = value - high.astype(jnp.float32)
    mid = rest.astype(jnp.bfloat16)
    return high, mid, (rest - mid.astype(jnp.float32)).astype(jnp.bfloat16)


def warp_kernel(
    split,
    owner_hbm,
    patch_hbm,
    index_hbm,
    table_hbm,
    taps_hbm,
    weights_hbm,
    shift_hbm,
    scale_hbm,
    bias_hbm,
    raw_hbm,
    flat_hbm,
    *rest,
):
    nz, pn, ns = split
    outs, rest = rest[: 2 * ns * pn - 2], rest[2 * ns * pn - 2 :]
    warp_body(
        split,
        (
            owner_hbm,
            patch_hbm,
            index_hbm,
            table_hbm,
            taps_hbm,
            weights_hbm,
            shift_hbm,
            scale_hbm,
            bias_hbm,
            raw_hbm,
            flat_hbm,
        ),
        outs,
        *rest,
    )


def warp_body(
    split,
    inputs,
    outs,
    owner_ref,
    patch_ref,
    index_ref,
    table_ref,
    taps_ref,
    weights_ref,
    shift_ref,
    scale_ref,
    bias_ref,
    raw_ref,
    flat_ref,
    count_ref,
    band_ref,
    left_ref,
    mid_ref,
    slot_rows,
    weight_rows,
    small_sem,
    flat_sem,
    raw_sem,
    out_ref,
    out_sem,
):
    (
        owner_hbm,
        patch_hbm,
        index_hbm,
        table_hbm,
        taps_hbm,
        weights_hbm,
        shift_hbm,
        scale_hbm,
        bias_hbm,
        raw_hbm,
        flat_hbm,
    ) = inputs
    nz, pn, ns = split
    my_sec, my_p, my_z = lax.axis_index("sec"), lax.axis_index("p"), lax.axis_index("z")
    visits, _, rows, cols = raw_ref.shape
    terms, tap_count = taps_ref.shape[1], taps_ref.shape[3]
    half = tap_count // 2
    per_dest = nz * CAP
    data_rows = per_dest * PART
    edge_rows = data_rows + FIELDS * per_dest

    small = [
        pltpu.make_async_copy(src, dst, small_sem.at[i])
        for i, (src, dst) in enumerate(
            (
                (taps_hbm, taps_ref),
                (bias_hbm, bias_ref),
                (owner_hbm, owner_ref),
                (patch_hbm, patch_ref),
                (index_hbm, index_ref),
                (table_hbm, table_ref),
                (weights_hbm, weights_ref),
                (shift_hbm, shift_ref),
                (scale_hbm, scale_ref),
            )
        )
    ]
    for copy in small:
        copy.start()
    flat_copy = pltpu.make_async_copy(flat_hbm, flat_ref, flat_sem)
    raw_copies = [
        pltpu.make_async_copy(raw_hbm.at[v], raw_ref.at[v], raw_sem.at[v]) for v in range(visits)
    ]
    raw_copies[0].start()
    flat_copy.start()
    for copy in raw_copies[1:]:
        copy.start()

    out_ref[...] = jnp.zeros_like(out_ref)
    slot_rows[...] = jnp.full(slot_rows.shape, -1.0, jnp.float32)
    weight_rows[...] = jnp.zeros_like(weight_rows)

    def clear(i, c):
        count_ref[i] = 0
        return c

    lax.fori_loop(0, count_ref.shape[0], clear, 0)
    for copy in small:
        copy.wait()

    def store_hat(ref, length, axis, shift, scale):
        centre = (length - 1) / 2.0
        count = length // SIDE
        for o in range(count):
            out_pos = o * SIDE + lax.broadcasted_iota(
                jnp.int32, (1, SIDE) if axis == 1 else (SIDE, 1), axis
            )
            source = scale * (out_pos.astype(jnp.float32) - centre) + centre + shift
            for i in range(count):
                at = (i, o) if axis == 1 else (o, i)
                place = tuple(pl.ds(k * SIDE, SIDE) for k in at)
                if abs(i - o) <= 1:
                    in_pos = i * SIDE + lax.broadcasted_iota(jnp.int32, (SIDE, SIDE), 1 - axis)
                    near = jnp.maximum(0.0, 1.0 - jnp.abs(in_pos.astype(jnp.float32) - source))
                    ref[place] = near.astype(jnp.bfloat16)
                else:
                    ref[place] = jnp.zeros((SIDE, SIDE), jnp.bfloat16)

    for visit in range(visits):
        for term in range(terms):
            for axis, reverse in ((1, True), (0, False)):
                row = tap_row(
                    lambda k: taps_ref[visit, term, axis, k],
                    tap_count,
                    SIDE - half,
                    3 * SIDE,
                    reverse,
                )
                store_band(
                    band_ref.at[visit, 2 * term + 1 - axis], toeplitz(row, SIDE).astype(jnp.bfloat16)
                )
        for axis, length in ((1, cols), (0, rows)):
            store_hat(
                band_ref.at[visit, 2 * terms + 1 - axis],
                length,
                axis,
                shift_ref[visit, 0, axis],
                scale_ref[visit, 0, axis],
            )

    def windows(length):
        wide = 2 * SIDE
        for at in range(0, length, wide):
            low, high = max(0, at - SIDE), min(length, at + wide + SIDE)
            yield pl.ds(at, min(wide, length - at)), pl.ds(low, high - low)

    def times_band(out, source, band):
        for o, k in windows(cols):
            out[:, o] = dot32(source[:, k], band[k, o]).astype(jnp.bfloat16)

    def band_times(out, band, source):
        for o, k in windows(rows):
            out[o, :] = dot32(band[o, k], source[k, :]).astype(jnp.bfloat16)

    row_blocks, col_blocks = rows // SIDE, cols // SIDE
    for visit in range(visits):
        left, mid = left_ref.at[visit], mid_ref.at[visit]
        bias = jnp.broadcast_to(bias_ref[visit], (SIDE, rows)).T
        raw_copies[visit].wait()
        if visit == 0:
            flat_copy.wait()
        for j in range(cols // SIDE):
            sl = pl.ds(j * SIDE, SIDE)
            left[:, sl] = ((raw_ref[visit, 0, :, sl] - bias) * flat_ref[0, :, sl]).astype(
                jnp.bfloat16
            )

        if terms == 1:
            times_band(mid, left, band_ref.at[visit, 0])
            for o, k in windows(rows):
                part = dot32(band_ref[visit, 1, o, k], mid[k, :])
                left[o, :] = (weights_ref[0, 0, visit] * part).astype(jnp.bfloat16)
        else:
            matched = None
            for term in range(terms):
                times_band(mid, left, band_ref.at[visit, 2 * term])
                part = weights_ref[0, term, visit] * dot32(band_ref[visit, 2 * term + 1], mid[...])
                matched = part if matched is None else matched + part
            left[...] = matched.astype(jnp.bfloat16)
        times_band(mid, left, band_ref.at[visit, 2 * terms])
        band_times(left, band_ref.at[visit, 2 * terms + 1], mid)

    for visit in range(visits):
        for i in range(row_blocks):
            for j in range(col_blocks):
                block = visit * (row_blocks * col_blocks) + i * col_blocks + j
                owner = owner_ref[block]
                rank = count_ref[owner]
                count_ref[owner] = rank + 1
                sec = owner // (nz * pn)
                dev = owner - sec * (nz * pn)
                z = dev // pn
                step = (dev - z * pn) ^ my_p
                step = jnp.where(my_sec == 0, step, turned(step, pn))
                dest = (sec ^ my_sec) * pn + step
                apart = z ^ my_z
                later = jnp.where(apart > 1, apart - 1, apart * (nz - 1))
                at = jnp.where(sec == 0, apart, later) * CAP + rank
                first = pl.multiple_of(at * PART, PART)
                columns = pl.ds(j * SIDE, SIDE)
                for target, source, count in (
                    (first, 0, HALO),
                    (first + HALO, SIDE - HALO, HALO),
                    (first + edge_rows, HALO, SIDE - 2 * HALO),
                ):
                    out_ref[dest, pl.ds(target, count), :] = left_ref[
                        visit, pl.ds(i * SIDE + source, count), columns
                    ]
                line = pl.ds(dest * per_dest + at, 1)
                slot_rows[line, :] = jnp.full((1, SIDE), patch_ref[block].astype(jnp.float32))
                weight_rows[line, :] = jnp.full((1, SIDE), table_ref[index_ref[block]])

    group = out_ref.shape[0]
    copies = []
    for dest in range(group):
        part = pl.ds(dest * per_dest, per_dest)
        fields = jnp.concatenate(
            [slot_rows[part, :]]
            + [w.astype(jnp.float32) for w in three_parts(weight_rows[part, :])],
            axis=0,
        )
        out_ref[dest, pl.ds(data_rows, fields.shape[0]), :] = fields.astype(jnp.bfloat16)
    whole = pl.ds(0, edge_rows + data_rows)
    pieces = [(k, whole if k in (0, pn) else pl.ds(0, edge_rows)) for k in range(group)]
    pieces += [(k, pl.ds(edge_rows, data_rows)) for k in range(group) if k not in (0, pn)]
    for out, (dest, rows_of) in enumerate(pieces):
        copies.append(
            pltpu.make_async_copy(out_ref.at[dest, rows_of], outs[out], out_sem.at[out])
        )
        copies[-1].start()
    for copy in copies:
        copy.wait()


def add_blocks(nz, ins, starts, weight_ref, outs):
    for z in range(nz):
        for place in range(PART // HALO):
            sums = [jnp.zeros((HALO, SIDE), jnp.float32) for _ in range(PATCH_DEV)]
            for g, (ref, start) in enumerate(zip(ins, starts)):
                for r in range(CAP):
                    at = z * CAP + r
                    value = ref[pl.ds(start + at * PART + place * HALO, HALO), :].astype(jnp.float32)
                    for j in range(PATCH_DEV):
                        sums[j] = sums[j] + weight_ref[g, j, pl.ds(at, 1), :] * value
            for j in range(PATCH_DEV):
                row = j * PART + place * HALO
                outs[z][pl.ds(row, HALO), :] = sums[j].astype(jnp.bfloat16)


def edge_sum_kernel(nz, sources, *refs):
    ins, outs, weight_ref = refs[:sources], refs[sources:-1], refs[-1]
    per_dest = nz * CAP
    for g in range(sources):
        fields = ins[g][pl.ds(per_dest * PART, FIELDS * per_dest), :].astype(jnp.float32)
        slot = fields[:per_dest]
        weight = (
            fields[per_dest : 2 * per_dest]
            + fields[2 * per_dest : 3 * per_dest]
            + fields[3 * per_dest :]
        )
        for j in range(PATCH_DEV):
            weight_ref[g, j] = jnp.where(slot == float(j), weight, 0.0)
    add_blocks(nz, ins, [0] * sources, weight_ref, outs)
    for z in range(nz):
        totals = []
        for j in range(PATCH_DEV):
            total = jnp.zeros((1, SIDE), jnp.float32)
            for g in range(sources):
                for r in range(CAP):
                    total = total + weight_ref[g, j, pl.ds(z * CAP + r, 1), :]
            totals.append(total)
        parts = [q.astype(jnp.float32) for q in three_parts(jnp.concatenate(totals, axis=0))]
        parts.append(jnp.zeros((PATCH_DEV, SIDE), jnp.float32))
        outs[z][pl.ds(PATCH_DEV * PART, FIELDS * PATCH_DEV), :] = jnp.concatenate(
            parts, axis=0
        ).astype(jnp.bfloat16)


def inner_sum_kernel(nz, sources, weight_ref, *refs):
    after = nz * CAP * (PART + FIELDS)
    starts = [after, after] + [0] * (sources - 2)
    add_blocks(nz, refs[:sources], starts, weight_ref, refs[sources:])


def totals_of(ins, start):
    total = jnp.zeros((PATCH_DEV, SIDE), jnp.float32)
    for ref in ins:
        extra = ref[pl.ds(start, FIELDS * PATCH_DEV), :].astype(jnp.float32)
        total = total + (
            extra[:PATCH_DEV] + extra[PATCH_DEV : 2 * PATCH_DEV] + extra[2 * PATCH_DEV : 3 * PATCH_DEV]
        )
    return jnp.maximum(total, 1.0)


def average(ins, row, count, total):
    numerator = ins[0][pl.ds(row, count), :].astype(jnp.float32)
    for ref in ins[1:]:
        numerator = numerator + ref[pl.ds(row, count), :].astype(jnp.float32)
    return numerator / total


def edges_kernel(*refs):
    ins, first_ref, second_ref = refs[:-2], refs[-2], refs[-1]
    odd = lax.axis_index("p") % 2
    total = totals_of(ins, 2 * PATCH_DEV * HALO)
    for j in range(PATCH_DEV):
        sl = pl.ds(j * SIDE, SIDE)
        rows = average(ins, 2 * j * HALO, 2 * HALO, total[j : j + 1])
        top, bottom = rows[:HALO], rows[HALO:]
        first_ref[:, sl] = jnp.where(odd == 0, bottom, top).astype(jnp.bfloat16)
        second_ref[:, sl] = jnp.where(odd == 0, top, bottom).astype(jnp.bfloat16)


def detect_kernel(nz, *refs):
    edges, inner = refs[:nz], refs[nz : 2 * nz]
    first_ref, second_ref, across_ref, centre_ref, edge_ref = refs[2 * nz : 2 * nz + 5]
    coadd_ref, out_ref, halo_ref = refs[2 * nz + 5 :]
    odd = lax.axis_index("p") % 2
    halo_ref[pl.ds(pl.multiple_of((1 - odd) * HALO, HALO), HALO)] = first_ref[...]
    halo_ref[pl.ds(pl.multiple_of(odd * HALO, HALO), HALO)] = second_ref[...]
    halo = halo_ref[...]
    total = totals_of(edges, 2 * PATCH_DEV * HALO)
    depth = SIDE - 2 * HALO
    for j in range(PATCH_DEV):
        sl = pl.ds(j * SIDE, SIDE)
        weight = total[j : j + 1]
        coadd_ref[pl.ds(0, HALO), sl] = average(edges, 2 * j * HALO, HALO, weight)
        coadd_ref[pl.ds(HALO, depth), sl] = average(inner, j * depth, depth, weight)
        coadd_ref[pl.ds(SIDE - HALO, HALO), sl] = average(edges, (2 * j + 1) * HALO, HALO, weight)
    main, rest = two_parts(coadd_ref[...])
    along = dot32(centre_ref[0], main) + (
        dot32(centre_ref[0], rest) + dot32(centre_ref[1], main)
    )
    ends = dot32(edge_ref[0], halo) + dot32(edge_ref[1], halo)
    along = jnp.concatenate(
        [along[:HALO] + ends[:HALO], along[HALO : SIDE - HALO], along[SIDE - HALO :] + ends[HALO:]],
        axis=0,
    )
    out_ref[...] = dot_parts(along, across_ref)


def prepare_kernel(taps_ref, *refs):
    own_hbm, across_ref, centre_ref, edge_ref, own_ref, band_ref, own_sem = refs
    own_copy = pltpu.make_async_copy(own_hbm, own_ref, own_sem)
    own_copy.start()
    tap_count = taps_ref.shape[1]
    half = tap_count // 2
    across = tap_row(lambda k: taps_ref[1, k], tap_count, SIDE - half, 3 * SIDE, True)
    store_band(band_ref, toeplitz(across, SIDE))
    across_ref[0], across_ref[1] = two_parts(band_ref[...])
    down = tap_row(lambda k: taps_ref[0, k], tap_count, SIDE - half, 3 * SIDE, False)
    centre_ref[0], centre_ref[1] = two_parts(toeplitz(down, SIDE)[:, SIDE : 2 * SIDE])
    lane = lax.broadcasted_iota(jnp.int32, (2 * HALO, SIDE), 1)
    row = lax.broadcasted_iota(jnp.int32, (2 * HALO, SIDE), 0)
    before = tap_row(lambda k: taps_ref[0, k], tap_count, HALO - half, SIDE, False)
    after = tap_row(lambda k: taps_ref[0, k], tap_count, SIDE - HALO - half, SIDE, False)
    edge = jnp.where(
        (row < HALO) & (lane < HALO),
        toeplitz(before, 2 * HALO),
        jnp.where(
            (row >= HALO) & (lane >= HALO) & (lane < 2 * HALO), toeplitz(after, 2 * HALO), 0.0
        ),
    )
    edge_ref[0], edge_ref[1] = two_parts(edge[:, : 2 * HALO])
    own_copy.wait()


def dot_parts(left, across_ref):
    main, rest = two_parts(left)
    both = dot32(jnp.concatenate([main, rest], axis=0), across_ref[0])
    return both[: left.shape[0]] + (dot32(main, across_ref[1]) + both[left.shape[0] :])


def per_device(
    split,
    raw_pixels,
    flat_field,
    bias_rows,
    psf_taps,
    term_weights,
    warp_shift,
    warp_scale,
    owner_of,
    patch_slot,
    weight_index,
    weight_table,
    detect_taps,
):
    nz, pn, ns = split
    devices = nz * pn * ns
    group = ns * pn
    visits, _, rows, cols = raw_pixels.shape
    blocks = owner_of.shape[0]
    terms = psf_taps.shape[1]
    per_dest = nz * CAP
    inner_rows = per_dest * PART
    edge_rows = inner_rows + FIELDS * per_dest
    width = PATCH_DEV * SIDE
    smem = pl.BlockSpec(memory_space=pltpu.SMEM)
    vmem = pl.BlockSpec(memory_space=pltpu.VMEM)
    hbm = pl.BlockSpec(memory_space=pltpu.HBM)
    params = pltpu.CompilerParams(vmem_limit_bytes=VMEM_LIMIT)

    def shaped(shape, dtype):
        return jax.ShapeDtypeStruct(shape, dtype)

    weights = term_weights.transpose(1, 2, 0)
    send = pl.pallas_call(
        functools.partial(warp_kernel, split),
        out_shape=[
            shaped((edge_rows + (inner_rows if k in (0, pn) else 0), SIDE), jnp.bfloat16)
            for k in range(group)
        ]
        + [shaped((inner_rows, SIDE), jnp.bfloat16)] * (group - 2),
        in_specs=[hbm] * 11,
        out_specs=[hbm] * (2 * group - 2),
        scratch_shapes=[
            pltpu.SMEM((blocks,), jnp.int32),
            pltpu.SMEM((blocks,), jnp.int32),
            pltpu.SMEM((blocks,), jnp.int32),
            pltpu.SMEM(weight_table.shape, jnp.float32),
            pltpu.SMEM(psf_taps.shape, jnp.float32),
            pltpu.SMEM(weights.shape, jnp.float32),
            pltpu.SMEM(warp_shift.shape, jnp.float32),
            pltpu.SMEM(warp_scale.shape, jnp.float32),
            pltpu.VMEM(bias_rows.shape, jnp.float32),
            pltpu.VMEM(raw_pixels.shape, jnp.float32),
            pltpu.VMEM(flat_field.shape, jnp.float32),
            pltpu.SMEM((devices,), jnp.int32),
            pltpu.VMEM((visits, 2 * terms + 2, rows, cols), jnp.bfloat16),
            pltpu.VMEM((visits, rows, cols), jnp.bfloat16),
            pltpu.VMEM((visits, rows, cols), jnp.bfloat16),
            pltpu.VMEM((group * per_dest, SIDE), jnp.float32),
            pltpu.VMEM((group * per_dest, SIDE), jnp.float32),
            pltpu.SemaphoreType.DMA((9,)),
            pltpu.SemaphoreType.DMA,
            pltpu.SemaphoreType.DMA((visits,)),
            pltpu.VMEM((group, edge_rows + inner_rows, SIDE), jnp.bfloat16),
            pltpu.SemaphoreType.DMA((2 * group - 2,)),
        ],
        compiler_params=pltpu.CompilerParams(vmem_limit_bytes=60 * 1024 * 1024),
        name="warp",
    )(
        owner_of.reshape(blocks),
        patch_slot.reshape(blocks),
        weight_index.reshape(blocks),
        weight_table,
        psf_taps,
        weights,
        warp_shift,
        warp_scale,
        bias_rows,
        raw_pixels,
        flat_field,
    )
    def in_plane(part, k):
        pairs = []
        for sec in range(ns):
            for p in range(pn):
                q = k % pn if sec == 0 else turned(k % pn, pn)
                pairs.append((sec * pn + p, (sec ^ (k // pn)) * pn + (p ^ q)))
        return lax.ppermute(part, ("sec", "p"), pairs)

    def along_z(part, d):
        pairs = []
        for i in range(devices):
            apart = d if i < nz * pn else shifted(d, nz)
            pairs.append((i, i ^ (apart * pn)))
        return lax.ppermute(part, every, pairs)

    every = ("sec", "z", "p")
    peers = sorted(range(1, group), key=lambda k: (k != pn, -bin(k % pn).count("1"), k))
    edge_blocks = [in_plane(send[k], k) for k in peers]

    across, centre, edge, own = pl.pallas_call(
        prepare_kernel,
        out_shape=(
            shaped((2, width, width), jnp.bfloat16),
            shaped((2, SIDE, SIDE), jnp.bfloat16),
            shaped((2, 2 * HALO, 2 * HALO), jnp.bfloat16),
            shaped((edge_rows + inner_rows, SIDE), jnp.bfloat16),
        ),
        in_specs=[smem, hbm],
        out_specs=(vmem,) * 4,
        scratch_shapes=[pltpu.VMEM((width, width), jnp.float32), pltpu.SemaphoreType.DMA],
        compiler_params=params,
        cost_estimate=pl.CostEstimate(flops=0, bytes_accessed=8 << 20, transcendentals=0),
        name="matrices",
    )(detect_taps, send[0])

    busy = pl.CostEstimate(flops=0, bytes_accessed=4 << 20, transcendentals=0)
    edge_sums = list(pl.pallas_call(
        functools.partial(edge_sum_kernel, nz, group),
        out_shape=[shaped((PATCH_DEV * (PART + FIELDS), SIDE), jnp.bfloat16)] * nz
        + [shaped((group, PATCH_DEV, per_dest, SIDE), jnp.float32)],
        in_specs=[vmem] * group,
        out_specs=[vmem] * (nz + 1),
        compiler_params=params,
        cost_estimate=busy,
        name="edge_sums",
    )(own, *edge_blocks))
    edges = [edge_sums[0]] + [along_z(edge_sums[d], d) for d in range(1, nz)]
    others = [k for k in range(group) if k not in (0, pn)]
    later = {k: send[group + i] for i, k in enumerate(others)}
    order = [k for k in peers if k != pn]
    held = lax.optimization_barrier(
        (edge_blocks[TIED], across, *(later[k] for k in order[:-TAIL]))
    )
    across = held[1]
    kept = lax.optimization_barrier((*edges[1:], *(later[k] for k in order[-TAIL:])))
    edges[1 : 1 + (nz - 1)], kept = kept[: (nz - 1)], kept[(nz - 1) :]
    inner_blocks = [in_plane(part, k) for part, k in zip((*held[2:], *kept), order)]
    first_rows, second_rows = pl.pallas_call(
        edges_kernel,
        out_shape=[shaped((HALO, width), jnp.bfloat16)] * 2,
        in_specs=[vmem] * nz,
        out_specs=[vmem] * 2,
        compiler_params=params,
        name="edge_rows",
    )(*edges)

    def swap(rows, start):
        pairs = [(i, i + 1) for i in range(start, devices - 1, 2)]
        return lax.ppermute(rows, every, pairs + [(j, i) for i, j in pairs])

    first_rows, second_rows, own = lax.optimization_barrier((first_rows, second_rows, own))
    first, second = swap(first_rows, 0), swap(second_rows, 1)

    inner_sums = pl.pallas_call(
        functools.partial(inner_sum_kernel, nz, group),
        out_shape=[shaped((PATCH_DEV * PART, SIDE), jnp.bfloat16)] * nz,
        in_specs=[vmem] * (group + 1),
        out_specs=[vmem] * nz,
        compiler_params=params,
        cost_estimate=busy,
        name="inner_sums",
    )(edge_sums[nz], own, edge_blocks[0], *inner_blocks)
    inner = [inner_sums[0]] + [along_z(inner_sums[d], d) for d in range(1, nz)]

    coadd, detection = pl.pallas_call(
        functools.partial(detect_kernel, nz),
        out_shape=[shaped((SIDE, width), jnp.float32)] * 2,
        in_specs=[vmem] * (2 * nz + 5),
        out_specs=[vmem] * 2,
        scratch_shapes=[pltpu.VMEM((2 * HALO, width), jnp.bfloat16)],
        compiler_params=params,
        name="coadd_detect",
    )(*edges, *inner, first, second, across, centre, edge)
    return coadd, detection


def solution(mesh):
    ns, nd = mesh.shape["sec"], mesh.shape["dev"]
    nz = math.gcd(nd, 4)
    pn = nd // nz
    cut = Mesh(mesh.devices.reshape(ns, nz, pn), ("sec", "z", "p"))
    every = ("sec", "z", "p")
    placed = (
        P(None, every, None, None),
        P(every, None, None),
        P(None, every, None),
        P(),
        P(None, every, None),
        P(None, every, None),
        P(None, every, None),
        P(every, None),
        P(every, None),
        P(every, None),
        P(),
        P(),
    )
    return jax.shard_map(
        functools.partial(per_device, (nz, pn, ns)),
        mesh=cut,
        in_specs=placed,
        out_specs=(P(every, None), P(every, None)),
        check_vma=False,
    )
```

```python
import functools
import math

import jax
import jax.numpy as jnp
from jax import lax
from jax.experimental import pallas as pl
from jax.experimental.pallas import tpu as pltpu
from jax.sharding import Mesh
from jax.sharding import PartitionSpec as P

SIDE = 128
CAP = 2
PATCH_DEV = 4
HALO = 32
FIELDS = 4
TIED = 2
EARLY = 3
TAIL = 2
PART = SIDE // 2
VMEM_LIMIT = 48 * 1024 * 1024


def turned(q, pn):
    bits = (pn.bit_length() - 1) // 2
    return ((q >> bits) | (q << bits)) & (pn - 1) if bits else q


def shifted(d, nz):
    return 0 if d == 0 else d % (nz - 1) + 1


def tap_row(tap, count, start, width, reverse):
    lane = lax.broadcasted_iota(jnp.int32, (1, width), 1)
    row = jnp.zeros((1, width), jnp.float32)
    for k in range(count):
        at = start + (count - 1 - k if reverse else k)
        row = jnp.where(lane == at % width, tap(k), row)
    return row


def toeplitz(row, height):
    return pltpu.roll(
        jnp.broadcast_to(row, (height, row.shape[1])), 0, 1, stride=1, stride_axis=0
    )


def store_band(band_ref, tiles):
    blocks = band_ref.shape[0] // SIDE
    for i in range(blocks):
        for j in range(blocks):
            place = (pl.ds(i * SIDE, SIDE), pl.ds(j * SIDE, SIDE))
            if abs(i - j) <= 1:
                first = (j - i + 1) * SIDE
                band_ref[place] = tiles[:, first : first + SIDE]
            else:
                band_ref[place] = jnp.zeros((SIDE, SIDE), band_ref.dtype)


def dot32(left, right):
    return jnp.dot(left, right, preferred_element_type=jnp.float32)


def two_parts(value):
    high = value.astype(jnp.bfloat16)
    return high, (value - high.astype(jnp.float32)).astype(jnp.bfloat16)


def three_parts(value):
    high = value.astype(jnp.bfloat16)
    rest = value - high.astype(jnp.float32)
    mid = rest.astype(jnp.bfloat16)
    return high, mid, (rest - mid.astype(jnp.float32)).astype(jnp.bfloat16)


def warp_kernel(
    split,
    owner_hbm,
    patch_hbm,
    index_hbm,
    table_hbm,
    taps_hbm,
    weights_hbm,
    shift_hbm,
    scale_hbm,
    bias_hbm,
    raw_hbm,
    flat_hbm,
    *rest,
):
    nz, pn, ns = split
    outs, rest = rest[: 2 * ns * pn - 2], rest[2 * ns * pn - 2 :]
    warp_body(
        split,
        (
            owner_hbm,
            patch_hbm,
            index_hbm,
            table_hbm,
            taps_hbm,
            weights_hbm,
            shift_hbm,
            scale_hbm,
            bias_hbm,
            raw_hbm,
            flat_hbm,
        ),
        outs,
        *rest,
    )


def warp_body(
    split,
    inputs,
    outs,
    owner_ref,
    patch_ref,
    index_ref,
    table_ref,
    taps_ref,
    weights_ref,
    shift_ref,
    scale_ref,
    bias_ref,
    raw_ref,
    flat_ref,
    count_ref,
    band_ref,
    left_ref,
    mid_ref,
    slot_rows,
    weight_rows,
    small_sem,
    flat_sem,
    raw_sem,
    out_ref,
    out_sem,
):
    (
        owner_hbm,
        patch_hbm,
        index_hbm,
        table_hbm,
        taps_hbm,
        weights_hbm,
        shift_hbm,
        scale_hbm,
        bias_hbm,
        raw_hbm,
        flat_hbm,
    ) = inputs
    nz, pn, ns = split
    my_sec, my_p, my_z = lax.axis_index("sec"), lax.axis_index("p"), lax.axis_index("z")
    visits, _, rows, cols = raw_ref.shape
    terms, tap_count = taps_ref.shape[1], taps_ref.shape[3]
    half = tap_count // 2
    per_dest = nz * CAP
    data_rows = per_dest * PART
    edge_rows = data_rows + FIELDS * per_dest

    small = [
        pltpu.make_async_copy(src, dst, small_sem.at[i])
        for i, (src, dst) in enumerate(
            (
                (taps_hbm, taps_ref),
                (bias_hbm, bias_ref),
                (owner_hbm, owner_ref),
                (patch_hbm, patch_ref),
                (index_hbm, index_ref),
                (table_hbm, table_ref),
                (weights_hbm, weights_ref),
                (shift_hbm, shift_ref),
                (scale_hbm, scale_ref),
            )
        )
    ]
    for copy in small:
        copy.start()
    flat_copy = pltpu.make_async_copy(flat_hbm, flat_ref, flat_sem)
    raw_copies = [
        pltpu.make_async_copy(raw_hbm.at[v], raw_ref.at[v], raw_sem.at[v]) for v in range(visits)
    ]
    raw_copies[0].start()
    flat_copy.start()
    for copy in raw_copies[1:]:
        copy.start()

    out_ref[...] = jnp.zeros_like(out_ref)
    slot_rows[...] = jnp.full(slot_rows.shape, -1.0, jnp.float32)
    weight_rows[...] = jnp.zeros_like(weight_rows)

    def clear(i, c):
        count_ref[i] = 0
        return c

    lax.fori_loop(0, count_ref.shape[0], clear, 0)
    for copy in small:
        copy.wait()

    def store_hat(ref, length, axis, shift, scale):
        centre = (length - 1) / 2.0
        count = length // SIDE
        for o in range(count):
            out_pos = o * SIDE + lax.broadcasted_iota(
                jnp.int32, (1, SIDE) if axis == 1 else (SIDE, 1), axis
            )
            source = scale * (out_pos.astype(jnp.float32) - centre) + centre + shift
            for i in range(count):
                at = (i, o) if axis == 1 else (o, i)
                place = tuple(pl.ds(k * SIDE, SIDE) for k in at)
                if abs(i - o) <= 1:
                    in_pos = i * SIDE + lax.broadcasted_iota(jnp.int32, (SIDE, SIDE), 1 - axis)
                    near = jnp.maximum(0.0, 1.0 - jnp.abs(in_pos.astype(jnp.float32) - source))
                    ref[place] = near.astype(jnp.bfloat16)
                else:
                    ref[place] = jnp.zeros((SIDE, SIDE), jnp.bfloat16)

    for visit in range(visits):
        for term in range(terms):
            for axis, reverse in ((1, True), (0, False)):
                row = tap_row(
                    lambda k: taps_ref[visit, term, axis, k],
                    tap_count,
                    SIDE - half,
                    3 * SIDE,
                    reverse,
                )
                store_band(
                    band_ref.at[visit, 2 * term + 1 - axis], toeplitz(row, SIDE).astype(jnp.bfloat16)
                )
        for axis, length in ((1, cols), (0, rows)):
            store_hat(
                band_ref.at[visit, 2 * terms + 1 - axis],
                length,
                axis,
                shift_ref[visit, 0, axis],
                scale_ref[visit, 0, axis],
            )

    def windows(length):
        wide = 2 * SIDE
        for at in range(0, length, wide):
            low, high = max(0, at - SIDE), min(length, at + wide + SIDE)
            yield pl.ds(at, min(wide, length - at)), pl.ds(low, high - low)

    def times_band(out, source, band):
        for o, k in windows(cols):
            out[:, o] = dot32(source[:, k], band[k, o]).astype(jnp.bfloat16)

    def band_times(out, band, source):
        for o, k in windows(rows):
            out[o, :] = dot32(band[o, k], source[k, :]).astype(jnp.bfloat16)

    row_blocks, col_blocks = rows // SIDE, cols // SIDE
    for visit in range(visits):
        left, mid = left_ref.at[visit], mid_ref.at[visit]
        bias = jnp.broadcast_to(bias_ref[visit], (SIDE, rows)).T
        raw_copies[visit].wait()
        if visit == 0:
            flat_copy.wait()
        for j in range(cols // SIDE):
            sl = pl.ds(j * SIDE, SIDE)
            left[:, sl] = ((raw_ref[visit, 0, :, sl] - bias) * flat_ref[0, :, sl]).astype(
                jnp.bfloat16
            )

        if terms == 1:
            times_band(mid, left, band_ref.at[visit, 0])
            for o, k in windows(rows):
                part = dot32(band_ref[visit, 1, o, k], mid[k, :])
                left[o, :] = (weights_ref[0, 0, visit] * part).astype(jnp.bfloat16)
        else:
            matched = None
            for term in range(terms):
                times_band(mid, left, band_ref.at[visit, 2 * term])
                part = weights_ref[0, term, visit] * dot32(band_ref[visit, 2 * term + 1], mid[...])
                matched = part if matched is None else matched + part
            left[...] = matched.astype(jnp.bfloat16)
        times_band(mid, left, band_ref.at[visit, 2 * terms])
        band_times(left, band_ref.at[visit, 2 * terms + 1], mid)

    for visit in range(visits):
        for i in range(row_blocks):
            for j in range(col_blocks):
                block = visit * (row_blocks * col_blocks) + i * col_blocks + j
                owner = owner_ref[block]
                rank = count_ref[owner]
                count_ref[owner] = rank + 1
                sec = owner // (nz * pn)
                dev = owner - sec * (nz * pn)
                z = dev // pn
                step = (dev - z * pn) ^ my_p
                step = jnp.where(my_sec == 0, step, turned(step, pn))
                dest = (sec ^ my_sec) * pn + step
                apart = z ^ my_z
                later = jnp.where(apart > 1, apart - 1, apart * (nz - 1))
                at = jnp.where(sec == 0, apart, later) * CAP + rank
                first = pl.multiple_of(at * PART, PART)
                columns = pl.ds(j * SIDE, SIDE)
                for target, source, count in (
                    (first, 0, HALO),
                    (first + HALO, SIDE - HALO, HALO),
                    (first + edge_rows, HALO, SIDE - 2 * HALO),
                ):
                    out_ref[dest, pl.ds(target, count), :] = left_ref[
                        visit, pl.ds(i * SIDE + source, count), columns
                    ]
                line = pl.ds(dest * per_dest + at, 1)
                slot_rows[line, :] = jnp.full((1, SIDE), patch_ref[block].astype(jnp.float32))
                weight_rows[line, :] = jnp.full((1, SIDE), table_ref[index_ref[block]])

    group = out_ref.shape[0]
    copies = []
    for dest in range(group):
        part = pl.ds(dest * per_dest, per_dest)
        fields = jnp.concatenate(
            [slot_rows[part, :]]
            + [w.astype(jnp.float32) for w in three_parts(weight_rows[part, :])],
            axis=0,
        )
        out_ref[dest, pl.ds(data_rows, fields.shape[0]), :] = fields.astype(jnp.bfloat16)
    whole = pl.ds(0, edge_rows + data_rows)
    pieces = [(k, whole if k in (0, pn) else pl.ds(0, edge_rows)) for k in range(group)]
    pieces += [(k, pl.ds(edge_rows, data_rows)) for k in range(group) if k not in (0, pn)]
    for out, (dest, rows_of) in enumerate(pieces):
        copies.append(
            pltpu.make_async_copy(out_ref.at[dest, rows_of], outs[out], out_sem.at[out])
        )
        copies[-1].start()
    for copy in copies:
        copy.wait()


def add_blocks(nz, ins, starts, weight_ref, outs):
    for z in range(nz):
        for place in range(PART // HALO):
            sums = [jnp.zeros((HALO, SIDE), jnp.float32) for _ in range(PATCH_DEV)]
            for g, (ref, start) in enumerate(zip(ins, starts)):
                for r in range(CAP):
                    at = z * CAP + r
                    value = ref[pl.ds(start + at * PART + place * HALO, HALO), :].astype(jnp.float32)
                    for j in range(PATCH_DEV):
                        sums[j] = sums[j] + weight_ref[g, j, pl.ds(at, 1), :] * value
            for j in range(PATCH_DEV):
                row = j * PART + place * HALO
                outs[z][pl.ds(row, HALO), :] = sums[j].astype(jnp.bfloat16)


def edge_sum_kernel(nz, sources, *refs):
    ins, outs, weight_ref = refs[:sources], refs[sources:-1], refs[-1]
    per_dest = nz * CAP
    for g in range(sources):
        fields = ins[g][pl.ds(per_dest * PART, FIELDS * per_dest), :].astype(jnp.float32)
        slot = fields[:per_dest]
        weight = (
            fields[per_dest : 2 * per_dest]
            + fields[2 * per_dest : 3 * per_dest]
            + fields[3 * per_dest :]
        )
        for j in range(PATCH_DEV):
            weight_ref[g, j] = jnp.where(slot == float(j), weight, 0.0)
    add_blocks(nz, ins, [0] * sources, weight_ref, outs)
    for z in range(nz):
        totals = []
        for j in range(PATCH_DEV):
            total = jnp.zeros((1, SIDE), jnp.float32)
            for g in range(sources):
                for r in range(CAP):
                    total = total + weight_ref[g, j, pl.ds(z * CAP + r, 1), :]
            totals.append(total)
        parts = [q.astype(jnp.float32) for q in three_parts(jnp.concatenate(totals, axis=0))]
        parts.append(jnp.zeros((PATCH_DEV, SIDE), jnp.float32))
        outs[z][pl.ds(PATCH_DEV * PART, FIELDS * PATCH_DEV), :] = jnp.concatenate(
            parts, axis=0
        ).astype(jnp.bfloat16)


def inner_sum_kernel(nz, sources, weight_ref, *refs):
    after = nz * CAP * (PART + FIELDS)
    starts = [after, after] + [0] * (sources - 2)
    add_blocks(nz, refs[:sources], starts, weight_ref, refs[sources:])


def totals_of(ins, start):
    total = jnp.zeros((PATCH_DEV, SIDE), jnp.float32)
    for ref in ins:
        extra = ref[pl.ds(start, FIELDS * PATCH_DEV), :].astype(jnp.float32)
        total = total + (
            extra[:PATCH_DEV] + extra[PATCH_DEV : 2 * PATCH_DEV] + extra[2 * PATCH_DEV : 3 * PATCH_DEV]
        )
    return jnp.maximum(total, 1.0)


def average(ins, row, count, total):
    numerator = ins[0][pl.ds(row, count), :].astype(jnp.float32)
    for ref in ins[1:]:
        numerator = numerator + ref[pl.ds(row, count), :].astype(jnp.float32)
    return numerator / total


def edges_kernel(*refs):
    ins, first_ref, second_ref = refs[:-2], refs[-2], refs[-1]
    odd = lax.axis_index("p") % 2
    total = totals_of(ins, 2 * PATCH_DEV * HALO)
    for j in range(PATCH_DEV):
        sl = pl.ds(j * SIDE, SIDE)
        rows = average(ins, 2 * j * HALO, 2 * HALO, total[j : j + 1])
        top, bottom = rows[:HALO], rows[HALO:]
        first_ref[:, sl] = jnp.where(odd == 0, bottom, top).astype(jnp.bfloat16)
        second_ref[:, sl] = jnp.where(odd == 0, top, bottom).astype(jnp.bfloat16)


def detect_kernel(nz, *refs):
    edges, inner = refs[:nz], refs[nz : 2 * nz]
    first_ref, second_ref, across_ref, centre_ref, edge_ref = refs[2 * nz : 2 * nz + 5]
    coadd_ref, out_ref, halo_ref = refs[2 * nz + 5 :]
    odd = lax.axis_index("p") % 2
    halo_ref[pl.ds(pl.multiple_of((1 - odd) * HALO, HALO), HALO)] = first_ref[...]
    halo_ref[pl.ds(pl.multiple_of(odd * HALO, HALO), HALO)] = second_ref[...]
    halo = halo_ref[...]
    total = totals_of(edges, 2 * PATCH_DEV * HALO)
    depth = SIDE - 2 * HALO
    for j in range(PATCH_DEV):
        sl = pl.ds(j * SIDE, SIDE)
        weight = total[j : j + 1]
        coadd_ref[pl.ds(0, HALO), sl] = average(edges, 2 * j * HALO, HALO, weight)
        coadd_ref[pl.ds(HALO, depth), sl] = average(inner, j * depth, depth, weight)
        coadd_ref[pl.ds(SIDE - HALO, HALO), sl] = average(edges, (2 * j + 1) * HALO, HALO, weight)
    main, rest = two_parts(coadd_ref[...])
    along = dot32(centre_ref[0], main) + (
        dot32(centre_ref[0], rest) + dot32(centre_ref[1], main)
    )
    ends = dot32(edge_ref[0], halo) + dot32(edge_ref[1], halo)
    along = jnp.concatenate(
        [along[:HALO] + ends[:HALO], along[HALO : SIDE - HALO], along[SIDE - HALO :] + ends[HALO:]],
        axis=0,
    )
    out_ref[...] = dot_parts(along, across_ref)


def prepare_kernel(taps_ref, *refs):
    own_hbm, across_ref, centre_ref, edge_ref, own_ref, band_ref, own_sem = refs
    own_copy = pltpu.make_async_copy(own_hbm, own_ref, own_sem)
    own_copy.start()
    tap_count = taps_ref.shape[1]
    half = tap_count // 2
    across = tap_row(lambda k: taps_ref[1, k], tap_count, SIDE - half, 3 * SIDE, True)
    store_band(band_ref, toeplitz(across, SIDE))
    across_ref[0], across_ref[1] = two_parts(band_ref[...])
    down = tap_row(lambda k: taps_ref[0, k], tap_count, SIDE - half, 3 * SIDE, False)
    centre_ref[0], centre_ref[1] = two_parts(toeplitz(down, SIDE)[:, SIDE : 2 * SIDE])
    lane = lax.broadcasted_iota(jnp.int32, (2 * HALO, SIDE), 1)
    row = lax.broadcasted_iota(jnp.int32, (2 * HALO, SIDE), 0)
    before = tap_row(lambda k: taps_ref[0, k], tap_count, HALO - half, SIDE, False)
    after = tap_row(lambda k: taps_ref[0, k], tap_count, SIDE - HALO - half, SIDE, False)
    edge = jnp.where(
        (row < HALO) & (lane < HALO),
        toeplitz(before, 2 * HALO),
        jnp.where(
            (row >= HALO) & (lane >= HALO) & (lane < 2 * HALO), toeplitz(after, 2 * HALO), 0.0
        ),
    )
    edge_ref[0], edge_ref[1] = two_parts(edge[:, : 2 * HALO])
    own_copy.wait()


def dot_parts(left, across_ref):
    main, rest = two_parts(left)
    both = dot32(jnp.concatenate([main, rest], axis=0), across_ref[0])
    return both[: left.shape[0]] + (dot32(main, across_ref[1]) + both[left.shape[0] :])


def per_device(
    split,
    raw_pixels,
    flat_field,
    bias_rows,
    psf_taps,
    term_weights,
    warp_shift,
    warp_scale,
    owner_of,
    patch_slot,
    weight_index,
    weight_table,
    detect_taps,
):
    nz, pn, ns = split
    devices = nz * pn * ns
    group = ns * pn
    visits, _, rows, cols = raw_pixels.shape
    blocks = owner_of.shape[0]
    terms = psf_taps.shape[1]
    per_dest = nz * CAP
    inner_rows = per_dest * PART
    edge_rows = inner_rows + FIELDS * per_dest
    width = PATCH_DEV * SIDE
    smem = pl.BlockSpec(memory_space=pltpu.SMEM)
    vmem = pl.BlockSpec(memory_space=pltpu.VMEM)
    hbm = pl.BlockSpec(memory_space=pltpu.HBM)
    params = pltpu.CompilerParams(vmem_limit_bytes=VMEM_LIMIT)

    def shaped(shape, dtype):
        return jax.ShapeDtypeStruct(shape, dtype)

    weights = term_weights.transpose(1, 2, 0)
    send = pl.pallas_call(
        functools.partial(warp_kernel, split),
        out_shape=[
            shaped((edge_rows + (inner_rows if k in (0, pn) else 0), SIDE), jnp.bfloat16)
            for k in range(group)
        ]
        + [shaped((inner_rows, SIDE), jnp.bfloat16)] * (group - 2),
        in_specs=[hbm] * 11,
        out_specs=[hbm] * (2 * group - 2),
        scratch_shapes=[
            pltpu.SMEM((blocks,), jnp.int32),
            pltpu.SMEM((blocks,), jnp.int32),
            pltpu.SMEM((blocks,), jnp.int32),
            pltpu.SMEM(weight_table.shape, jnp.float32),
            pltpu.SMEM(psf_taps.shape, jnp.float32),
            pltpu.SMEM(weights.shape, jnp.float32),
            pltpu.SMEM(warp_shift.shape, jnp.float32),
            pltpu.SMEM(warp_scale.shape, jnp.float32),
            pltpu.VMEM(bias_rows.shape, jnp.float32),
            pltpu.VMEM(raw_pixels.shape, jnp.float32),
            pltpu.VMEM(flat_field.shape, jnp.float32),
            pltpu.SMEM((devices,), jnp.int32),
            pltpu.VMEM((visits, 2 * terms + 2, rows, cols), jnp.bfloat16),
            pltpu.VMEM((visits, rows, cols), jnp.bfloat16),
            pltpu.VMEM((visits, rows, cols), jnp.bfloat16),
            pltpu.VMEM((group * per_dest, SIDE), jnp.float32),
            pltpu.VMEM((group * per_dest, SIDE), jnp.float32),
            pltpu.SemaphoreType.DMA((9,)),
            pltpu.SemaphoreType.DMA,
            pltpu.SemaphoreType.DMA((visits,)),
            pltpu.VMEM((group, edge_rows + inner_rows, SIDE), jnp.bfloat16),
            pltpu.SemaphoreType.DMA((2 * group - 2,)),
        ],
        compiler_params=pltpu.CompilerParams(vmem_limit_bytes=60 * 1024 * 1024),
        name="warp",
    )(
        owner_of.reshape(blocks),
        patch_slot.reshape(blocks),
        weight_index.reshape(blocks),
        weight_table,
        psf_taps,
        weights,
        warp_shift,
        warp_scale,
        bias_rows,
        raw_pixels,
        flat_field,
    )
    def in_plane(part, k):
        pairs = []
        for sec in range(ns):
            for p in range(pn):
                q = k % pn if sec == 0 else turned(k % pn, pn)
                pairs.append((sec * pn + p, (sec ^ (k // pn)) * pn + (p ^ q)))
        return lax.ppermute(part, ("sec", "p"), pairs)

    def along_z(part, d):
        pairs = []
        for i in range(devices):
            apart = d if i < nz * pn else shifted(d, nz)
            pairs.append((i, i ^ (apart * pn)))
        return lax.ppermute(part, every, pairs)

    every = ("sec", "z", "p")
    peers = sorted(range(1, group), key=lambda k: (k != pn, -bin(k % pn).count("1"), k))
    edge_blocks = [in_plane(send[k], k) for k in peers]

    across, centre, edge, own = pl.pallas_call(
        prepare_kernel,
        out_shape=(
            shaped((2, width, width), jnp.bfloat16),
            shaped((2, SIDE, SIDE), jnp.bfloat16),
            shaped((2, 2 * HALO, 2 * HALO), jnp.bfloat16),
            shaped((edge_rows + inner_rows, SIDE), jnp.bfloat16),
        ),
        in_specs=[smem, hbm],
        out_specs=(vmem,) * 4,
        scratch_shapes=[pltpu.VMEM((width, width), jnp.float32), pltpu.SemaphoreType.DMA],
        compiler_params=params,
        cost_estimate=pl.CostEstimate(flops=0, bytes_accessed=8 << 20, transcendentals=0),
        name="matrices",
    )(detect_taps, send[0])

    busy = pl.CostEstimate(flops=0, bytes_accessed=4 << 20, transcendentals=0)
    edge_sums = list(pl.pallas_call(
        functools.partial(edge_sum_kernel, nz, group),
        out_shape=[shaped((PATCH_DEV * (PART + FIELDS), SIDE), jnp.bfloat16)] * nz
        + [shaped((group, PATCH_DEV, per_dest, SIDE), jnp.float32)],
        in_specs=[vmem] * group,
        out_specs=[vmem] * (nz + 1),
        compiler_params=params,
        cost_estimate=busy,
        name="edge_sums",
    )(own, *edge_blocks))
    edges = [edge_sums[0]] + [along_z(edge_sums[d], d) for d in range(1, nz)]
    others = [k for k in range(group) if k not in (0, pn)]
    later = {k: send[group + i] for i, k in enumerate(others)}
    order = [k for k in peers if k != pn]
    held = lax.optimization_barrier(
        (edge_blocks[TIED], across, *(later[k] for k in order[:-TAIL]))
    )
    across = held[1]
    kept = lax.optimization_barrier((*edges[1:], *(later[k] for k in order[-TAIL:])))
    edges[1 : 1 + (nz - 1)], kept = kept[: (nz - 1)], kept[(nz - 1) :]
    inner_blocks = [in_plane(part, k) for part, k in zip((*held[2:], *kept), order)]
    held = lax.optimization_barrier((*inner_blocks[:EARLY], *edges))
    inner_blocks[:EARLY], edges = held[:EARLY], list(held[EARLY:])
    first_rows, second_rows = pl.pallas_call(
        edges_kernel,
        out_shape=[shaped((HALO, width), jnp.bfloat16)] * 2,
        in_specs=[vmem] * nz,
        out_specs=[vmem] * 2,
        compiler_params=params,
        name="edge_rows",
    )(*edges)

    def swap(rows, start):
        pairs = [(i, i + 1) for i in range(start, devices - 1, 2)]
        return lax.ppermute(rows, every, pairs + [(j, i) for i, j in pairs])

    first, second = swap(first_rows, 0), swap(second_rows, 1)
    first, second, own = lax.optimization_barrier((first, second, own))

    inner_sums = pl.pallas_call(
        functools.partial(inner_sum_kernel, nz, group),
        out_shape=[shaped((PATCH_DEV * PART, SIDE), jnp.bfloat16)] * nz,
        in_specs=[vmem] * (group + 1),
        out_specs=[vmem] * nz,
        compiler_params=params,
        cost_estimate=busy,
        name="inner_sums",
    )(edge_sums[nz], own, edge_blocks[0], *inner_blocks)
    inner = [inner_sums[0]] + [along_z(inner_sums[d], d) for d in range(1, nz)]

    coadd, detection = pl.pallas_call(
        functools.partial(detect_kernel, nz),
        out_shape=[shaped((SIDE, width), jnp.float32)] * 2,
        in_specs=[vmem] * (2 * nz + 5),
        out_specs=[vmem] * 2,
        scratch_shapes=[pltpu.VMEM((2 * HALO, width), jnp.bfloat16)],
        compiler_params=params,
        name="coadd_detect",
    )(*edges, *inner, first, second, across, centre, edge)
    return coadd, detection


def solution(mesh):
    ns, nd = mesh.shape["sec"], mesh.shape["dev"]
    nz = math.gcd(nd, 4)
    pn = nd // nz
    cut = Mesh(mesh.devices.reshape(ns, nz, pn), ("sec", "z", "p"))
    every = ("sec", "z", "p")
    placed = (
        P(None, every, None, None),
        P(every, None, None),
        P(None, every, None),
        P(),
        P(None, every, None),
        P(None, every, None),
        P(None, every, None),
        P(every, None),
        P(every, None),
        P(every, None),
        P(),
        P(),
    )
    return jax.shard_map(
        functools.partial(per_device, (nz, pn, ns)),
        mesh=cut,
        in_specs=placed,
        out_specs=(P(every, None), P(every, None)),
        check_vma=False,
    )
```

```python
import functools
import math

import jax
import jax.numpy as jnp
from jax import lax
from jax.experimental import pallas as pl
from jax.experimental.pallas import tpu as pltpu
from jax.sharding import Mesh
from jax.sharding import PartitionSpec as P

SIDE = 128
CAP = 2
PATCH_DEV = 4
HALO = 32
FIELDS = 4
TIED = 2
TAIL = 2
PART = SIDE // 2
VMEM_LIMIT = 48 * 1024 * 1024


def turned(q, pn):
    bits = (pn.bit_length() - 1) // 2
    return ((q >> bits) | (q << bits)) & (pn - 1) if bits else q


def shifted(d, nz):
    return 0 if d == 0 else d % (nz - 1) + 1


def tap_row(tap, count, start, width, reverse):
    lane = lax.broadcasted_iota(jnp.int32, (1, width), 1)
    row = jnp.zeros((1, width), jnp.float32)
    for k in range(count):
        at = start + (count - 1 - k if reverse else k)
        row = jnp.where(lane == at % width, tap(k), row)
    return row


def toeplitz(row, height):
    return pltpu.roll(
        jnp.broadcast_to(row, (height, row.shape[1])), 0, 1, stride=1, stride_axis=0
    )


def store_band(band_ref, tiles):
    blocks = band_ref.shape[0] // SIDE
    for i in range(blocks):
        for j in range(blocks):
            place = (pl.ds(i * SIDE, SIDE), pl.ds(j * SIDE, SIDE))
            if abs(i - j) <= 1:
                first = (j - i + 1) * SIDE
                band_ref[place] = tiles[:, first : first + SIDE]
            else:
                band_ref[place] = jnp.zeros((SIDE, SIDE), band_ref.dtype)


def dot32(left, right):
    return jnp.dot(left, right, preferred_element_type=jnp.float32)


def two_parts(value):
    high = value.astype(jnp.bfloat16)
    return high, (value - high.astype(jnp.float32)).astype(jnp.bfloat16)


def three_parts(value):
    high = value.astype(jnp.bfloat16)
    rest = value - high.astype(jnp.float32)
    mid = rest.astype(jnp.bfloat16)
    return high, mid, (rest - mid.astype(jnp.float32)).astype(jnp.bfloat16)


def warp_kernel(
    split,
    owner_hbm,
    patch_hbm,
    index_hbm,
    table_hbm,
    taps_hbm,
    weights_hbm,
    shift_hbm,
    scale_hbm,
    bias_hbm,
    raw_hbm,
    flat_hbm,
    *rest,
):
    nz, pn, ns = split
    outs, rest = rest[: 2 * ns * pn - 2], rest[2 * ns * pn - 2 :]
    warp_body(
        split,
        (
            owner_hbm,
            patch_hbm,
            index_hbm,
            table_hbm,
            taps_hbm,
            weights_hbm,
            shift_hbm,
            scale_hbm,
            bias_hbm,
            raw_hbm,
            flat_hbm,
        ),
        outs,
        *rest,
    )


def warp_body(
    split,
    inputs,
    outs,
    owner_ref,
    patch_ref,
    index_ref,
    table_ref,
    taps_ref,
    weights_ref,
    shift_ref,
    scale_ref,
    bias_ref,
    raw_ref,
    flat_ref,
    count_ref,
    band_ref,
    left_ref,
    mid_ref,
    slot_rows,
    weight_rows,
    small_sem,
    flat_sem,
    raw_sem,
    out_ref,
    out_sem,
):
    (
        owner_hbm,
        patch_hbm,
        index_hbm,
        table_hbm,
        taps_hbm,
        weights_hbm,
        shift_hbm,
        scale_hbm,
        bias_hbm,
        raw_hbm,
        flat_hbm,
    ) = inputs
    nz, pn, ns = split
    my_sec, my_p, my_z = lax.axis_index("sec"), lax.axis_index("p"), lax.axis_index("z")
    visits, _, rows, cols = raw_ref.shape
    terms, tap_count = taps_ref.shape[1], taps_ref.shape[3]
    half = tap_count // 2
    per_dest = nz * CAP
    data_rows = per_dest * PART
    edge_rows = data_rows + FIELDS * per_dest

    small = [
        pltpu.make_async_copy(src, dst, small_sem.at[i])
        for i, (src, dst) in enumerate(
            (
                (taps_hbm, taps_ref),
                (bias_hbm, bias_ref),
                (owner_hbm, owner_ref),
                (patch_hbm, patch_ref),
                (index_hbm, index_ref),
                (table_hbm, table_ref),
                (weights_hbm, weights_ref),
                (shift_hbm, shift_ref),
                (scale_hbm, scale_ref),
            )
        )
    ]
    for copy in small:
        copy.start()
    flat_copy = pltpu.make_async_copy(flat_hbm, flat_ref, flat_sem)
    raw_copies = [
        pltpu.make_async_copy(raw_hbm.at[v], raw_ref.at[v], raw_sem.at[v]) for v in range(visits)
    ]
    raw_copies[0].start()
    flat_copy.start()
    for copy in raw_copies[1:]:
        copy.start()

    out_ref[...] = jnp.zeros_like(out_ref)
    slot_rows[...] = jnp.full(slot_rows.shape, -1.0, jnp.float32)
    weight_rows[...] = jnp.zeros_like(weight_rows)

    def clear(i, c):
        count_ref[i] = 0
        return c

    lax.fori_loop(0, count_ref.shape[0], clear, 0)
    for copy in small:
        copy.wait()

    def store_hat(ref, length, axis, shift, scale):
        centre = (length - 1) / 2.0
        count = length // SIDE
        for o in range(count):
            out_pos = o * SIDE + lax.broadcasted_iota(
                jnp.int32, (1, SIDE) if axis == 1 else (SIDE, 1), axis
            )
            source = scale * (out_pos.astype(jnp.float32) - centre) + centre + shift
            for i in range(count):
                at = (i, o) if axis == 1 else (o, i)
                place = tuple(pl.ds(k * SIDE, SIDE) for k in at)
                if abs(i - o) <= 1:
                    in_pos = i * SIDE + lax.broadcasted_iota(jnp.int32, (SIDE, SIDE), 1 - axis)
                    near = jnp.maximum(0.0, 1.0 - jnp.abs(in_pos.astype(jnp.float32) - source))
                    ref[place] = near.astype(jnp.bfloat16)
                else:
                    ref[place] = jnp.zeros((SIDE, SIDE), jnp.bfloat16)

    for visit in range(visits):
        for term in range(terms):
            for axis, reverse in ((1, True), (0, False)):
                row = tap_row(
                    lambda k: taps_ref[visit, term, axis, k],
                    tap_count,
                    SIDE - half,
                    3 * SIDE,
                    reverse,
                )
                store_band(
                    band_ref.at[visit, 2 * term + 1 - axis], toeplitz(row, SIDE).astype(jnp.bfloat16)
                )
        for axis, length in ((1, cols), (0, rows)):
            store_hat(
                band_ref.at[visit, 2 * terms + 1 - axis],
                length,
                axis,
                shift_ref[visit, 0, axis],
                scale_ref[visit, 0, axis],
            )

    def windows(length):
        wide = 2 * SIDE
        for at in range(0, length, wide):
            low, high = max(0, at - SIDE), min(length, at + wide + SIDE)
            yield pl.ds(at, min(wide, length - at)), pl.ds(low, high - low)

    def times_band(out, source, band):
        for o, k in windows(cols):
            out[:, o] = dot32(source[:, k], band[k, o]).astype(jnp.bfloat16)

    def band_times(out, band, source):
        for o, k in windows(rows):
            out[o, :] = dot32(band[o, k], source[k, :]).astype(jnp.bfloat16)

    row_blocks, col_blocks = rows // SIDE, cols // SIDE
    for visit in range(visits):
        left, mid = left_ref.at[visit], mid_ref.at[visit]
        bias = jnp.broadcast_to(bias_ref[visit], (SIDE, rows)).T
        raw_copies[visit].wait()
        if visit == 0:
            flat_copy.wait()
        for j in range(cols // SIDE):
            sl = pl.ds(j * SIDE, SIDE)
            left[:, sl] = ((raw_ref[visit, 0, :, sl] - bias) * flat_ref[0, :, sl]).astype(
                jnp.bfloat16
            )

        if terms == 1:
            times_band(mid, left, band_ref.at[visit, 0])
            for o, k in windows(rows):
                part = dot32(band_ref[visit, 1, o, k], mid[k, :])
                left[o, :] = (weights_ref[0, 0, visit] * part).astype(jnp.bfloat16)
        else:
            matched = None
            for term in range(terms):
                times_band(mid, left, band_ref.at[visit, 2 * term])
                part = weights_ref[0, term, visit] * dot32(band_ref[visit, 2 * term + 1], mid[...])
                matched = part if matched is None else matched + part
            left[...] = matched.astype(jnp.bfloat16)
        times_band(mid, left, band_ref.at[visit, 2 * terms])
        band_times(left, band_ref.at[visit, 2 * terms + 1], mid)

    for visit in range(visits):
        for i in range(row_blocks):
            for j in range(col_blocks):
                block = visit * (row_blocks * col_blocks) + i * col_blocks + j
                owner = owner_ref[block]
                rank = count_ref[owner]
                count_ref[owner] = rank + 1
                sec = owner // (nz * pn)
                dev = owner - sec * (nz * pn)
                z = dev // pn
                step = (dev - z * pn) ^ my_p
                step = jnp.where(my_sec == 0, step, turned(step, pn))
                dest = (sec ^ my_sec) * pn + step
                apart = z ^ my_z
                later = jnp.where(apart > 1, apart - 1, apart * (nz - 1))
                at = jnp.where(sec == 0, apart, later) * CAP + rank
                first = pl.multiple_of(at * PART, PART)
                columns = pl.ds(j * SIDE, SIDE)
                for target, source, count in (
                    (first, 0, HALO),
                    (first + HALO, SIDE - HALO, HALO),
                    (first + edge_rows, HALO, SIDE - 2 * HALO),
                ):
                    out_ref[dest, pl.ds(target, count), :] = left_ref[
                        visit, pl.ds(i * SIDE + source, count), columns
                    ]
                line = pl.ds(dest * per_dest + at, 1)
                slot_rows[line, :] = jnp.full((1, SIDE), patch_ref[block].astype(jnp.float32))
                weight_rows[line, :] = jnp.full((1, SIDE), table_ref[index_ref[block]])

    group = out_ref.shape[0]
    copies = []
    for dest in range(group):
        part = pl.ds(dest * per_dest, per_dest)
        fields = jnp.concatenate(
            [slot_rows[part, :]]
            + [w.astype(jnp.float32) for w in three_parts(weight_rows[part, :])],
            axis=0,
        )
        out_ref[dest, pl.ds(data_rows, fields.shape[0]), :] = fields.astype(jnp.bfloat16)
    whole = pl.ds(0, edge_rows + data_rows)
    pieces = [(k, whole if k in (0, pn) else pl.ds(0, edge_rows)) for k in range(group)]
    pieces += [(k, pl.ds(edge_rows, data_rows)) for k in range(group) if k not in (0, pn)]
    for out, (dest, rows_of) in enumerate(pieces):
        copies.append(
            pltpu.make_async_copy(out_ref.at[dest, rows_of], outs[out], out_sem.at[out])
        )
        copies[-1].start()
    for copy in copies:
        copy.wait()


def add_blocks(nz, ins, starts, weight_ref, outs):
    for z in range(nz):
        for place in range(PART // HALO):
            sums = [jnp.zeros((HALO, SIDE), jnp.float32) for _ in range(PATCH_DEV)]
            for g, (ref, start) in enumerate(zip(ins, starts)):
                for r in range(CAP):
                    at = z * CAP + r
                    value = ref[pl.ds(start + at * PART + place * HALO, HALO), :].astype(jnp.float32)
                    for j in range(PATCH_DEV):
                        sums[j] = sums[j] + weight_ref[g, j, pl.ds(at, 1), :] * value
            for j in range(PATCH_DEV):
                row = j * PART + place * HALO
                outs[z][pl.ds(row, HALO), :] = sums[j].astype(jnp.bfloat16)


def edge_sum_kernel(nz, sources, *refs):
    ins, outs, weight_ref = refs[:sources], refs[sources:-1], refs[-1]
    per_dest = nz * CAP
    for g in range(sources):
        fields = ins[g][pl.ds(per_dest * PART, FIELDS * per_dest), :].astype(jnp.float32)
        slot = fields[:per_dest]
        weight = (
            fields[per_dest : 2 * per_dest]
            + fields[2 * per_dest : 3 * per_dest]
            + fields[3 * per_dest :]
        )
        for j in range(PATCH_DEV):
            weight_ref[g, j] = jnp.where(slot == float(j), weight, 0.0)
    add_blocks(nz, ins, [0] * sources, weight_ref, outs)
    for z in range(nz):
        totals = []
        for j in range(PATCH_DEV):
            total = jnp.zeros((1, SIDE), jnp.float32)
            for g in range(sources):
                for r in range(CAP):
                    total = total + weight_ref[g, j, pl.ds(z * CAP + r, 1), :]
            totals.append(total)
        parts = [q.astype(jnp.float32) for q in three_parts(jnp.concatenate(totals, axis=0))]
        parts.append(jnp.zeros((PATCH_DEV, SIDE), jnp.float32))
        outs[z][pl.ds(PATCH_DEV * PART, FIELDS * PATCH_DEV), :] = jnp.concatenate(
            parts, axis=0
        ).astype(jnp.bfloat16)


def inner_sum_kernel(nz, sources, weight_ref, *refs):
    after = nz * CAP * (PART + FIELDS)
    starts = [after, after] + [0] * (sources - 2)
    add_blocks(nz, refs[:sources], starts, weight_ref, refs[sources:])


def totals_of(ins, start):
    total = jnp.zeros((PATCH_DEV, SIDE), jnp.float32)
    for ref in ins:
        extra = ref[pl.ds(start, FIELDS * PATCH_DEV), :].astype(jnp.float32)
        total = total + (
            extra[:PATCH_DEV] + extra[PATCH_DEV : 2 * PATCH_DEV] + extra[2 * PATCH_DEV : 3 * PATCH_DEV]
        )
    return jnp.maximum(total, 1.0)


def average(ins, row, count, total):
    numerator = ins[0][pl.ds(row, count), :].astype(jnp.float32)
    for ref in ins[1:]:
        numerator = numerator + ref[pl.ds(row, count), :].astype(jnp.float32)
    return numerator / total


def edges_kernel(*refs):
    ins, first_ref, second_ref = refs[:-2], refs[-2], refs[-1]
    odd = lax.axis_index("p") % 2
    total = totals_of(ins, 2 * PATCH_DEV * HALO)
    for j in range(PATCH_DEV):
        sl = pl.ds(j * SIDE, SIDE)
        rows = average(ins, 2 * j * HALO, 2 * HALO, total[j : j + 1])
        top, bottom = rows[:HALO], rows[HALO:]
        first_ref[:, sl] = jnp.where(odd == 0, bottom, top).astype(jnp.bfloat16)
        second_ref[:, sl] = jnp.where(odd == 0, top, bottom).astype(jnp.bfloat16)


def detect_kernel(nz, *refs):
    edges, inner = refs[:nz], refs[nz : 2 * nz]
    first_ref, second_ref, across_ref, centre_ref, edge_ref = refs[2 * nz : 2 * nz + 5]
    coadd_ref, out_ref, halo_ref = refs[2 * nz + 5 :]
    odd = lax.axis_index("p") % 2
    halo_ref[pl.ds(pl.multiple_of((1 - odd) * HALO, HALO), HALO)] = first_ref[...]
    halo_ref[pl.ds(pl.multiple_of(odd * HALO, HALO), HALO)] = second_ref[...]
    halo = halo_ref[...]
    total = totals_of(edges, 2 * PATCH_DEV * HALO)
    depth = SIDE - 2 * HALO
    for j in range(PATCH_DEV):
        sl = pl.ds(j * SIDE, SIDE)
        weight = total[j : j + 1]
        coadd_ref[pl.ds(0, HALO), sl] = average(edges, 2 * j * HALO, HALO, weight)
        coadd_ref[pl.ds(HALO, depth), sl] = average(inner, j * depth, depth, weight)
        coadd_ref[pl.ds(SIDE - HALO, HALO), sl] = average(edges, (2 * j + 1) * HALO, HALO, weight)
    main, rest = two_parts(coadd_ref[...])
    along = dot32(centre_ref[0], main) + (
        dot32(centre_ref[0], rest) + dot32(centre_ref[1], main)
    )
    ends = dot32(edge_ref[0], halo) + dot32(edge_ref[1], halo)
    along = jnp.concatenate(
        [along[:HALO] + ends[:HALO], along[HALO : SIDE - HALO], along[SIDE - HALO :] + ends[HALO:]],
        axis=0,
    )
    out_ref[...] = dot_parts(along, across_ref)


def prepare_kernel(taps_ref, *refs):
    own_hbm, across_ref, centre_ref, edge_ref, own_ref, band_ref, own_sem = refs
    own_copy = pltpu.make_async_copy(own_hbm, own_ref, own_sem)
    own_copy.start()
    tap_count = taps_ref.shape[1]
    half = tap_count // 2
    across = tap_row(lambda k: taps_ref[1, k], tap_count, SIDE - half, 3 * SIDE, True)
    store_band(band_ref, toeplitz(across, SIDE))
    across_ref[0], across_ref[1] = two_parts(band_ref[...])
    down = tap_row(lambda k: taps_ref[0, k], tap_count, SIDE - half, 3 * SIDE, False)
    centre_ref[0], centre_ref[1] = two_parts(toeplitz(down, SIDE)[:, SIDE : 2 * SIDE])
    lane = lax.broadcasted_iota(jnp.int32, (2 * HALO, SIDE), 1)
    row = lax.broadcasted_iota(jnp.int32, (2 * HALO, SIDE), 0)
    before = tap_row(lambda k: taps_ref[0, k], tap_count, HALO - half, SIDE, False)
    after = tap_row(lambda k: taps_ref[0, k], tap_count, SIDE - HALO - half, SIDE, False)
    edge = jnp.where(
        (row < HALO) & (lane < HALO),
        toeplitz(before, 2 * HALO),
        jnp.where(
            (row >= HALO) & (lane >= HALO) & (lane < 2 * HALO), toeplitz(after, 2 * HALO), 0.0
        ),
    )
    edge_ref[0], edge_ref[1] = two_parts(edge[:, : 2 * HALO])
    own_copy.wait()


def dot_parts(left, across_ref):
    main, rest = two_parts(left)
    both = dot32(jnp.concatenate([main, rest], axis=0), across_ref[0])
    return both[: left.shape[0]] + (dot32(main, across_ref[1]) + both[left.shape[0] :])


def per_device(
    split,
    raw_pixels,
    flat_field,
    bias_rows,
    psf_taps,
    term_weights,
    warp_shift,
    warp_scale,
    owner_of,
    patch_slot,
    weight_index,
    weight_table,
    detect_taps,
):
    nz, pn, ns = split
    devices = nz * pn * ns
    group = ns * pn
    visits, _, rows, cols = raw_pixels.shape
    blocks = owner_of.shape[0]
    terms = psf_taps.shape[1]
    per_dest = nz * CAP
    inner_rows = per_dest * PART
    edge_rows = inner_rows + FIELDS * per_dest
    width = PATCH_DEV * SIDE
    smem = pl.BlockSpec(memory_space=pltpu.SMEM)
    vmem = pl.BlockSpec(memory_space=pltpu.VMEM)
    hbm = pl.BlockSpec(memory_space=pltpu.HBM)
    params = pltpu.CompilerParams(vmem_limit_bytes=VMEM_LIMIT)

    def shaped(shape, dtype):
        return jax.ShapeDtypeStruct(shape, dtype)

    weights = term_weights.transpose(1, 2, 0)
    send = pl.pallas_call(
        functools.partial(warp_kernel, split),
        out_shape=[
            shaped((edge_rows + (inner_rows if k in (0, pn) else 0), SIDE), jnp.bfloat16)
            for k in range(group)
        ]
        + [shaped((inner_rows, SIDE), jnp.bfloat16)] * (group - 2),
        in_specs=[hbm] * 11,
        out_specs=[hbm] * (2 * group - 2),
        scratch_shapes=[
            pltpu.SMEM((blocks,), jnp.int32),
            pltpu.SMEM((blocks,), jnp.int32),
            pltpu.SMEM((blocks,), jnp.int32),
            pltpu.SMEM(weight_table.shape, jnp.float32),
            pltpu.SMEM(psf_taps.shape, jnp.float32),
            pltpu.SMEM(weights.shape, jnp.float32),
            pltpu.SMEM(warp_shift.shape, jnp.float32),
            pltpu.SMEM(warp_scale.shape, jnp.float32),
            pltpu.VMEM(bias_rows.shape, jnp.float32),
            pltpu.VMEM(raw_pixels.shape, jnp.float32),
            pltpu.VMEM(flat_field.shape, jnp.float32),
            pltpu.SMEM((devices,), jnp.int32),
            pltpu.VMEM((visits, 2 * terms + 2, rows, cols), jnp.bfloat16),
            pltpu.VMEM((visits, rows, cols), jnp.bfloat16),
            pltpu.VMEM((visits, rows, cols), jnp.bfloat16),
            pltpu.VMEM((group * per_dest, SIDE), jnp.float32),
            pltpu.VMEM((group * per_dest, SIDE), jnp.float32),
            pltpu.SemaphoreType.DMA((9,)),
            pltpu.SemaphoreType.DMA,
            pltpu.SemaphoreType.DMA((visits,)),
            pltpu.VMEM((group, edge_rows + inner_rows, SIDE), jnp.bfloat16),
            pltpu.SemaphoreType.DMA((2 * group - 2,)),
        ],
        compiler_params=pltpu.CompilerParams(vmem_limit_bytes=60 * 1024 * 1024),
        name="warp",
    )(
        owner_of.reshape(blocks),
        patch_slot.reshape(blocks),
        weight_index.reshape(blocks),
        weight_table,
        psf_taps,
        weights,
        warp_shift,
        warp_scale,
        bias_rows,
        raw_pixels,
        flat_field,
    )
    def in_plane(part, k):
        pairs = []
        for sec in range(ns):
            for p in range(pn):
                q = k % pn if sec == 0 else turned(k % pn, pn)
                pairs.append((sec * pn + p, (sec ^ (k // pn)) * pn + (p ^ q)))
        return lax.ppermute(part, ("sec", "p"), pairs)

    def along_z(part, d):
        pairs = []
        for i in range(devices):
            apart = d if i < nz * pn else shifted(d, nz)
            pairs.append((i, i ^ (apart * pn)))
        return lax.ppermute(part, every, pairs)

    every = ("sec", "z", "p")
    peers = sorted(range(1, group), key=lambda k: (k != pn, -bin(k % pn).count("1"), k))
    edge_blocks = [in_plane(send[k], k) for k in peers]

    across, centre, edge, own = pl.pallas_call(
        prepare_kernel,
        out_shape=(
            shaped((2, width, width), jnp.bfloat16),
            shaped((2, SIDE, SIDE), jnp.bfloat16),
            shaped((2, 2 * HALO, 2 * HALO), jnp.bfloat16),
            shaped((edge_rows + inner_rows, SIDE), jnp.bfloat16),
        ),
        in_specs=[smem, hbm],
        out_specs=(vmem,) * 4,
        scratch_shapes=[pltpu.VMEM((width, width), jnp.float32), pltpu.SemaphoreType.DMA],
        compiler_params=params,
        cost_estimate=pl.CostEstimate(flops=0, bytes_accessed=8 << 20, transcendentals=0),
        name="matrices",
    )(detect_taps, send[0])

    busy = pl.CostEstimate(flops=0, bytes_accessed=4 << 20, transcendentals=0)
    edge_sums = list(pl.pallas_call(
        functools.partial(edge_sum_kernel, nz, group),
        out_shape=[shaped((PATCH_DEV * (PART + FIELDS), SIDE), jnp.bfloat16)] * nz
        + [shaped((group, PATCH_DEV, per_dest, SIDE), jnp.float32)],
        in_specs=[vmem] * group,
        out_specs=[vmem] * (nz + 1),
        compiler_params=params,
        cost_estimate=busy,
        name="edge_sums",
    )(own, *edge_blocks))
    edges = [edge_sums[0]] + [along_z(edge_sums[d], d) for d in range(1, nz)]
    others = [k for k in range(group) if k not in (0, pn)]
    later = {k: send[group + i] for i, k in enumerate(others)}
    order = [k for k in peers if k != pn]
    held = lax.optimization_barrier(
        (edge_blocks[0], edge_blocks[TIED], across, *(later[k] for k in order[:-TAIL]))
    )
    edge_blocks[0], edge_blocks[TIED], across = held[:3]
    kept = lax.optimization_barrier((*edges[1:], *(later[k] for k in order[-TAIL:])))
    edges[1 : 1 + (nz - 1)], kept = kept[: (nz - 1)], kept[(nz - 1) :]
    inner_blocks = [in_plane(part, k) for part, k in zip((*held[3:], *kept), order)]
    first_rows, second_rows = pl.pallas_call(
        edges_kernel,
        out_shape=[shaped((HALO, width), jnp.bfloat16)] * 2,
        in_specs=[vmem] * nz,
        out_specs=[vmem] * 2,
        compiler_params=params,
        name="edge_rows",
    )(*edges)

    def swap(rows, start):
        pairs = [(i, i + 1) for i in range(start, devices - 1, 2)]
        return lax.ppermute(rows, every, pairs + [(j, i) for i, j in pairs])

    first_rows, second_rows, own = lax.optimization_barrier((first_rows, second_rows, own))
    first, second = swap(first_rows, 0), swap(second_rows, 1)

    inner_sums = pl.pallas_call(
        functools.partial(inner_sum_kernel, nz, group),
        out_shape=[shaped((PATCH_DEV * PART, SIDE), jnp.bfloat16)] * nz,
        in_specs=[vmem] * (group + 1),
        out_specs=[vmem] * nz,
        compiler_params=params,
        cost_estimate=busy,
        name="inner_sums",
    )(edge_sums[nz], own, edge_blocks[0], *inner_blocks)
    inner = [inner_sums[0]] + [along_z(inner_sums[d], d) for d in range(1, nz)]

    coadd, detection = pl.pallas_call(
        functools.partial(detect_kernel, nz),
        out_shape=[shaped((SIDE, width), jnp.float32)] * 2,
        in_specs=[vmem] * (2 * nz + 5),
        out_specs=[vmem] * 2,
        scratch_shapes=[pltpu.VMEM((2 * HALO, width), jnp.bfloat16)],
        compiler_params=params,
        name="coadd_detect",
    )(*edges, *inner, first, second, across, centre, edge)
    return coadd, detection


def solution(mesh):
    ns, nd = mesh.shape["sec"], mesh.shape["dev"]
    nz = math.gcd(nd, 4)
    pn = nd // nz
    cut = Mesh(mesh.devices.reshape(ns, nz, pn), ("sec", "z", "p"))
    every = ("sec", "z", "p")
    placed = (
        P(None, every, None, None),
        P(every, None, None),
        P(None, every, None),
        P(),
        P(None, every, None),
        P(None, every, None),
        P(None, every, None),
        P(every, None),
        P(every, None),
        P(every, None),
        P(),
        P(),
    )
    return jax.shard_map(
        functools.partial(per_device, (nz, pn, ns)),
        mesh=cut,
        in_specs=placed,
        out_specs=(P(every, None), P(every, None)),
        check_vma=False,
    )
```

```python
import functools
import math

import jax
import jax.numpy as jnp
from jax import lax
from jax.experimental import pallas as pl
from jax.experimental.pallas import tpu as pltpu
from jax.sharding import Mesh
from jax.sharding import PartitionSpec as P

SIDE = 128
CAP = 2
PATCH_DEV = 4
HALO = 32
FIELDS = 4
TIED = 2
TAIL = 2
PART = SIDE // 2
VMEM_LIMIT = 48 * 1024 * 1024


def turned(q, pn):
    bits = (pn.bit_length() - 1) // 2
    return ((q >> bits) | (q << bits)) & (pn - 1) if bits else q


def shifted(d, nz):
    return 0 if d == 0 else d % (nz - 1) + 1


def tap_row(tap, count, start, width, reverse):
    lane = lax.broadcasted_iota(jnp.int32, (1, width), 1)
    row = jnp.zeros((1, width), jnp.float32)
    for k in range(count):
        at = start + (count - 1 - k if reverse else k)
        row = jnp.where(lane == at % width, tap(k), row)
    return row


def toeplitz(row, height):
    return pltpu.roll(
        jnp.broadcast_to(row, (height, row.shape[1])), 0, 1, stride=1, stride_axis=0
    )


def store_band(band_ref, tiles):
    blocks = band_ref.shape[0] // SIDE
    for i in range(blocks):
        for j in range(blocks):
            place = (pl.ds(i * SIDE, SIDE), pl.ds(j * SIDE, SIDE))
            if abs(i - j) <= 1:
                first = (j - i + 1) * SIDE
                band_ref[place] = tiles[:, first : first + SIDE]
            else:
                band_ref[place] = jnp.zeros((SIDE, SIDE), band_ref.dtype)


def dot32(left, right):
    return jnp.dot(left, right, preferred_element_type=jnp.float32)


def two_parts(value):
    high = value.astype(jnp.bfloat16)
    return high, (value - high.astype(jnp.float32)).astype(jnp.bfloat16)


def three_parts(value):
    high = value.astype(jnp.bfloat16)
    rest = value - high.astype(jnp.float32)
    mid = rest.astype(jnp.bfloat16)
    return high, mid, (rest - mid.astype(jnp.float32)).astype(jnp.bfloat16)


def warp_kernel(
    split,
    owner_hbm,
    patch_hbm,
    index_hbm,
    table_hbm,
    taps_hbm,
    weights_hbm,
    shift_hbm,
    scale_hbm,
    bias_hbm,
    raw_hbm,
    flat_hbm,
    *rest,
):
    nz, pn, ns = split
    outs, rest = rest[: 2 * ns * pn - 2], rest[2 * ns * pn - 2 :]
    warp_body(
        split,
        (
            owner_hbm,
            patch_hbm,
            index_hbm,
            table_hbm,
            taps_hbm,
            weights_hbm,
            shift_hbm,
            scale_hbm,
            bias_hbm,
            raw_hbm,
            flat_hbm,
        ),
        outs,
        *rest,
    )


def warp_body(
    split,
    inputs,
    outs,
    owner_ref,
    patch_ref,
    index_ref,
    table_ref,
    taps_ref,
    weights_ref,
    shift_ref,
    scale_ref,
    bias_ref,
    raw_ref,
    flat_ref,
    count_ref,
    band_ref,
    left_ref,
    mid_ref,
    slot_rows,
    weight_rows,
    small_sem,
    flat_sem,
    raw_sem,
    out_ref,
    out_sem,
):
    (
        owner_hbm,
        patch_hbm,
        index_hbm,
        table_hbm,
        taps_hbm,
        weights_hbm,
        shift_hbm,
        scale_hbm,
        bias_hbm,
        raw_hbm,
        flat_hbm,
    ) = inputs
    nz, pn, ns = split
    my_sec, my_p, my_z = lax.axis_index("sec"), lax.axis_index("p"), lax.axis_index("z")
    visits, _, rows, cols = raw_ref.shape
    terms, tap_count = taps_ref.shape[1], taps_ref.shape[3]
    half = tap_count // 2
    per_dest = nz * CAP
    data_rows = per_dest * PART
    edge_rows = data_rows + FIELDS * per_dest

    small = [
        pltpu.make_async_copy(src, dst, small_sem.at[i])
        for i, (src, dst) in enumerate(
            (
                (taps_hbm, taps_ref),
                (bias_hbm, bias_ref),
                (owner_hbm, owner_ref),
                (patch_hbm, patch_ref),
                (index_hbm, index_ref),
                (table_hbm, table_ref),
                (weights_hbm, weights_ref),
                (shift_hbm, shift_ref),
                (scale_hbm, scale_ref),
            )
        )
    ]
    for copy in small:
        copy.start()
    flat_copy = pltpu.make_async_copy(flat_hbm, flat_ref, flat_sem)
    raw_copies = [
        pltpu.make_async_copy(raw_hbm.at[v], raw_ref.at[v], raw_sem.at[v]) for v in range(visits)
    ]
    raw_copies[0].start()
    flat_copy.start()
    for copy in raw_copies[1:]:
        copy.start()

    out_ref[...] = jnp.zeros_like(out_ref)
    slot_rows[...] = jnp.full(slot_rows.shape, -1.0, jnp.float32)
    weight_rows[...] = jnp.zeros_like(weight_rows)

    def clear(i, c):
        count_ref[i] = 0
        return c

    lax.fori_loop(0, count_ref.shape[0], clear, 0)
    for copy in small:
        copy.wait()

    def store_hat(ref, length, axis, shift, scale):
        centre = (length - 1) / 2.0
        count = length // SIDE
        for o in range(count):
            out_pos = o * SIDE + lax.broadcasted_iota(
                jnp.int32, (1, SIDE) if axis == 1 else (SIDE, 1), axis
            )
            source = scale * (out_pos.astype(jnp.float32) - centre) + centre + shift
            for i in range(count):
                at = (i, o) if axis == 1 else (o, i)
                place = tuple(pl.ds(k * SIDE, SIDE) for k in at)
                if abs(i - o) <= 1:
                    in_pos = i * SIDE + lax.broadcasted_iota(jnp.int32, (SIDE, SIDE), 1 - axis)
                    near = jnp.maximum(0.0, 1.0 - jnp.abs(in_pos.astype(jnp.float32) - source))
                    ref[place] = near.astype(jnp.bfloat16)
                else:
                    ref[place] = jnp.zeros((SIDE, SIDE), jnp.bfloat16)

    for visit in range(visits):
        for term in range(terms):
            for axis, reverse in ((1, True), (0, False)):
                row = tap_row(
                    lambda k: taps_ref[visit, term, axis, k],
                    tap_count,
                    SIDE - half,
                    3 * SIDE,
                    reverse,
                )
                store_band(
                    band_ref.at[visit, 2 * term + 1 - axis], toeplitz(row, SIDE).astype(jnp.bfloat16)
                )
        for axis, length in ((1, cols), (0, rows)):
            store_hat(
                band_ref.at[visit, 2 * terms + 1 - axis],
                length,
                axis,
                shift_ref[visit, 0, axis],
                scale_ref[visit, 0, axis],
            )

    def windows(length):
        wide = 2 * SIDE
        for at in range(0, length, wide):
            low, high = max(0, at - SIDE), min(length, at + wide + SIDE)
            yield pl.ds(at, min(wide, length - at)), pl.ds(low, high - low)

    def times_band(out, source, band):
        for o, k in windows(cols):
            out[:, o] = dot32(source[:, k], band[k, o]).astype(jnp.bfloat16)

    def band_times(out, band, source):
        for o, k in windows(rows):
            out[o, :] = dot32(band[o, k], source[k, :]).astype(jnp.bfloat16)

    row_blocks, col_blocks = rows // SIDE, cols // SIDE
    for visit in range(visits):
        left, mid = left_ref.at[visit], mid_ref.at[visit]
        bias = jnp.broadcast_to(bias_ref[visit], (SIDE, rows)).T
        raw_copies[visit].wait()
        if visit == 0:
            flat_copy.wait()
        for j in range(cols // SIDE):
            sl = pl.ds(j * SIDE, SIDE)
            left[:, sl] = ((raw_ref[visit, 0, :, sl] - bias) * flat_ref[0, :, sl]).astype(
                jnp.bfloat16
            )

        if terms == 1:
            times_band(mid, left, band_ref.at[visit, 0])
            for o, k in windows(rows):
                part = dot32(band_ref[visit, 1, o, k], mid[k, :])
                left[o, :] = (weights_ref[0, 0, visit] * part).astype(jnp.bfloat16)
        else:
            matched = None
            for term in range(terms):
                times_band(mid, left, band_ref.at[visit, 2 * term])
                part = weights_ref[0, term, visit] * dot32(band_ref[visit, 2 * term + 1], mid[...])
                matched = part if matched is None else matched + part
            left[...] = matched.astype(jnp.bfloat16)
        times_band(mid, left, band_ref.at[visit, 2 * terms])
        band_times(left, band_ref.at[visit, 2 * terms + 1], mid)

    for visit in range(visits):
        for i in range(row_blocks):
            for j in range(col_blocks):
                block = visit * (row_blocks * col_blocks) + i * col_blocks + j
                owner = owner_ref[block]
                rank = count_ref[owner]
                count_ref[owner] = rank + 1
                sec = owner // (nz * pn)
                dev = owner - sec * (nz * pn)
                z = dev // pn
                step = (dev - z * pn) ^ my_p
                step = jnp.where(my_sec == 0, step, turned(step, pn))
                dest = (sec ^ my_sec) * pn + step
                apart = z ^ my_z
                later = jnp.where(apart > 1, apart - 1, apart * (nz - 1))
                at = jnp.where(sec == 0, apart, later) * CAP + rank
                first = pl.multiple_of(at * PART, PART)
                columns = pl.ds(j * SIDE, SIDE)
                for target, source, count in (
                    (first, 0, HALO),
                    (first + HALO, SIDE - HALO, HALO),
                    (first + edge_rows, HALO, SIDE - 2 * HALO),
                ):
                    out_ref[dest, pl.ds(target, count), :] = left_ref[
                        visit, pl.ds(i * SIDE + source, count), columns
                    ]
                line = pl.ds(dest * per_dest + at, 1)
                slot_rows[line, :] = jnp.full((1, SIDE), patch_ref[block].astype(jnp.float32))
                weight_rows[line, :] = jnp.full((1, SIDE), table_ref[index_ref[block]])

    group = out_ref.shape[0]
    copies = []
    for dest in range(group):
        part = pl.ds(dest * per_dest, per_dest)
        fields = jnp.concatenate(
            [slot_rows[part, :]]
            + [w.astype(jnp.float32) for w in three_parts(weight_rows[part, :])],
            axis=0,
        )
        out_ref[dest, pl.ds(data_rows, fields.shape[0]), :] = fields.astype(jnp.bfloat16)
    whole = pl.ds(0, edge_rows + data_rows)
    pieces = [(k, whole if k in (0, pn) else pl.ds(0, edge_rows)) for k in range(group)]
    pieces += [(k, pl.ds(edge_rows, data_rows)) for k in range(group) if k not in (0, pn)]
    for out, (dest, rows_of) in enumerate(pieces):
        copies.append(
            pltpu.make_async_copy(out_ref.at[dest, rows_of], outs[out], out_sem.at[out])
        )
        copies[-1].start()
    for copy in copies:
        copy.wait()


def add_blocks(nz, ins, starts, weight_ref, outs):
    for z in range(nz):
        for place in range(PART // HALO):
            sums = [jnp.zeros((HALO, SIDE), jnp.float32) for _ in range(PATCH_DEV)]
            for g, (ref, start) in enumerate(zip(ins, starts)):
                for r in range(CAP):
                    at = z * CAP + r
                    value = ref[pl.ds(start + at * PART + place * HALO, HALO), :].astype(jnp.float32)
                    for j in range(PATCH_DEV):
                        sums[j] = sums[j] + weight_ref[g, j, pl.ds(at, 1), :] * value
            for j in range(PATCH_DEV):
                row = j * PART + place * HALO
                outs[z][pl.ds(row, HALO), :] = sums[j].astype(jnp.bfloat16)


def edge_sum_kernel(nz, sources, *refs):
    ins, outs, weight_ref = refs[:sources], refs[sources:-1], refs[-1]
    per_dest = nz * CAP
    for g in range(sources):
        fields = ins[g][pl.ds(per_dest * PART, FIELDS * per_dest), :].astype(jnp.float32)
        slot = fields[:per_dest]
        weight = (
            fields[per_dest : 2 * per_dest]
            + fields[2 * per_dest : 3 * per_dest]
            + fields[3 * per_dest :]
        )
        for j in range(PATCH_DEV):
            weight_ref[g, j] = jnp.where(slot == float(j), weight, 0.0)
    add_blocks(nz, ins, [0] * sources, weight_ref, outs)
    for z in range(nz):
        totals = []
        for j in range(PATCH_DEV):
            total = jnp.zeros((1, SIDE), jnp.float32)
            for g in range(sources):
                for r in range(CAP):
                    total = total + weight_ref[g, j, pl.ds(z * CAP + r, 1), :]
            totals.append(total)
        parts = [q.astype(jnp.float32) for q in three_parts(jnp.concatenate(totals, axis=0))]
        parts.append(jnp.zeros((PATCH_DEV, SIDE), jnp.float32))
        outs[z][pl.ds(PATCH_DEV * PART, FIELDS * PATCH_DEV), :] = jnp.concatenate(
            parts, axis=0
        ).astype(jnp.bfloat16)


def inner_sum_kernel(nz, sources, weight_ref, *refs):
    after = nz * CAP * (PART + FIELDS)
    starts = [after, after] + [0] * (sources - 2)
    add_blocks(nz, refs[:sources], starts, weight_ref, refs[sources:])


def totals_of(ins, start):
    total = jnp.zeros((PATCH_DEV, SIDE), jnp.float32)
    for ref in ins:
        extra = ref[pl.ds(start, FIELDS * PATCH_DEV), :].astype(jnp.float32)
        total = total + (
            extra[:PATCH_DEV] + extra[PATCH_DEV : 2 * PATCH_DEV] + extra[2 * PATCH_DEV : 3 * PATCH_DEV]
        )
    return jnp.maximum(total, 1.0)


def average(ins, row, count, total):
    numerator = ins[0][pl.ds(row, count), :].astype(jnp.float32)
    for ref in ins[1:]:
        numerator = numerator + ref[pl.ds(row, count), :].astype(jnp.float32)
    return numerator / total


def edges_kernel(*refs):
    ins, first_ref, second_ref = refs[:-2], refs[-2], refs[-1]
    odd = lax.axis_index("p") % 2
    total = totals_of(ins, 2 * PATCH_DEV * HALO)
    for j in range(PATCH_DEV):
        sl = pl.ds(j * SIDE, SIDE)
        rows = average(ins, 2 * j * HALO, 2 * HALO, total[j : j + 1])
        top, bottom = rows[:HALO], rows[HALO:]
        first_ref[:, sl] = jnp.where(odd == 0, bottom, top).astype(jnp.bfloat16)
        second_ref[:, sl] = jnp.where(odd == 0, top, bottom).astype(jnp.bfloat16)


def detect_kernel(nz, *refs):
    edges, inner = refs[:nz], refs[nz : 2 * nz]
    second_ref, first_ref, across_ref, centre_ref, edge_ref = refs[2 * nz : 2 * nz + 5]
    coadd_ref, out_ref, halo_ref = refs[2 * nz + 5 :]
    odd = lax.axis_index("p") % 2
    halo_ref[pl.ds(pl.multiple_of((1 - odd) * HALO, HALO), HALO)] = first_ref[...]
    halo_ref[pl.ds(pl.multiple_of(odd * HALO, HALO), HALO)] = second_ref[...]
    halo = halo_ref[...]
    total = totals_of(edges, 2 * PATCH_DEV * HALO)
    depth = SIDE - 2 * HALO
    for j in range(PATCH_DEV):
        sl = pl.ds(j * SIDE, SIDE)
        weight = total[j : j + 1]
        coadd_ref[pl.ds(0, HALO), sl] = average(edges, 2 * j * HALO, HALO, weight)
        coadd_ref[pl.ds(HALO, depth), sl] = average(inner, j * depth, depth, weight)
        coadd_ref[pl.ds(SIDE - HALO, HALO), sl] = average(edges, (2 * j + 1) * HALO, HALO, weight)
    main, rest = two_parts(coadd_ref[...])
    along = dot32(centre_ref[0], main) + (
        dot32(centre_ref[0], rest) + dot32(centre_ref[1], main)
    )
    ends = dot32(edge_ref[0], halo) + dot32(edge_ref[1], halo)
    along = jnp.concatenate(
        [along[:HALO] + ends[:HALO], along[HALO : SIDE - HALO], along[SIDE - HALO :] + ends[HALO:]],
        axis=0,
    )
    out_ref[...] = dot_parts(along, across_ref)


def prepare_kernel(taps_ref, *refs):
    own_hbm, across_ref, centre_ref, edge_ref, own_ref, band_ref, own_sem = refs
    own_copy = pltpu.make_async_copy(own_hbm, own_ref, own_sem)
    own_copy.start()
    tap_count = taps_ref.shape[1]
    half = tap_count // 2
    across = tap_row(lambda k: taps_ref[1, k], tap_count, SIDE - half, 3 * SIDE, True)
    store_band(band_ref, toeplitz(across, SIDE))
    across_ref[0], across_ref[1] = two_parts(band_ref[...])
    down = tap_row(lambda k: taps_ref[0, k], tap_count, SIDE - half, 3 * SIDE, False)
    centre_ref[0], centre_ref[1] = two_parts(toeplitz(down, SIDE)[:, SIDE : 2 * SIDE])
    lane = lax.broadcasted_iota(jnp.int32, (2 * HALO, SIDE), 1)
    row = lax.broadcasted_iota(jnp.int32, (2 * HALO, SIDE), 0)
    before = tap_row(lambda k: taps_ref[0, k], tap_count, HALO - half, SIDE, False)
    after = tap_row(lambda k: taps_ref[0, k], tap_count, SIDE - HALO - half, SIDE, False)
    edge = jnp.where(
        (row < HALO) & (lane < HALO),
        toeplitz(before, 2 * HALO),
        jnp.where(
            (row >= HALO) & (lane >= HALO) & (lane < 2 * HALO), toeplitz(after, 2 * HALO), 0.0
        ),
    )
    edge_ref[0], edge_ref[1] = two_parts(edge[:, : 2 * HALO])
    own_copy.wait()


def dot_parts(left, across_ref):
    main, rest = two_parts(left)
    both = dot32(jnp.concatenate([main, rest], axis=0), across_ref[0])
    return both[: left.shape[0]] + (dot32(main, across_ref[1]) + both[left.shape[0] :])


def per_device(
    split,
    raw_pixels,
    flat_field,
    bias_rows,
    psf_taps,
    term_weights,
    warp_shift,
    warp_scale,
    owner_of,
    patch_slot,
    weight_index,
    weight_table,
    detect_taps,
):
    nz, pn, ns = split
    devices = nz * pn * ns
    group = ns * pn
    visits, _, rows, cols = raw_pixels.shape
    blocks = owner_of.shape[0]
    terms = psf_taps.shape[1]
    per_dest = nz * CAP
    inner_rows = per_dest * PART
    edge_rows = inner_rows + FIELDS * per_dest
    width = PATCH_DEV * SIDE
    smem = pl.BlockSpec(memory_space=pltpu.SMEM)
    vmem = pl.BlockSpec(memory_space=pltpu.VMEM)
    hbm = pl.BlockSpec(memory_space=pltpu.HBM)
    params = pltpu.CompilerParams(vmem_limit_bytes=VMEM_LIMIT)

    def shaped(shape, dtype):
        return jax.ShapeDtypeStruct(shape, dtype)

    weights = term_weights.transpose(1, 2, 0)
    send = pl.pallas_call(
        functools.partial(warp_kernel, split),
        out_shape=[
            shaped((edge_rows + (inner_rows if k in (0, pn) else 0), SIDE), jnp.bfloat16)
            for k in range(group)
        ]
        + [shaped((inner_rows, SIDE), jnp.bfloat16)] * (group - 2),
        in_specs=[hbm] * 11,
        out_specs=[hbm] * (2 * group - 2),
        scratch_shapes=[
            pltpu.SMEM((blocks,), jnp.int32),
            pltpu.SMEM((blocks,), jnp.int32),
            pltpu.SMEM((blocks,), jnp.int32),
            pltpu.SMEM(weight_table.shape, jnp.float32),
            pltpu.SMEM(psf_taps.shape, jnp.float32),
            pltpu.SMEM(weights.shape, jnp.float32),
            pltpu.SMEM(warp_shift.shape, jnp.float32),
            pltpu.SMEM(warp_scale.shape, jnp.float32),
            pltpu.VMEM(bias_rows.shape, jnp.float32),
            pltpu.VMEM(raw_pixels.shape, jnp.float32),
            pltpu.VMEM(flat_field.shape, jnp.float32),
            pltpu.SMEM((devices,), jnp.int32),
            pltpu.VMEM((visits, 2 * terms + 2, rows, cols), jnp.bfloat16),
            pltpu.VMEM((visits, rows, cols), jnp.bfloat16),
            pltpu.VMEM((visits, rows, cols), jnp.bfloat16),
            pltpu.VMEM((group * per_dest, SIDE), jnp.float32),
            pltpu.VMEM((group * per_dest, SIDE), jnp.float32),
            pltpu.SemaphoreType.DMA((9,)),
            pltpu.SemaphoreType.DMA,
            pltpu.SemaphoreType.DMA((visits,)),
            pltpu.VMEM((group, edge_rows + inner_rows, SIDE), jnp.bfloat16),
            pltpu.SemaphoreType.DMA((2 * group - 2,)),
        ],
        compiler_params=pltpu.CompilerParams(vmem_limit_bytes=60 * 1024 * 1024),
        name="warp",
    )(
        owner_of.reshape(blocks),
        patch_slot.reshape(blocks),
        weight_index.reshape(blocks),
        weight_table,
        psf_taps,
        weights,
        warp_shift,
        warp_scale,
        bias_rows,
        raw_pixels,
        flat_field,
    )
    def in_plane(part, k):
        pairs = []
        for sec in range(ns):
            for p in range(pn):
                q = k % pn if sec == 0 else turned(k % pn, pn)
                pairs.append((sec * pn + p, (sec ^ (k // pn)) * pn + (p ^ q)))
        return lax.ppermute(part, ("sec", "p"), pairs)

    def along_z(part, d):
        pairs = []
        for i in range(devices):
            apart = d if i < nz * pn else shifted(d, nz)
            pairs.append((i, i ^ (apart * pn)))
        return lax.ppermute(part, every, pairs)

    every = ("sec", "z", "p")
    peers = sorted(range(1, group), key=lambda k: (k != pn, -bin(k % pn).count("1"), k))
    edge_blocks = [in_plane(send[k], k) for k in peers]

    across, centre, edge, own = pl.pallas_call(
        prepare_kernel,
        out_shape=(
            shaped((2, width, width), jnp.bfloat16),
            shaped((2, SIDE, SIDE), jnp.bfloat16),
            shaped((2, 2 * HALO, 2 * HALO), jnp.bfloat16),
            shaped((edge_rows + inner_rows, SIDE), jnp.bfloat16),
        ),
        in_specs=[smem, hbm],
        out_specs=(vmem,) * 4,
        scratch_shapes=[pltpu.VMEM((width, width), jnp.float32), pltpu.SemaphoreType.DMA],
        compiler_params=params,
        cost_estimate=pl.CostEstimate(flops=0, bytes_accessed=8 << 20, transcendentals=0),
        name="matrices",
    )(detect_taps, send[0])

    busy = pl.CostEstimate(flops=0, bytes_accessed=4 << 20, transcendentals=0)
    edge_sums = list(pl.pallas_call(
        functools.partial(edge_sum_kernel, nz, group),
        out_shape=[shaped((PATCH_DEV * (PART + FIELDS), SIDE), jnp.bfloat16)] * nz
        + [shaped((group, PATCH_DEV, per_dest, SIDE), jnp.float32)],
        in_specs=[vmem] * group,
        out_specs=[vmem] * (nz + 1),
        compiler_params=params,
        cost_estimate=busy,
        name="edge_sums",
    )(own, *edge_blocks))
    edges = [edge_sums[0]] + [along_z(edge_sums[d], d) for d in range(1, nz)]
    others = [k for k in range(group) if k not in (0, pn)]
    later = {k: send[group + i] for i, k in enumerate(others)}
    order = [k for k in peers if k != pn]
    held = lax.optimization_barrier(
        (edge_blocks[TIED], across, *(later[k] for k in order[:-TAIL]))
    )
    across = held[1]
    kept = lax.optimization_barrier((*edges[1:], *(later[k] for k in order[-TAIL:])))
    edges[1 : 1 + (nz - 1)], kept = kept[: (nz - 1)], kept[(nz - 1) :]
    inner_blocks = [in_plane(part, k) for part, k in zip((*held[2:], *kept), order)]
    first_rows, second_rows = pl.pallas_call(
        edges_kernel,
        out_shape=[shaped((HALO, width), jnp.bfloat16)] * 2,
        in_specs=[vmem] * nz,
        out_specs=[vmem] * 2,
        compiler_params=params,
        name="edge_rows",
    )(*edges)

    def swap(rows, start):
        pairs = [(i, i + 1) for i in range(start, devices - 1, 2)]
        return lax.ppermute(rows, every, pairs + [(j, i) for i, j in pairs])

    first_rows, second_rows, own = lax.optimization_barrier((first_rows, second_rows, own))
    second = swap(second_rows, 1)
    first = swap(first_rows, 0)

    inner_sums = pl.pallas_call(
        functools.partial(inner_sum_kernel, nz, group),
        out_shape=[shaped((PATCH_DEV * PART, SIDE), jnp.bfloat16)] * nz,
        in_specs=[vmem] * (group + 1),
        out_specs=[vmem] * nz,
        compiler_params=params,
        cost_estimate=busy,
        name="inner_sums",
    )(edge_sums[nz], own, edge_blocks[0], *inner_blocks)
    inner = [inner_sums[0]] + [along_z(inner_sums[d], d) for d in range(1, nz)]

    coadd, detection = pl.pallas_call(
        functools.partial(detect_kernel, nz),
        out_shape=[shaped((SIDE, width), jnp.float32)] * 2,
        in_specs=[vmem] * (2 * nz + 5),
        out_specs=[vmem] * 2,
        scratch_shapes=[pltpu.VMEM((2 * HALO, width), jnp.bfloat16)],
        compiler_params=params,
        name="coadd_detect",
    )(*edges, *inner, second, first, across, centre, edge)
    return coadd, detection


def solution(mesh):
    ns, nd = mesh.shape["sec"], mesh.shape["dev"]
    nz = math.gcd(nd, 4)
    pn = nd // nz
    cut = Mesh(mesh.devices.reshape(ns, nz, pn), ("sec", "z", "p"))
    every = ("sec", "z", "p")
    placed = (
        P(None, every, None, None),
        P(every, None, None),
        P(None, every, None),
        P(),
        P(None, every, None),
        P(None, every, None),
        P(None, every, None),
        P(every, None),
        P(every, None),
        P(every, None),
        P(),
        P(),
    )
    return jax.shard_map(
        functools.partial(per_device, (nz, pn, ns)),
        mesh=cut,
        in_specs=placed,
        out_specs=(P(every, None), P(every, None)),
        check_vma=False,
    )
```

```python
import functools
import math

import jax
import jax.numpy as jnp
from jax import lax
from jax.experimental import pallas as pl
from jax.experimental.pallas import tpu as pltpu
from jax.sharding import Mesh
from jax.sharding import PartitionSpec as P

SIDE = 128
CAP = 2
PATCH_DEV = 4
HALO = 32
FIELDS = 4
TIED = 2
TAIL = 2
PART = SIDE // 2
VMEM_LIMIT = 48 * 1024 * 1024


def turned(q, pn):
    bits = (pn.bit_length() - 1) // 2
    return ((q >> bits) | (q << bits)) & (pn - 1) if bits else q


def shifted(d, nz):
    return 0 if d == 0 else d % (nz - 1) + 1


def tap_row(tap, count, start, width, reverse):
    lane = lax.broadcasted_iota(jnp.int32, (1, width), 1)
    row = jnp.zeros((1, width), jnp.float32)
    for k in range(count):
        at = start + (count - 1 - k if reverse else k)
        row = jnp.where(lane == at % width, tap(k), row)
    return row


def toeplitz(row, height):
    return pltpu.roll(
        jnp.broadcast_to(row, (height, row.shape[1])), 0, 1, stride=1, stride_axis=0
    )


def store_band(band_ref, tiles):
    blocks = band_ref.shape[0] // SIDE
    for i in range(blocks):
        for j in range(blocks):
            place = (pl.ds(i * SIDE, SIDE), pl.ds(j * SIDE, SIDE))
            if abs(i - j) <= 1:
                first = (j - i + 1) * SIDE
                band_ref[place] = tiles[:, first : first + SIDE]
            else:
                band_ref[place] = jnp.zeros((SIDE, SIDE), band_ref.dtype)


def dot32(left, right):
    return jnp.dot(left, right, preferred_element_type=jnp.float32)


def two_parts(value):
    high = value.astype(jnp.bfloat16)
    return high, (value - high.astype(jnp.float32)).astype(jnp.bfloat16)


def three_parts(value):
    high = value.astype(jnp.bfloat16)
    rest = value - high.astype(jnp.float32)
    mid = rest.astype(jnp.bfloat16)
    return high, mid, (rest - mid.astype(jnp.float32)).astype(jnp.bfloat16)


def warp_kernel(
    split,
    owner_hbm,
    patch_hbm,
    index_hbm,
    table_hbm,
    taps_hbm,
    weights_hbm,
    shift_hbm,
    scale_hbm,
    bias_hbm,
    raw_hbm,
    flat_hbm,
    *rest,
):
    nz, pn, ns = split
    outs, rest = rest[: 2 * ns * pn - 2], rest[2 * ns * pn - 2 :]
    warp_body(
        split,
        (
            owner_hbm,
            patch_hbm,
            index_hbm,
            table_hbm,
            taps_hbm,
            weights_hbm,
            shift_hbm,
            scale_hbm,
            bias_hbm,
            raw_hbm,
            flat_hbm,
        ),
        outs,
        *rest,
    )


def warp_body(
    split,
    inputs,
    outs,
    owner_ref,
    patch_ref,
    index_ref,
    table_ref,
    taps_ref,
    weights_ref,
    shift_ref,
    scale_ref,
    bias_ref,
    raw_ref,
    flat_ref,
    count_ref,
    band_ref,
    left_ref,
    mid_ref,
    slot_rows,
    weight_rows,
    small_sem,
    flat_sem,
    raw_sem,
    out_ref,
    out_sem,
):
    (
        owner_hbm,
        patch_hbm,
        index_hbm,
        table_hbm,
        taps_hbm,
        weights_hbm,
        shift_hbm,
        scale_hbm,
        bias_hbm,
        raw_hbm,
        flat_hbm,
    ) = inputs
    nz, pn, ns = split
    my_sec, my_p, my_z = lax.axis_index("sec"), lax.axis_index("p"), lax.axis_index("z")
    visits, _, rows, cols = raw_ref.shape
    terms, tap_count = taps_ref.shape[1], taps_ref.shape[3]
    half = tap_count // 2
    per_dest = nz * CAP
    data_rows = per_dest * PART
    edge_rows = data_rows + FIELDS * per_dest

    small = [
        pltpu.make_async_copy(src, dst, small_sem.at[i])
        for i, (src, dst) in enumerate(
            (
                (taps_hbm, taps_ref),
                (bias_hbm, bias_ref),
                (owner_hbm, owner_ref),
                (patch_hbm, patch_ref),
                (index_hbm, index_ref),
                (table_hbm, table_ref),
                (weights_hbm, weights_ref),
                (shift_hbm, shift_ref),
                (scale_hbm, scale_ref),
            )
        )
    ]
    for copy in small:
        copy.start()
    flat_copy = pltpu.make_async_copy(flat_hbm, flat_ref, flat_sem)
    raw_copies = [
        pltpu.make_async_copy(raw_hbm.at[v], raw_ref.at[v], raw_sem.at[v]) for v in range(visits)
    ]
    raw_copies[0].start()
    flat_copy.start()
    for copy in raw_copies[1:]:
        copy.start()

    out_ref[...] = jnp.zeros_like(out_ref)
    slot_rows[...] = jnp.full(slot_rows.shape, -1.0, jnp.float32)
    weight_rows[...] = jnp.zeros_like(weight_rows)

    def clear(i, c):
        count_ref[i] = 0
        return c

    lax.fori_loop(0, count_ref.shape[0], clear, 0)
    for copy in small:
        copy.wait()

    def store_hat(ref, length, axis, shift, scale):
        centre = (length - 1) / 2.0
        count = length // SIDE
        for o in range(count):
            out_pos = o * SIDE + lax.broadcasted_iota(
                jnp.int32, (1, SIDE) if axis == 1 else (SIDE, 1), axis
            )
            source = scale * (out_pos.astype(jnp.float32) - centre) + centre + shift
            for i in range(count):
                at = (i, o) if axis == 1 else (o, i)
                place = tuple(pl.ds(k * SIDE, SIDE) for k in at)
                if abs(i - o) <= 1:
                    in_pos = i * SIDE + lax.broadcasted_iota(jnp.int32, (SIDE, SIDE), 1 - axis)
                    near = jnp.maximum(0.0, 1.0 - jnp.abs(in_pos.astype(jnp.float32) - source))
                    ref[place] = near.astype(jnp.bfloat16)
                else:
                    ref[place] = jnp.zeros((SIDE, SIDE), jnp.bfloat16)

    for visit in range(visits):
        for term in range(terms):
            for axis, reverse in ((1, True), (0, False)):
                row = tap_row(
                    lambda k: taps_ref[visit, term, axis, k],
                    tap_count,
                    SIDE - half,
                    3 * SIDE,
                    reverse,
                )
                store_band(
                    band_ref.at[visit, 2 * term + 1 - axis], toeplitz(row, SIDE).astype(jnp.bfloat16)
                )
        for axis, length in ((1, cols), (0, rows)):
            store_hat(
                band_ref.at[visit, 2 * terms + 1 - axis],
                length,
                axis,
                shift_ref[visit, 0, axis],
                scale_ref[visit, 0, axis],
            )

    def windows(length):
        wide = 2 * SIDE
        for at in range(0, length, wide):
            low, high = max(0, at - SIDE), min(length, at + wide + SIDE)
            yield pl.ds(at, min(wide, length - at)), pl.ds(low, high - low)

    def times_band(out, source, band):
        for o, k in windows(cols):
            out[:, o] = dot32(source[:, k], band[k, o]).astype(jnp.bfloat16)

    def band_times(out, band, source):
        for o, k in windows(rows):
            out[o, :] = dot32(band[o, k], source[k, :]).astype(jnp.bfloat16)

    row_blocks, col_blocks = rows // SIDE, cols // SIDE
    for visit in range(visits):
        left, mid = left_ref.at[visit], mid_ref.at[visit]
        bias = jnp.broadcast_to(bias_ref[visit], (SIDE, rows)).T
        raw_copies[visit].wait()
        if visit == 0:
            flat_copy.wait()
        for j in range(cols // SIDE):
            sl = pl.ds(j * SIDE, SIDE)
            left[:, sl] = ((raw_ref[visit, 0, :, sl] - bias) * flat_ref[0, :, sl]).astype(
                jnp.bfloat16
            )

        if terms == 1:
            times_band(mid, left, band_ref.at[visit, 0])
            for o, k in windows(rows):
                part = dot32(band_ref[visit, 1, o, k], mid[k, :])
                left[o, :] = (weights_ref[0, 0, visit] * part).astype(jnp.bfloat16)
        else:
            matched = None
            for term in range(terms):
                times_band(mid, left, band_ref.at[visit, 2 * term])
                part = weights_ref[0, term, visit] * dot32(band_ref[visit, 2 * term + 1], mid[...])
                matched = part if matched is None else matched + part
            left[...] = matched.astype(jnp.bfloat16)
        times_band(mid, left, band_ref.at[visit, 2 * terms])
        band_times(left, band_ref.at[visit, 2 * terms + 1], mid)

    for visit in range(visits):
        for i in range(row_blocks):
            for j in range(col_blocks):
                block = visit * (row_blocks * col_blocks) + i * col_blocks + j
                owner = owner_ref[block]
                rank = count_ref[owner]
                count_ref[owner] = rank + 1
                sec = owner // (nz * pn)
                dev = owner - sec * (nz * pn)
                z = dev // pn
                step = (dev - z * pn) ^ my_p
                step = jnp.where(my_sec == 0, step, turned(step, pn))
                dest = (sec ^ my_sec) * pn + step
                apart = z ^ my_z
                later = jnp.where(apart > 1, apart - 1, apart * (nz - 1))
                at = jnp.where(sec == 0, apart, later) * CAP + rank
                first = pl.multiple_of(at * PART, PART)
                columns = pl.ds(j * SIDE, SIDE)
                for target, source, count in (
                    (first, 0, HALO),
                    (first + HALO, SIDE - HALO, HALO),
                    (first + edge_rows, HALO, SIDE - 2 * HALO),
                ):
                    out_ref[dest, pl.ds(target, count), :] = left_ref[
                        visit, pl.ds(i * SIDE + source, count), columns
                    ]
                line = pl.ds(dest * per_dest + at, 1)
                slot_rows[line, :] = jnp.full((1, SIDE), patch_ref[block].astype(jnp.float32))
                weight_rows[line, :] = jnp.full((1, SIDE), table_ref[index_ref[block]])

    group = out_ref.shape[0]
    copies = []
    for dest in range(group):
        part = pl.ds(dest * per_dest, per_dest)
        fields = jnp.concatenate(
            [slot_rows[part, :]]
            + [w.astype(jnp.float32) for w in three_parts(weight_rows[part, :])],
            axis=0,
        )
        out_ref[dest, pl.ds(data_rows, fields.shape[0]), :] = fields.astype(jnp.bfloat16)
    whole = pl.ds(0, edge_rows + data_rows)
    pieces = [(k, whole if k in (0, pn) else pl.ds(0, edge_rows)) for k in range(group)]
    pieces += [(k, pl.ds(edge_rows, data_rows)) for k in range(group) if k not in (0, pn)]
    for out, (dest, rows_of) in enumerate(pieces):
        copies.append(
            pltpu.make_async_copy(out_ref.at[dest, rows_of], outs[out], out_sem.at[out])
        )
        copies[-1].start()
    for copy in copies:
        copy.wait()


def add_blocks(nz, ins, starts, weight_ref, outs):
    for z in range(nz):
        for place in range(PART // HALO):
            sums = [jnp.zeros((HALO, SIDE), jnp.float32) for _ in range(PATCH_DEV)]
            for g, (ref, start) in enumerate(zip(ins, starts)):
                for r in range(CAP):
                    at = z * CAP + r
                    value = ref[pl.ds(start + at * PART + place * HALO, HALO), :].astype(jnp.float32)
                    for j in range(PATCH_DEV):
                        sums[j] = sums[j] + weight_ref[g, j, pl.ds(at, 1), :] * value
            for j in range(PATCH_DEV):
                row = j * PART + place * HALO
                outs[z][pl.ds(row, HALO), :] = sums[j].astype(jnp.bfloat16)


def edge_sum_kernel(nz, sources, *refs):
    ins, outs, weight_ref = refs[:sources], refs[sources:-1], refs[-1]
    per_dest = nz * CAP
    for g in range(sources):
        fields = ins[g][pl.ds(per_dest * PART, FIELDS * per_dest), :].astype(jnp.float32)
        slot = fields[:per_dest]
        weight = (
            fields[per_dest : 2 * per_dest]
            + fields[2 * per_dest : 3 * per_dest]
            + fields[3 * per_dest :]
        )
        for j in range(PATCH_DEV):
            weight_ref[g, j] = jnp.where(slot == float(j), weight, 0.0)
    add_blocks(nz, ins, [0] * sources, weight_ref, outs)
    for z in range(nz):
        totals = []
        for j in range(PATCH_DEV):
            total = jnp.zeros((1, SIDE), jnp.float32)
            for g in range(sources):
                for r in range(CAP):
                    total = total + weight_ref[g, j, pl.ds(z * CAP + r, 1), :]
            totals.append(total)
        parts = [q.astype(jnp.float32) for q in three_parts(jnp.concatenate(totals, axis=0))]
        parts.append(jnp.zeros((PATCH_DEV, SIDE), jnp.float32))
        outs[z][pl.ds(PATCH_DEV * PART, FIELDS * PATCH_DEV), :] = jnp.concatenate(
            parts, axis=0
        ).astype(jnp.bfloat16)


def inner_sum_kernel(nz, sources, weight_ref, *refs):
    after = nz * CAP * (PART + FIELDS)
    starts = [after, after] + [0] * (sources - 2)
    add_blocks(nz, refs[:sources], starts, weight_ref, refs[sources:])


def totals_of(ins, start):
    total = jnp.zeros((PATCH_DEV, SIDE), jnp.float32)
    for ref in ins:
        extra = ref[pl.ds(start, FIELDS * PATCH_DEV), :].astype(jnp.float32)
        total = total + (
            extra[:PATCH_DEV] + extra[PATCH_DEV : 2 * PATCH_DEV] + extra[2 * PATCH_DEV : 3 * PATCH_DEV]
        )
    return jnp.maximum(total, 1.0)


def average(ins, row, count, total):
    numerator = ins[0][pl.ds(row, count), :].astype(jnp.float32)
    for ref in ins[1:]:
        numerator = numerator + ref[pl.ds(row, count), :].astype(jnp.float32)
    return numerator / total


def edges_kernel(*refs):
    ins, first_ref, second_ref = refs[:-2], refs[-2], refs[-1]
    odd = lax.axis_index("p") % 2
    total = totals_of(ins, 2 * PATCH_DEV * HALO)
    for j in range(PATCH_DEV):
        sl = pl.ds(j * SIDE, SIDE)
        rows = average(ins, 2 * j * HALO, 2 * HALO, total[j : j + 1])
        top, bottom = rows[:HALO], rows[HALO:]
        first_ref[:, sl] = jnp.where(odd == 0, bottom, top).astype(jnp.bfloat16)
        second_ref[:, sl] = jnp.where(odd == 0, top, bottom).astype(jnp.bfloat16)


def detect_kernel(nz, *refs):
    edges, inner = refs[:nz], refs[nz : 2 * nz]
    first_ref, second_ref, across_ref, centre_ref, edge_ref = refs[2 * nz : 2 * nz + 5]
    coadd_ref, out_ref, halo_ref = refs[2 * nz + 5 :]
    odd = lax.axis_index("p") % 2
    halo_ref[pl.ds(pl.multiple_of((1 - odd) * HALO, HALO), HALO)] = first_ref[...]
    halo_ref[pl.ds(pl.multiple_of(odd * HALO, HALO), HALO)] = second_ref[...]
    halo = halo_ref[...]
    total = totals_of(edges, 2 * PATCH_DEV * HALO)
    depth = SIDE - 2 * HALO
    for j in range(PATCH_DEV):
        sl = pl.ds(j * SIDE, SIDE)
        weight = total[j : j + 1]
        coadd_ref[pl.ds(0, HALO), sl] = average(edges, 2 * j * HALO, HALO, weight)
        coadd_ref[pl.ds(HALO, depth), sl] = average(inner, j * depth, depth, weight)
        coadd_ref[pl.ds(SIDE - HALO, HALO), sl] = average(edges, (2 * j + 1) * HALO, HALO, weight)
    main, rest = two_parts(coadd_ref[...])
    along = dot32(centre_ref[0], main) + (
        dot32(centre_ref[0], rest) + dot32(centre_ref[1], main)
    )
    ends = dot32(edge_ref[0], halo) + dot32(edge_ref[1], halo)
    along = jnp.concatenate(
        [along[:HALO] + ends[:HALO], along[HALO : SIDE - HALO], along[SIDE - HALO :] + ends[HALO:]],
        axis=0,
    )
    out_ref[...] = dot_parts(along, across_ref)


def prepare_kernel(taps_ref, *refs):
    own_hbm, across_ref, centre_ref, edge_ref, own_ref, band_ref, own_sem = refs
    own_copy = pltpu.make_async_copy(own_hbm, own_ref, own_sem)
    own_copy.start()
    tap_count = taps_ref.shape[1]
    half = tap_count // 2
    across = tap_row(lambda k: taps_ref[1, k], tap_count, SIDE - half, 3 * SIDE, True)
    store_band(band_ref, toeplitz(across, SIDE))
    across_ref[0], across_ref[1] = two_parts(band_ref[...])
    down = tap_row(lambda k: taps_ref[0, k], tap_count, SIDE - half, 3 * SIDE, False)
    centre_ref[0], centre_ref[1] = two_parts(toeplitz(down, SIDE)[:, SIDE : 2 * SIDE])
    lane = lax.broadcasted_iota(jnp.int32, (2 * HALO, SIDE), 1)
    row = lax.broadcasted_iota(jnp.int32, (2 * HALO, SIDE), 0)
    before = tap_row(lambda k: taps_ref[0, k], tap_count, HALO - half, SIDE, False)
    after = tap_row(lambda k: taps_ref[0, k], tap_count, SIDE - HALO - half, SIDE, False)
    edge = jnp.where(
        (row < HALO) & (lane < HALO),
        toeplitz(before, 2 * HALO),
        jnp.where(
            (row >= HALO) & (lane >= HALO) & (lane < 2 * HALO), toeplitz(after, 2 * HALO), 0.0
        ),
    )
    edge_ref[0], edge_ref[1] = two_parts(edge[:, : 2 * HALO])
    own_copy.wait()


def dot_parts(left, across_ref):
    main, rest = two_parts(left)
    both = dot32(jnp.concatenate([main, rest], axis=0), across_ref[0])
    return both[: left.shape[0]] + (dot32(main, across_ref[1]) + both[left.shape[0] :])


def per_device(
    split,
    raw_pixels,
    flat_field,
    bias_rows,
    psf_taps,
    term_weights,
    warp_shift,
    warp_scale,
    owner_of,
    patch_slot,
    weight_index,
    weight_table,
    detect_taps,
):
    nz, pn, ns = split
    devices = nz * pn * ns
    group = ns * pn
    visits, _, rows, cols = raw_pixels.shape
    blocks = owner_of.shape[0]
    terms = psf_taps.shape[1]
    per_dest = nz * CAP
    inner_rows = per_dest * PART
    edge_rows = inner_rows + FIELDS * per_dest
    width = PATCH_DEV * SIDE
    smem = pl.BlockSpec(memory_space=pltpu.SMEM)
    vmem = pl.BlockSpec(memory_space=pltpu.VMEM)
    hbm = pl.BlockSpec(memory_space=pltpu.HBM)
    params = pltpu.CompilerParams(vmem_limit_bytes=VMEM_LIMIT)

    def shaped(shape, dtype):
        return jax.ShapeDtypeStruct(shape, dtype)

    weights = term_weights.transpose(1, 2, 0)
    send = pl.pallas_call(
        functools.partial(warp_kernel, split),
        out_shape=[
            shaped((edge_rows + (inner_rows if k in (0, pn) else 0), SIDE), jnp.bfloat16)
            for k in range(group)
        ]
        + [shaped((inner_rows, SIDE), jnp.bfloat16)] * (group - 2),
        in_specs=[hbm] * 11,
        out_specs=[hbm] * (2 * group - 2),
        scratch_shapes=[
            pltpu.SMEM((blocks,), jnp.int32),
            pltpu.SMEM((blocks,), jnp.int32),
            pltpu.SMEM((blocks,), jnp.int32),
            pltpu.SMEM(weight_table.shape, jnp.float32),
            pltpu.SMEM(psf_taps.shape, jnp.float32),
            pltpu.SMEM(weights.shape, jnp.float32),
            pltpu.SMEM(warp_shift.shape, jnp.float32),
            pltpu.SMEM(warp_scale.shape, jnp.float32),
            pltpu.VMEM(bias_rows.shape, jnp.float32),
            pltpu.VMEM(raw_pixels.shape, jnp.float32),
            pltpu.VMEM(flat_field.shape, jnp.float32),
            pltpu.SMEM((devices,), jnp.int32),
            pltpu.VMEM((visits, 2 * terms + 2, rows, cols), jnp.bfloat16),
            pltpu.VMEM((visits, rows, cols), jnp.bfloat16),
            pltpu.VMEM((visits, rows, cols), jnp.bfloat16),
            pltpu.VMEM((group * per_dest, SIDE), jnp.float32),
            pltpu.VMEM((group * per_dest, SIDE), jnp.float32),
            pltpu.SemaphoreType.DMA((9,)),
            pltpu.SemaphoreType.DMA,
            pltpu.SemaphoreType.DMA((visits,)),
            pltpu.VMEM((group, edge_rows + inner_rows, SIDE), jnp.bfloat16),
            pltpu.SemaphoreType.DMA((2 * group - 2,)),
        ],
        compiler_params=pltpu.CompilerParams(vmem_limit_bytes=60 * 1024 * 1024),
        name="warp",
    )(
        owner_of.reshape(blocks),
        patch_slot.reshape(blocks),
        weight_index.reshape(blocks),
        weight_table,
        psf_taps,
        weights,
        warp_shift,
        warp_scale,
        bias_rows,
        raw_pixels,
        flat_field,
    )
    def in_plane(part, k):
        pairs = []
        for sec in range(ns):
            for p in range(pn):
                q = k % pn if sec == 0 else turned(k % pn, pn)
                pairs.append((sec * pn + p, (sec ^ (k // pn)) * pn + (p ^ q)))
        return lax.ppermute(part, ("sec", "p"), pairs)

    def along_z(part, d):
        pairs = []
        for i in range(devices):
            apart = d if i < nz * pn else shifted(d, nz)
            pairs.append((i, i ^ (apart * pn)))
        return lax.ppermute(part, every, pairs)

    every = ("sec", "z", "p")
    peers = sorted(range(1, group), key=lambda k: (k != pn, -bin(k % pn).count("1"), k))
    edge_blocks = [in_plane(send[k], k) for k in peers]

    across, centre, edge, own = pl.pallas_call(
        prepare_kernel,
        out_shape=(
            shaped((2, width, width), jnp.bfloat16),
            shaped((2, SIDE, SIDE), jnp.bfloat16),
            shaped((2, 2 * HALO, 2 * HALO), jnp.bfloat16),
            shaped((edge_rows + inner_rows, SIDE), jnp.bfloat16),
        ),
        in_specs=[smem, hbm],
        out_specs=(vmem,) * 4,
        scratch_shapes=[pltpu.VMEM((width, width), jnp.float32), pltpu.SemaphoreType.DMA],
        compiler_params=params,
        cost_estimate=pl.CostEstimate(flops=0, bytes_accessed=8 << 20, transcendentals=0),
        name="matrices",
    )(detect_taps, send[0])

    busy = pl.CostEstimate(flops=0, bytes_accessed=4 << 20, transcendentals=0)
    edge_sums = list(pl.pallas_call(
        functools.partial(edge_sum_kernel, nz, group),
        out_shape=[shaped((PATCH_DEV * (PART + FIELDS), SIDE), jnp.bfloat16)] * nz
        + [shaped((group, PATCH_DEV, per_dest, SIDE), jnp.float32)],
        in_specs=[vmem] * group,
        out_specs=[vmem] * (nz + 1),
        compiler_params=params,
        cost_estimate=busy,
        name="edge_sums",
    )(own, *edge_blocks))
    edges = [edge_sums[0]] + [along_z(edge_sums[d], d) for d in range(1, nz)]
    others = [k for k in range(group) if k not in (0, pn)]
    later = {k: send[group + i] for i, k in enumerate(others)}
    order = [k for k in peers if k != pn]
    held = lax.optimization_barrier(
        (edge_blocks[TIED], across, *(later[k] for k in order[:-TAIL]))
    )
    across = held[1]
    kept = lax.optimization_barrier((*edges[1:3], *(later[k] for k in order[-TAIL:])))
    edges[1 : 1 + 2], kept = kept[: 2], kept[2 :]
    inner_blocks = [in_plane(part, k) for part, k in zip((*held[2:], *kept), order)]
    first_rows, second_rows = pl.pallas_call(
        edges_kernel,
        out_shape=[shaped((HALO, width), jnp.bfloat16)] * 2,
        in_specs=[vmem] * nz,
        out_specs=[vmem] * 2,
        compiler_params=params,
        name="edge_rows",
    )(*edges)

    def swap(rows, start):
        pairs = [(i, i + 1) for i in range(start, devices - 1, 2)]
        return lax.ppermute(rows, every, pairs + [(j, i) for i, j in pairs])

    first_rows, second_rows, own = lax.optimization_barrier((first_rows, second_rows, own))
    first, second = swap(first_rows, 0), swap(second_rows, 1)

    inner_sums = pl.pallas_call(
        functools.partial(inner_sum_kernel, nz, group),
        out_shape=[shaped((PATCH_DEV * PART, SIDE), jnp.bfloat16)] * nz,
        in_specs=[vmem] * (group + 1),
        out_specs=[vmem] * nz,
        compiler_params=params,
        cost_estimate=busy,
        name="inner_sums",
    )(edge_sums[nz], own, edge_blocks[0], *inner_blocks)
    inner = [inner_sums[0]] + [along_z(inner_sums[d], d) for d in range(1, nz)]

    coadd, detection = pl.pallas_call(
        functools.partial(detect_kernel, nz),
        out_shape=[shaped((SIDE, width), jnp.float32)] * 2,
        in_specs=[vmem] * (2 * nz + 5),
        out_specs=[vmem] * 2,
        scratch_shapes=[pltpu.VMEM((2 * HALO, width), jnp.bfloat16)],
        compiler_params=params,
        name="coadd_detect",
    )(*edges, *inner, first, second, across, centre, edge)
    return coadd, detection


def solution(mesh):
    ns, nd = mesh.shape["sec"], mesh.shape["dev"]
    nz = math.gcd(nd, 4)
    pn = nd // nz
    cut = Mesh(mesh.devices.reshape(ns, nz, pn), ("sec", "z", "p"))
    every = ("sec", "z", "p")
    placed = (
        P(None, every, None, None),
        P(every, None, None),
        P(None, every, None),
        P(),
        P(None, every, None),
        P(None, every, None),
        P(None, every, None),
        P(every, None),
        P(every, None),
        P(every, None),
        P(),
        P(),
    )
    return jax.shard_map(
        functools.partial(per_device, (nz, pn, ns)),
        mesh=cut,
        in_specs=placed,
        out_specs=(P(every, None), P(every, None)),
        check_vma=False,
    )
```
